32 devices in a mesh: groups: 2 (over y), pool: 4 (over z), tensor: 4 (over x, core).
Axes of the slice: x: 2, y: 2, z: 4, core: 2. Of those that a mesh axis runs over, the one named last changes fastest.
Arguments:
- tokens: bfloat16 [8192, 8192], P(('groups', 'pool'), 'tensor'), parts along dimension 0, may hold values from -6 to 6
- value_weight: bfloat16 [8192, 1024], P('tensor'), may hold values from -0.0625 to 0.0625
- adapter_down_weight: bfloat16 [32, 8192, 64], P(('groups', 'pool'), 'tensor'), parts along dimension 0, may hold values from -0.0625 to 0.0625
- adapter_up_weight: bfloat16 [32, 64, 1024], P(('groups', 'pool'), None, 'tensor'), parts along dimension 0, may hold values from -0.75 to 0.75
- adapter_of_block: int32 [8, 8], P(('groups', 'pool')), parts along dimension 0, may hold values from 0 to 15, as said below
- adapter_pool_slot: int32 [32], P('groups'), parts along dimension 0, may hold values from 0 to 15, as said below
- live_block_tokens: int32 [8, 8], P(('groups', 'pool')), parts along dimension 0, may hold values from 1 to 128, 576 in all within a row
Outputs:
- value_rows: bfloat16 [8192, 1024], P(('groups', 'pool'), 'tensor'), parts along dimension 0
The draws below stay inside these ranges and needn't reach their ends.
There are 2 independent parts, one for each index of `groups`. The reference program is written for one: setup_inputs(seed, part) draws one part's arguments, and reference() takes and returns one part's arrays. A program takes and returns all parts, laid end to end along the dimension named above; an argument that names none is the same for every part. Nothing has to cross between parts.
Inputs may be any that keep to these rules, and one draw needn't show every extreme that they name: `adapter_of_block`: adapter numbers below 16. The blocks of one index of pool use adapters whose slots lie on at most 2 blocks' worth of any one pool index (slot s lies on pool index s // 4); in every draw some pool index holds the adapter of 2 blocks of every pool index. `adapter_pool_slot`: each slot holds exactly one adapter.
All inputs are finite; a program needn't handle non-finite values.
Results may differ from the reference program's by a relative error of at most 0.0033.
Values may be sent and summed in bfloat16 or wider, within the bound.
No kernel may reach another device: no remote copies, remote signals or barrier semaphores. Data moves between devices by JAX's collectives and lax.ppermute only.
A program may use at most 192 MiB of HBM per device.

```python
import math
import jax
import jax.numpy as jnp
import numpy as np
from jax import lax

MODEL_WIDTH = 8192
VALUE_WIDTH = 1024
ADAPTER_RANK = 64
BLOCK_ROWS_PAD = 128
BLK_DEV = 8
ADP_DEV = 4
TOKENS = 4096
ADAPTER_COUNT = 16
CAP = 2
N_POOL = 4


def pool_layout(key):
    return jax.random.permutation(key, ADAPTER_COUNT).astype(jnp.int32)


def draw_adapter_pool_slot(key, part):
    slot_table = pool_layout(key)
    return slot_table


def draw_adapter_of_block(key, part):
    slot_table = pool_layout(key)
    key = jax.random.fold_in(key, 23)
    keys = jax.random.split(key, 5)
    holder = jnp.argsort(slot_table).astype(jnp.int32)
    hot_owner = jax.random.randint(keys[0], (), 0, N_POOL)
    hot_sub = jax.random.randint(keys[1], (), 0, ADP_DEV)
    owner_ids = jnp.arange(N_POOL, dtype=jnp.int32)
    scores = jax.random.randint(keys[2], (N_POOL, N_POOL), 0, 1048576) * N_POOL + owner_ids[None, :]
    scores = jnp.where(owner_ids[None, :] == hot_owner, -1, scores)
    owner_order = jnp.argsort(scores, axis=1).astype(jnp.int32)
    owners = jnp.tile(owner_order, (1, CAP))[:, :BLK_DEV]
    subs = jax.random.randint(keys[3], (N_POOL, BLK_DEV), 0, ADP_DEV)
    subs = jnp.where(owners == hot_owner, hot_sub, subs)
    place_scores = jax.random.randint(keys[4], (N_POOL, BLK_DEV), 0, 1048576) * BLK_DEV + jnp.arange(BLK_DEV, dtype=jnp.int32)[None, :]
    shuffle = jnp.argsort(place_scores, axis=1).astype(jnp.int32)
    owners = jnp.take_along_axis(owners, shuffle, axis=1)
    subs = jnp.take_along_axis(subs, shuffle, axis=1)
    slots = owners * ADP_DEV + subs
    return holder[slots].astype(jnp.int32)


def block_scale(stream_key, extent, shards, smallest, high):
    def one(position, parts):
        draws = jax.random.uniform(jax.random.fold_in(jax.random.fold_in(stream_key, 6), position), (parts,), jnp.float32, smallest / len(shards), high / len(shards))
        return jnp.repeat(jnp.exp(draws), extent[position] // parts).reshape((-1,) + (1,) * (len(extent) - position - 1))

    factor_of = one(*shards[0])
    for cut in shards[1:]:
        factor_of = factor_of * one(*cut)
    return factor_of


def profile(number_of, total, bound, skew):
    loads = [(1 << 20) // math.isqrt(standing ** skew) + 1 for standing in range(2, number_of + 1)]
    spare, counts = total - bound - (number_of - 1), [1] * (number_of - 1)
    while spare > 0:
        movable = [i for i in range(number_of - 1) if counts[i] < bound]
        pool, remaining = sum([loads[i] for i in movable]), spare
        for i in movable:
            more = min(bound - counts[i], max(1, remaining * loads[i] // pool), spare)
            counts[i] = counts[i] + more
            spare = spare - more
    return np.array([bound] + counts)


def uneven(own_key, number_of, total, limit, lean):
    if number_of == 2:
        one = jax.random.randint(own_key, (), max(1, total - limit), min(limit, total - 1) + 1)
        return jnp.stack([one, total - one])
    lengths = jnp.asarray(profile(number_of, total, limit, lean), jnp.int32)
    twos = (number_of - 1) // 2
    giver, receiver = lengths[1:1 + 2 * twos:2], lengths[2:2 + 2 * twos:2]
    room = jnp.minimum(giver - 1, limit - receiver)
    shifted = jax.random.randint(jax.random.fold_in(own_key, 1), (twos,), 0, 1 << 20) % (room + 1)
    lengths = lengths.at[1:1 + 2 * twos:2].set(giver - shifted).at[2:2 + 2 * twos:2].set(receiver + shifted)
    return lengths[jax.random.permutation(jax.random.fold_in(own_key, 2), number_of)]


def gaussian(own_key, dims, width, most, shards=(), kind=jnp.bfloat16):
    values = width * jax.random.normal(own_key, dims, jnp.float32)
    if shards:
        values = values * block_scale(own_key, dims, shards, -0.22, 0.18)
    return jnp.clip(values, -most, most).astype(kind)


def setup_inputs(seed: int = 0, part: int = 0) -> dict:
    key_list = jax.random.split(jax.random.key(seed), 8)
    part_keys = jax.random.split(jax.random.fold_in(key_list[7], part), 8)
    return {
        "tokens": gaussian(part_keys[0], (TOKENS, MODEL_WIDTH), 1.0, 6.0, ((0, 4), (1, 4))),
        "value_weight": gaussian(key_list[1], (MODEL_WIDTH, VALUE_WIDTH), MODEL_WIDTH ** -0.5, 0.0625, ((0, 4),)),
        "adapter_down_weight": gaussian(part_keys[2], (ADAPTER_COUNT, MODEL_WIDTH, ADAPTER_RANK), MODEL_WIDTH ** -0.5, 0.0625, ((0, 4), (1, 4))),
        "adapter_up_weight": gaussian(part_keys[3], (ADAPTER_COUNT, ADAPTER_RANK, VALUE_WIDTH), ADAPTER_RANK ** -0.5, 0.75, ((0, 4), (2, 4))),
        "adapter_of_block": draw_adapter_of_block(jax.random.fold_in(jax.random.fold_in(key_list[7], part), 71), part),
        "adapter_pool_slot": draw_adapter_pool_slot(jax.random.fold_in(jax.random.fold_in(key_list[7], part), 71), part),
        "live_block_tokens": jax.vmap(lambda own: uneven(own, BLK_DEV, BLOCK_ROWS_PAD + (BLK_DEV - 1) * BLOCK_ROWS_PAD // 2, BLOCK_ROWS_PAD, 1))(jax.random.split(part_keys[6], N_POOL)).reshape((N_POOL, BLK_DEV)).astype(jnp.int32),
    }


ADAPTER_SCALE = 0.5


def reference(tokens, value_weight, adapter_down_weight, adapter_up_weight, adapter_of_block, adapter_pool_slot, live_block_tokens):
    base_output_full = jnp.dot(tokens, value_weight, preferred_element_type=jnp.float32)
    slot_ids = adapter_pool_slot[adapter_of_block.reshape(-1)].astype(jnp.int32)
    row_blocks = tokens.reshape(-1, BLOCK_ROWS_PAD, MODEL_WIDTH)

    def per_block(items):
        rows_by_block, single_pool_slot = items
        down_weight_panel = lax.dynamic_index_in_dim(adapter_down_weight, single_pool_slot, 0, keepdims=False)
        up_weight_panel = lax.dynamic_index_in_dim(adapter_up_weight, single_pool_slot, 0, keepdims=False)
        shrunk = jnp.dot(rows_by_block, down_weight_panel, preferred_element_type=jnp.float32).astype(jnp.bfloat16)
        return jnp.dot(shrunk, up_weight_panel, preferred_element_type=jnp.float32)

    adapter_delta_rows = lax.map(per_block, (row_blocks, slot_ids))
    live_rows = jnp.arange(BLOCK_ROWS_PAD, dtype=jnp.int32)[None, :] < live_block_tokens.reshape(-1)[:, None]
    combined_output = base_output_full.reshape(-1, BLOCK_ROWS_PAD, VALUE_WIDTH) + ADAPTER_SCALE * adapter_delta_rows
    combined_output = jnp.where(live_rows[:, :, None], combined_output, jnp.zeros_like(combined_output))
    return combined_output.reshape(TOKENS, VALUE_WIDTH).astype(jnp.bfloat16)
```

```python
import functools

import jax
import jax.numpy as jnp
from jax import lax
from jax.experimental import pallas as pl
from jax.experimental.pallas import tpu as pltpu
from jax.sharding import PartitionSpec as P

ADAPTER_SCALE = 0.5
ROW_TILE = 256
VMEM_BYTES = 32 * 1024 * 1024


def swap(value, axis, distance):
    pairs = [(i, i ^ distance) for i in range(lax.axis_size(axis))]
    return lax.ppermute(value, axis, pairs)


def base_kernel(chunks, tokens_ref, weight_ref, part_ref):
    del chunks
    tile = min(ROW_TILE, tokens_ref.shape[0])

    @pl.loop(0, tokens_ref.shape[0] // tile)
    def _(step):
        rows = pl.ds(pl.multiple_of(step * tile, tile), tile)
        part_ref[0, rows, :] = jnp.dot(
            tokens_ref[rows, :], weight_ref[...], preferred_element_type=jnp.float32
        )


def base_chunks(tokens, weight, chunks, width):
    rows, depth = tokens.shape
    count = chunks.shape[0]
    return pl.pallas_call(
        base_kernel,
        grid_spec=pltpu.PrefetchScalarGridSpec(
            num_scalar_prefetch=1,
            grid=(count,),
            in_specs=[
                pl.BlockSpec((rows, depth), lambda i, c: (0, 0)),
                pl.BlockSpec((depth, width), lambda i, c: (0, c[i])),
            ],
            out_specs=pl.BlockSpec((1, rows, width), lambda i, c: (i, 0, 0)),
        ),
        out_shape=jax.ShapeDtypeStruct((count, rows, width), jnp.float32),
        compiler_params=pltpu.CompilerParams(vmem_limit_bytes=VMEM_BYTES),
        cost_estimate=pl.CostEstimate(
            flops=2 * rows * depth * width * count,
            bytes_accessed=2 * rows * depth + (2 * depth + 4 * rows) * width * count,
            transcendentals=0,
        ),
    )(chunks, tokens, weight)


def pack_kernel(slots, down_ref, up_ref, *rest):
    del slots
    out_ref = rest[-1]
    depth = down_ref.shape[2]
    out_ref[:, :, :depth] = down_ref[...]
    out_ref[:, :, depth:] = up_ref[...]


def pack_panels(slots, down, up, after=None):
    count = slots.shape[0]
    rank, depth = down.shape[1:]
    width = up.shape[2]
    gate = [] if after is None else [after]
    return pl.pallas_call(
        pack_kernel,
        grid_spec=pltpu.PrefetchScalarGridSpec(
            num_scalar_prefetch=1,
            grid=(count,),
            in_specs=[
                pl.BlockSpec((1, rank, depth), lambda i, s: (s[i], 0, 0)),
                pl.BlockSpec((1, rank, width), lambda i, s: (s[i], 0, 0)),
            ]
            + [pl.BlockSpec(memory_space=pl.ANY)] * len(gate),
            out_specs=pl.BlockSpec((1, rank, depth + width), lambda i, s: (i, 0, 0)),
        ),
        out_shape=jax.ShapeDtypeStruct((count, rank, depth + width), down.dtype),
        compiler_params=pltpu.CompilerParams(vmem_limit_bytes=VMEM_BYTES),
    )(slots, down, up, *gate)


def shrink_kernel(scalars, token_ref, *refs):
    out_ref = refs[-1]

    def term(panel):
        out_ref[0] = lax.dot_general(
            panel, token_ref[0], (((1,), (1,)), ((), ())), preferred_element_type=jnp.float32
        )

    if len(refs) == 2:
        term(refs[0][0])
    else:
        term(jnp.where(scalars[0] != 0, refs[0][0], refs[1][0]))


def panel_spec(shape, column, row):
    return pl.BlockSpec(shape, lambda i, s: (s[row + i], 0, column))


def shrink(row_blocks, blocks, sources, first):
    count = blocks.shape[0]
    rows_by_block, depth = row_blocks.shape[1:]
    rank = sources[0][0].shape[1]
    scalars = jnp.concatenate([first.astype(jnp.int32)[None], blocks] + [s[1] for s in sources])
    specs = [pl.BlockSpec((1, rows_by_block, depth), lambda i, s: (s[1 + i], 0, 0))]
    for number in range(len(sources)):
        specs.append(panel_spec((1, rank, depth), 0, 1 + count * (number + 1)))
    return pl.pallas_call(
        shrink_kernel,
        grid_spec=pltpu.PrefetchScalarGridSpec(
            num_scalar_prefetch=1,
            grid=(count,),
            in_specs=specs,
            out_specs=pl.BlockSpec((1, rank, rows_by_block), lambda i, s: (i, 0, 0)),
        ),
        out_shape=jax.ShapeDtypeStruct((count, rank, rows_by_block), jnp.float32),
        compiler_params=pltpu.CompilerParams(vmem_limit_bytes=VMEM_BYTES),
        cost_estimate=pl.CostEstimate(
            flops=2 * rank * depth * rows_by_block * count,
            bytes_accessed=2 * depth * (rank + rows_by_block) * count,
            transcendentals=0,
        ),
    )(scalars, row_blocks, *[s[0] for s in sources])


def combine_kernel(count, part_count, up_count, scalars, *refs):
    parts = refs[:part_count]
    mine_ref, far_ref = refs[part_count : part_count + 2]
    ups = refs[part_count + 2 : part_count + 2 + up_count]
    out_ref = refs[-1]
    total = parts[0][0]
    for part in parts[1:]:
        total = total + part[0]
    up = ups[0][0] if up_count == 1 else jnp.where(scalars[0] != 0, ups[0][0], ups[1][0])
    delta = lax.dot_general(
        total.astype(jnp.bfloat16), up, (((0,), (0,)), ((), ())), preferred_element_type=jnp.float32
    )
    live = scalars[1 + count + pl.program_id(0)]
    row = lax.broadcasted_iota(jnp.int32, delta.shape, 0)
    value = mine_ref[...] + far_ref[...] + ADAPTER_SCALE * delta
    out_ref[...] = jnp.where(row < live, value, 0.0).astype(out_ref.dtype)


def combine(blocks, live, parts, base_mine, base_far, sources, first, out):
    count = blocks.shape[0]
    rank, rows_by_block = parts[0].shape[1:]
    rows, width = base_mine.shape
    scalars = jnp.concatenate(
        [first.astype(jnp.int32)[None], blocks, live[blocks]] + [s[1] for s in sources]
    )
    specs = [pl.BlockSpec((1, rank, rows_by_block), lambda i, s: (i, 0, 0)) for _ in parts]
    specs += [pl.BlockSpec((rows_by_block, width), lambda i, s: (s[1 + i], 0))] * 2
    for number, source in enumerate(sources):
        specs.append(panel_spec((1, rank, width), source[2], 1 + count * (number + 2)))
    operands = [*parts, base_mine, base_far, *[s[0] for s in sources]]
    aliases = {}
    if out is not None:
        specs.append(pl.BlockSpec(memory_space=pl.ANY))
        operands.append(out)
        aliases = {len(operands): 0}
    return pl.pallas_call(
        functools.partial(combine_kernel, count, len(parts), len(sources)),
        grid_spec=pltpu.PrefetchScalarGridSpec(
            num_scalar_prefetch=1,
            grid=(count,),
            in_specs=specs,
            out_specs=pl.BlockSpec((rows_by_block, width), lambda i, s: (s[1 + i], 0)),
        ),
        out_shape=jax.ShapeDtypeStruct((rows, width), jnp.bfloat16),
        input_output_aliases=aliases,
        compiler_params=pltpu.CompilerParams(vmem_limit_bytes=VMEM_BYTES),
    )(scalars, *operands)


def base_sum(tokens, weight, width):
    tensor_size = lax.axis_size("tensor")
    place = lax.axis_index("tensor")
    distance = 1
    chunks = jnp.arange(tensor_size, dtype=jnp.int32)
    order = [k ^ (tensor_size - 1) for k in range(tensor_size)]
    order = sorted(order, key=lambda k: (1 - (k & 1), k), reverse=False)
    chunks = place ^ jnp.asarray(order, jnp.int32)
    half = tensor_size // 2
    sent = base_chunks(tokens, weight, chunks[:half], width)
    kept = base_chunks(tokens, weight, chunks[half:], width)
    kept_order = order[half:]
    sent_order = order[:half]
    arrived = swap(sent, "tensor", distance)
    rows_of = {k ^ 1: i for i, k in enumerate(sent_order)}
    held = {k: (kept[i], arrived[rows_of[k]]) for i, k in enumerate(kept_order)}
    held = {k: (a, b) for k, (a, b) in held.items()}
    distance = 2
    while distance < tensor_size:
        out = {k: a + b for k, (a, b) in held.items() if k & distance}
        held = {
            k: (a + b, swap(out[k | distance], "tensor", distance))
            for k, (a, b) in held.items()
            if not k & distance
        }
        distance *= 2
    return held[0]


def reduce_parts(part):
    return [part] + [swap(part, "tensor", m) for m in range(1, lax.axis_size("tensor"))]


def picks(slot_ids, holder, holder_slots, count):
    hit = slot_ids // holder_slots == holder
    rank = jnp.cumsum(hit.astype(jnp.int32)) - 1
    chosen = hit[None, :] & (rank[None, :] == jnp.arange(count, dtype=jnp.int32)[:, None])
    number = jnp.arange(slot_ids.shape[0], dtype=jnp.int32)
    blocks = jnp.sum(jnp.where(chosen, number[None, :], 0), axis=1)
    slots = jnp.sum(jnp.where(chosen, (slot_ids % holder_slots)[None, :], 0), axis=1)
    return blocks, slots


def on_line_of_four(row_blocks, down, up, names, table, live, base, capacity):
    here = lax.axis_index("pool")
    inner = (here == 1) | (here == 2)
    holder_slots, _, depth = down.shape
    up_column = depth // up.shape[2]

    def across(value, pairs):
        return lax.ppermute(value, "pool", pairs)

    inner_down = across(down, [(1, 2), (2, 1)])
    inner_up = across(up, [(1, 2), (2, 1)])
    asked = [names] + [swap(names, "pool", m) for m in range(1, 4)]
    asked = [table[a[0]] for a in asked]

    def wanted(distance, holder):
        return picks(asked[distance], holder, holder_slots, capacity)[1]

    near = across(
        pack_panels(wanted(1, here), down, up), [(0, 1), (1, 0), (2, 3), (3, 2)]
    )
    to_inner = across(pack_panels(wanted(2, here), down, up, near), [(0, 2), (3, 1)])
    to_outer = across(pack_panels(wanted(3, here), down, up, near), [(0, 3), (3, 0)])
    forwarded = across(
        pack_panels(wanted(1, here ^ 3), inner_down, inner_up), [(1, 0), (2, 3)]
    )

    ranks = jnp.arange(capacity, dtype=jnp.int32)
    base_mine, base_far = base
    always = jnp.bool_(True)
    own_blocks, own_slots = picks(asked[0], here, holder_slots, capacity)
    near_blocks, _ = picks(asked[0], here ^ 1, holder_slots, capacity)
    early_blocks, early_slots = picks(
        asked[0], here ^ jnp.where(inner, 3, 2), holder_slots, capacity
    )
    late_blocks, _ = picks(asked[0], here ^ jnp.where(inner, 2, 3), holder_slots, capacity)
    phases = [
        (own_blocks, [(down, own_slots)], [(up, own_slots, 0)], always),
        (near_blocks, [(near, ranks)], [(near, ranks, up_column)], always),
        (
            early_blocks,
            [(inner_down, early_slots), (forwarded, ranks)],
            [(inner_up, early_slots, 0), (forwarded, ranks, up_column)],
            inner,
        ),
        (
            late_blocks,
            [(to_inner, ranks), (to_outer, ranks)],
            [(to_inner, ranks, up_column), (to_outer, ranks, up_column)],
            inner,
        ),
    ]
    out = None
    for blocks, panels, ups, first in phases:
        parts = reduce_parts(shrink(row_blocks, blocks, panels, first))
        out = combine(blocks, live, parts, base_mine, base_far, ups, first, out)
    return out


def on_any_pool(row_blocks, down, up, names, table, live, base, capacity):
    pool_size = lax.axis_size("pool")
    here = lax.axis_index("pool")
    holder_slots, _, depth = down.shape
    asked = table[lax.all_gather(names[0], "pool")]
    arrived = []
    for distance in range(pool_size):
        asker = lax.rem(here + distance, pool_size)
        _, slots = picks(asked[asker], here, holder_slots, capacity)
        panels = pack_panels(slots, down, up)
        pairs = [(i, (i + distance) % pool_size) for i in range(pool_size)]
        arrived.append(lax.ppermute(panels, "pool", pairs) if distance else panels)
    arrived = jnp.concatenate(arrived)
    own = asked[here]
    owners = own // holder_slots
    blocks = jnp.arange(own.shape[0], dtype=jnp.int32)
    earlier = (owners[:, None] == owners[None, :]) & (blocks[:, None] > blocks[None, :])
    ranks = jnp.sum(earlier.astype(jnp.int32), axis=1)
    place = lax.rem(here - owners + pool_size, pool_size) * capacity + ranks
    always = jnp.bool_(True)
    parts = reduce_parts(shrink(row_blocks, blocks, [(arrived, place)], always))
    ups = [(arrived, place, depth // up.shape[2])]
    return combine(blocks, live, parts, *base, ups, always, None)


def on_device(
    tokens,
    value_weight,
    adapter_down_weight,
    adapter_up_weight,
    adapter_of_block,
    adapter_pool_slot,
    live_block_tokens,
):
    pool_size = lax.axis_size("pool")
    blocks = adapter_of_block.shape[1]
    capacity = -(-blocks // pool_size)
    down = jnp.transpose(adapter_down_weight, (0, 2, 1))
    row_blocks = tokens.reshape(blocks, tokens.shape[0] // blocks, tokens.shape[1])
    base = base_sum(tokens, value_weight, adapter_up_weight.shape[2])
    whole = pool_size == 4 and blocks == capacity * pool_size
    route = on_line_of_four if whole else on_any_pool
    return route(
        row_blocks,
        down,
        adapter_up_weight,
        adapter_of_block,
        adapter_pool_slot,
        live_block_tokens[0],
        base,
        capacity,
    )


def solution(mesh):
    return jax.shard_map(
        on_device,
        mesh=mesh,
        in_specs=(
            P(("groups", "pool"), "tensor"),
            P("tensor", None),
            P(("groups", "pool"), "tensor", None),
            P(("groups", "pool"), None, "tensor"),
            P(("groups", "pool"), None),
            P("groups"),
            P(("groups", "pool"), None),
        ),
        out_specs=P(("groups", "pool"), "tensor"),
        check_vma=False,
    )
```

```python
import functools

import jax
import jax.numpy as jnp
from jax import lax
from jax.experimental import pallas as pl
from jax.experimental.pallas import tpu as pltpu
from jax.sharding import PartitionSpec as P

ADAPTER_SCALE = 0.5
ROW_TILE = 256
PARAMS = pltpu.CompilerParams(vmem_limit_bytes=16 * 1024 * 1024)
NO_COST = pl.CostEstimate(flops=0, bytes_accessed=0, transcendentals=0)
ANY = pl.BlockSpec(memory_space=pl.ANY)
SMEM = pl.BlockSpec(memory_space=pltpu.SMEM)


def swap(value, axis, distance):
    pairs = [(i, i ^ distance) for i in range(lax.axis_size(axis))]
    return lax.ppermute(value, axis, pairs)


def base_kernel(order, tokens_ref, weight_ref, *refs):
    width = refs[-1].shape[2]
    place = lax.axis_index("tensor")
    outs = refs[-2:]
    half = len(order) // 2
    for number, offset in enumerate(order):
        columns = pl.ds(pl.multiple_of((place ^ offset) * width, width), width)
        outs[number // half][number % half] = jnp.dot(
            tokens_ref[...], weight_ref[:, columns], preferred_element_type=jnp.float32
        )


def base_chunks(tokens, weight, order, width, after):
    rows, depth = tokens.shape
    tile = min(ROW_TILE, rows)
    half = len(order) // 2
    out = jax.ShapeDtypeStruct((half, rows, width), jnp.float32)
    return pl.pallas_call(
        functools.partial(base_kernel, order),
        grid=(rows // tile,),
        in_specs=[
            pl.BlockSpec((tile, depth), lambda i: (i, 0)),
            pl.BlockSpec(weight.shape, lambda i: (0, 0), pipeline_mode=pl.Buffered(1)),
        ]
        + [ANY] * len(after),
        out_specs=[pl.BlockSpec((half, tile, width), lambda i: (0, i, 0))] * 2,
        out_shape=[out, out],
        compiler_params=PARAMS,
        cost_estimate=NO_COST,
    )(tokens, weight, *after)


def add_kernel(kept_ref, arrived_ref, out_ref, mine_ref):
    half = kept_ref.shape[0] // 2
    for i in range(half):
        mine_ref[i] = kept_ref[i] + arrived_ref[i]
        out_ref[i] = kept_ref[half + i] + arrived_ref[half + i]


def add_halves(kept, arrived):
    count, rows, width = kept.shape
    tile = min(ROW_TILE, rows)
    half = count // 2
    out = jax.ShapeDtypeStruct((half, rows, width), jnp.float32)
    return pl.pallas_call(
        add_kernel,
        grid=(rows // tile,),
        in_specs=[pl.BlockSpec((count, tile, width), lambda i: (0, i, 0))] * 2,
        out_specs=[pl.BlockSpec((half, tile, width), lambda i: (0, i, 0))] * 2,
        out_shape=[out, out],
        compiler_params=PARAMS,
        cost_estimate=NO_COST,
    )(kept, arrived)


def base_sum(tokens, weight, width, after):
    size = lax.axis_size("tensor")
    kept_order = [k for k in range(size) if not k & 1]
    kept_order.sort(key=lambda k: [k >> bit & 1 for bit in range(1, size.bit_length())])
    sent, kept = base_chunks(tokens, weight, [k ^ 1 for k in kept_order] + kept_order, width, after)
    arrived = swap(sent, "tensor", 1)
    distance = 2
    while distance < size:
        sent, kept = add_halves(kept, arrived)
        arrived = swap(sent, "tensor", distance)
        distance *= 2
    return kept[0], arrived[0]


def pick(names_ref, table_ref, holder, holder_slots, count):
    blocks = [jnp.int32(0)] * count
    slots = [jnp.int32(0)] * count
    seen = jnp.int32(0)
    for j in range(names_ref.shape[1]):
        slot = table_ref[names_ref[0, j]]
        hit = lax.div(slot, jnp.int32(holder_slots)) == holder
        for k in range(count):
            chosen = hit & (seen == k)
            blocks[k] = jnp.where(chosen, jnp.int32(j), blocks[k])
            slots[k] = jnp.where(chosen, lax.rem(slot, jnp.int32(holder_slots)), slots[k])
        seen = seen + hit.astype(jnp.int32)
    return blocks, slots


def panel_copies(k, slot, down_ref, up_ref, out_ref, sems):
    depth = down_ref.shape[2]
    width = up_ref.shape[2]
    return [
        pltpu.make_async_copy(down_ref.at[slot], out_ref.at[k, :, pl.ds(0, depth)], sems.at[k, 0]),
        pltpu.make_async_copy(up_ref.at[slot], out_ref.at[k, :, pl.ds(depth, width)], sems.at[k, 1]),
    ]


def run_copies(copies):
    for copy in copies:
        copy.start()
    return copies


def plan_kernel(
    capacity,
    names_ref,
    first_ref,
    second_ref,
    third_ref,
    table_ref,
    down_ref,
    up_ref,
    near_ref,
    plan_ref,
    sems,
):
    here = lax.axis_index("pool")
    holder_slots = down_ref.shape[0]
    find = functools.partial(
        pick, table_ref=table_ref, holder_slots=holder_slots, count=capacity
    )
    copies = []
    for k, slot in enumerate(find(first_ref, holder=here)[1]):
        copies += run_copies(panel_copies(k, slot, down_ref, up_ref, near_ref, sems))
    inner = (here == 1) | (here == 2)
    own = find(names_ref, holder=here)
    near = find(names_ref, holder=here ^ 1)
    early = find(names_ref, holder=here ^ jnp.where(inner, 3, 2))
    late = find(names_ref, holder=here ^ jnp.where(inner, 2, 3))
    rows = [
        own[0],
        near[0],
        early[0],
        late[0],
        own[1],
        early[1],
        find(second_ref, holder=here)[1],
        find(third_ref, holder=here)[1],
        find(first_ref, holder=here ^ 3)[1],
        [inner.astype(jnp.int32)] * capacity,
    ]
    for number, row in enumerate(rows):
        for k in range(capacity):
            plan_ref[number * capacity + k] = row[k]
    for copy in copies:
        copy.wait()


OWN, EARLY, TO_INNER, TO_OUTER, FORWARD, INNER, PLAN_ROWS = 4, 5, 6, 7, 8, 9, 10


def make_plan(names, others, table, down, up, capacity):
    rank, depth = down.shape[1:]
    width = up.shape[2]
    return pl.pallas_call(
        functools.partial(plan_kernel, capacity),
        in_specs=[SMEM] * 5 + [ANY] * 2,
        out_specs=[ANY, SMEM],
        out_shape=[
            jax.ShapeDtypeStruct((capacity, rank, depth + width), down.dtype),
            jax.ShapeDtypeStruct((PLAN_ROWS * capacity,), jnp.int32),
        ],
        scratch_shapes=[pltpu.SemaphoreType.DMA((capacity, 2))],
        compiler_params=PARAMS,
        cost_estimate=NO_COST,
    )(names, *others, table, down, up)


def pack_kernel(starts, capacity, plan_ref, down_ref, up_ref, *rest):
    count = len(starts)
    sems = rest[-1]
    outs = rest[-1 - count : -1]
    copies = []
    for number, start in enumerate(starts):
        for k in range(capacity):
            slot = plan_ref[start + k]
            copies += run_copies(
                panel_copies(k, slot, down_ref, up_ref, outs[number], sems.at[number])
            )
    for copy in copies:
        copy.wait()


def pack_panels(plan, starts, capacity, down, up, after=()):
    rank, depth = down.shape[1:]
    width = up.shape[2]
    out = jax.ShapeDtypeStruct((capacity, rank, depth + width), down.dtype)
    return pl.pallas_call(
        functools.partial(pack_kernel, starts, capacity),
        in_specs=[SMEM] + [ANY] * (2 + len(after)),
        out_specs=[ANY] * len(starts),
        out_shape=[out] * len(starts),
        scratch_shapes=[pltpu.SemaphoreType.DMA((len(starts), capacity, 2))],
        compiler_params=PARAMS,
        cost_estimate=NO_COST,
    )(plan, down, up, *after)


def step_of(i, start, count):
    return jnp.clip(i - start, 0, count - 1)


def source_specs(phases, shape, columns):
    specs, operands, start = [], [], 0
    for (_, count, sources), places in zip(phases, columns):
        for (panels, row), column in zip(sources, places):

            def index(i, plan, *_, start=start, count=count, row=row, column=column):
                k = step_of(i, start, count)
                return (k if row is None else plan[row + k], 0, column)

            specs.append(pl.BlockSpec(shape, index))
            operands.append(panels)
        start += count
    return specs, operands


def block_index(phases):
    def index(i, plan):
        found, start = jnp.int32(0), 0
        for row, count, _ in phases:
            inside = (i >= start) & (i < start + count)
            found = jnp.where(inside, plan[row + step_of(i, start, count)], found)
            start += count
        return found

    return index


def for_phase(phases, choose, plan_ref, refs, act):
    start, at = 0, 0
    step = pl.program_id(0)
    for _, count, sources in phases:
        mine = refs[at : at + len(sources)]

        @pl.when((step >= start) & (step < start + count))
        def _(mine=mine):
            if len(mine) == 1:
                act(mine[0])
            else:
                first = plan_ref[choose] != 0
                pl.when(first)(lambda: act(mine[0]))
                pl.when(jnp.logical_not(first))(lambda: act(mine[1]))

        start += count
        at += len(sources)


def shrink_kernel(phases, choose, plan_ref, token_ref, *refs):
    out_ref = refs[-1]

    def act(panel_ref):
        out_ref[0] = lax.dot_general(
            panel_ref[0],
            token_ref[0],
            (((1,), (1,)), ((), ())),
            preferred_element_type=jnp.float32,
        )

    for_phase(phases, choose, plan_ref, refs, act)


def shrink(plan, row_blocks, phases, choose, after=()):
    rows, depth = row_blocks.shape[1:]
    rank = phases[0][2][0][0].shape[1]
    total = sum(count for _, count, _ in phases)
    columns = [[0] * len(sources) for _, _, sources in phases]
    specs, operands = source_specs(phases, (1, rank, depth), columns)
    block = block_index(phases)
    shapes = [(row, count, [None] * len(sources)) for row, count, sources in phases]
    return pl.pallas_call(
        functools.partial(shrink_kernel, shapes, choose),
        grid_spec=pltpu.PrefetchScalarGridSpec(
            num_scalar_prefetch=1,
            grid=(total,),
            in_specs=[pl.BlockSpec((1, rows, depth), lambda i, plan: (block(i, plan), 0, 0))]
            + specs
            + [ANY] * len(after),
            out_specs=pl.BlockSpec((1, rank, rows), lambda i, plan: (i, 0, 0)),
        ),
        out_shape=jax.ShapeDtypeStruct((total, rank, rows), jnp.float32),
        compiler_params=PARAMS,
        cost_estimate=NO_COST,
    )(plan, row_blocks, *operands, *after)


def exchange(part):
    return [part] + [swap(part, "tensor", m) for m in range(1, lax.axis_size("tensor"))]


def combine_kernel(phases, choose, part_count, block, plan_ref, live_ref, *refs):
    parts = refs[:part_count]
    mine_ref, far_ref = refs[part_count : part_count + 2]
    out_ref = refs[-1]
    total = parts[0][0]
    for part in parts[1:]:
        total = total + part[0]
    shrunk = total.astype(jnp.bfloat16)
    live = live_ref[block(pl.program_id(0), plan_ref)]

    def act(up_ref):
        delta = lax.dot_general(
            shrunk, up_ref[0], (((0,), (0,)), ((), ())), preferred_element_type=jnp.float32
        )
        row = lax.broadcasted_iota(jnp.int32, delta.shape, 0)
        value = mine_ref[...] + far_ref[...] + ADAPTER_SCALE * delta
        out_ref[...] = jnp.where(row < live, value, 0.0).astype(out_ref.dtype)

    for_phase(phases, choose, plan_ref, refs[part_count + 2 :], act)


def combine(plan, live, parts, base, phases, columns, choose, out=None, after=()):
    rank, block_rows = parts[0].shape[1:]
    rows, width = base[0].shape
    total = sum(count for _, count, _ in phases)
    block = block_index(phases)
    specs = [pl.BlockSpec((1, rank, block_rows), lambda i, plan, live: (i, 0, 0))] * len(parts)
    specs += [pl.BlockSpec((block_rows, width), lambda i, plan, live: (block(i, plan), 0))] * 2
    more, operands = source_specs(phases, (1, rank, width), columns)
    specs += more + [ANY] * len(after)
    operands = [*parts, *base, *operands, *after]
    aliases = {}
    if out is not None:
        specs.append(ANY)
        operands.append(out)
        aliases = {1 + len(operands): 0}
    shapes = [(row, count, [None] * len(sources)) for row, count, sources in phases]
    return pl.pallas_call(
        functools.partial(combine_kernel, shapes, choose, len(parts), block_index(shapes)),
        grid_spec=pltpu.PrefetchScalarGridSpec(
            num_scalar_prefetch=2,
            grid=(total,),
            in_specs=specs,
            out_specs=pl.BlockSpec(
                (block_rows, width), lambda i, plan, live: (block(i, plan), 0)
            ),
        ),
        out_shape=jax.ShapeDtypeStruct((rows, width), jnp.bfloat16),
        input_output_aliases=aliases,
        compiler_params=PARAMS,
        cost_estimate=NO_COST,
    )(plan, live, *operands)


def on_line_of_four(tokens, weight, row_blocks, down, up, names, table, live, capacity):
    up_column = down.shape[2] // up.shape[2]

    def across(value, pairs):
        return lax.ppermute(value, "pool", pairs)

    others = [swap(names, "pool", m) for m in range(1, 4)]
    inner_down = across(down, [(1, 2), (2, 1)])
    inner_up = across(up, [(1, 2), (2, 1)])
    near_out, plan = make_plan(names, others, table, down, up, capacity)
    near = across(near_out, [(0, 1), (1, 0), (2, 3), (3, 2)])
    base = base_sum(tokens, weight, up.shape[2], [near_out])
    inner_out, outer_out = pack_panels(
        plan, [TO_INNER * capacity, TO_OUTER * capacity], capacity, down, up, [near]
    )
    to_inner = across(inner_out, [(0, 2), (3, 1)])
    to_outer = across(outer_out, [(0, 3), (3, 0)])
    (forward_out,) = pack_panels(
        plan, [FORWARD * capacity], capacity, inner_down, inner_up, [outer_out]
    )
    forwarded = across(forward_out, [(1, 0), (2, 3)])

    choose = INNER * capacity
    first = [
        (0, capacity, [(down, OWN * capacity)]),
        (capacity, capacity, [(near, None)]),
        (2 * capacity, capacity, [(inner_down, EARLY * capacity), (forwarded, None)]),
    ]
    last = [(3 * capacity, capacity, [(to_inner, None), (to_outer, None)])]
    first_up = [
        (0, capacity, [(up, OWN * capacity)]),
        (capacity, capacity, [(near, None)]),
        (2 * capacity, capacity, [(inner_up, EARLY * capacity), (forwarded, None)]),
    ]
    first_columns = [[0], [up_column], [0, up_column]]
    first_part = shrink(plan, row_blocks, first, choose)
    first_parts = exchange(first_part)
    last_part = shrink(plan, row_blocks, last, choose, [first_part])
    last_parts = exchange(last_part)
    out = combine(
        plan, live, first_parts, base, first_up, first_columns, choose, after=[last_part]
    )
    return combine(plan, live, last_parts, base, last, [[up_column] * 2], choose, out)


def on_any_pool(tokens, weight, row_blocks, down, up, names, table, live, capacity):
    pool_size = lax.axis_size("pool")
    here = lax.axis_index("pool")
    holder_slots, _, depth = down.shape
    asked = table[lax.all_gather(names[0], "pool")]
    count = jnp.arange(capacity, dtype=jnp.int32)
    arrived = []
    for distance in range(pool_size):
        slots = asked[lax.rem(here + distance, pool_size)]
        hit = slots // holder_slots == here
        chosen = hit[None, :] & (jnp.cumsum(hit.astype(jnp.int32))[None, :] == 1 + count[:, None])
        plan = jnp.sum(jnp.where(chosen, (slots % holder_slots)[None, :], 0), axis=1)
        (panels,) = pack_panels(plan, [0], capacity, down, up)
        pairs = [(i, (i + distance) % pool_size) for i in range(pool_size)]
        arrived.append(lax.ppermute(panels, "pool", pairs) if distance else panels)
    arrived = jnp.concatenate(arrived)
    owners = asked[here] // holder_slots
    blocks = jnp.arange(owners.shape[0], dtype=jnp.int32)
    earlier = (owners[:, None] == owners[None, :]) & (blocks[:, None] > blocks[None, :])
    ranks = jnp.sum(earlier.astype(jnp.int32), axis=1)
    places = lax.rem(here - owners + pool_size, pool_size) * capacity + ranks
    plan = jnp.concatenate([blocks, places])
    base = base_sum(tokens, weight, up.shape[2], [])
    phases = [(0, blocks.shape[0], [(arrived, blocks.shape[0])])]
    parts = exchange(shrink(plan, row_blocks, phases, 0))
    return combine(plan, live, parts, base, phases, [[depth // up.shape[2]]], 0)


def on_device(
    tokens,
    value_weight,
    adapter_down_weight,
    adapter_up_weight,
    adapter_of_block,
    adapter_pool_slot,
    live_block_tokens,
):
    pool_size = lax.axis_size("pool")
    blocks = adapter_of_block.shape[1]
    capacity = -(-blocks // pool_size)
    row_blocks = tokens.reshape(blocks, tokens.shape[0] // blocks, tokens.shape[1])
    line = pool_size == 4 and blocks == capacity * pool_size
    route = on_line_of_four if line else on_any_pool
    return route(
        tokens,
        value_weight,
        row_blocks,
        jnp.transpose(adapter_down_weight, (0, 2, 1)),
        adapter_up_weight,
        adapter_of_block,
        adapter_pool_slot,
        live_block_tokens[0],
        capacity,
    )


def solution(mesh):
    return jax.shard_map(
        on_device,
        mesh=mesh,
        in_specs=(
            P(("groups", "pool"), "tensor"),
            P("tensor", None),
            P(("groups", "pool"), "tensor", None),
            P(("groups", "pool"), None, "tensor"),
            P(("groups", "pool"), None),
            P("groups"),
            P(("groups", "pool"), None),
        ),
        out_specs=P(("groups", "pool"), "tensor"),
        check_vma=False,
    )
```

```python
import functools

import jax
import jax.numpy as jnp
from jax import lax
from jax.experimental import pallas as pl
from jax.experimental.pallas import tpu as pltpu
from jax.sharding import PartitionSpec as P

ADAPTER_SCALE = 0.5
ROW_TILE = 128
PARAMS = pltpu.CompilerParams(vmem_limit_bytes=20 * 1024 * 1024)
NO_COST = pl.CostEstimate(flops=0, bytes_accessed=0, transcendentals=0)
LONG = pl.CostEstimate(flops=4 * 10**10, bytes_accessed=0, transcendentals=0)
ANY = pl.BlockSpec(memory_space=pl.ANY)
SMEM = pl.BlockSpec(memory_space=pltpu.SMEM)


def in_hbm(value):
    return pltpu.with_memory_space_constraint(value, pltpu.HBM)


def swap(value, axis, distance):
    pairs = [(i, i ^ distance) for i in range(lax.axis_size(axis))]
    return lax.ppermute(value, axis, pairs)


def piece_rows(rows):
    tile = min(ROW_TILE, rows)
    tiles = rows // tile
    counts = [(tiles + 2 - i) // 3 for i in range(3)]
    return [count * tile for count in counts if count]


def base_kernel(order, tokens_ref, weight_ref, *refs):
    kept_ref = refs[-1]
    half, rows, width = kept_ref.shape
    sizes = piece_rows(rows)
    sent_refs = refs[-1 - len(sizes) : -1]
    place = lax.axis_index("tensor")
    step = pl.program_id(0)
    columns = place ^ jnp.where(step < half, order[0], order[half])
    for number in range(1, half):
        columns = jnp.where(step == number, place ^ order[number], columns)
        columns = jnp.where(step == half + number, place ^ order[half + number], columns)
    columns = pl.ds(pl.multiple_of(columns * width, width), width)
    start = 0
    for sent_ref, size in zip(sent_refs, sizes):
        part = jnp.dot(
            tokens_ref[start : start + size, :],
            weight_ref[:, columns],
            preferred_element_type=jnp.float32,
        )

        @pl.when(step < half)
        def _(sent_ref=sent_ref, part=part):
            sent_ref[jnp.minimum(step, half - 1)] = part

        @pl.when(step >= half)
        def _(start=start, size=size, part=part):
            kept_ref[jnp.maximum(step - half, 0), start : start + size, :] = part

        start += size


def base_chunks(tokens, weight, order, width, after):
    rows, depth = tokens.shape
    half = len(order) // 2
    shapes = [(half, size, width) for size in piece_rows(rows)] + [(half, rows, width)]
    *sent, kept = pl.pallas_call(
        functools.partial(base_kernel, order),
        grid=(len(order),),
        in_specs=[
            pl.BlockSpec(tokens.shape, lambda i: (0, 0), pipeline_mode=pl.Buffered(1)),
            pl.BlockSpec(weight.shape, lambda i: (0, 0), pipeline_mode=pl.Buffered(1)),
        ]
        + [ANY] * len(after),
        out_specs=[pl.BlockSpec(shape, lambda i: (0, 0, 0)) for shape in shapes],
        out_shape=[jax.ShapeDtypeStruct(shape, jnp.float32) for shape in shapes],
        compiler_params=PARAMS,
        cost_estimate=NO_COST,
    )(in_hbm(tokens), in_hbm(weight), *after)
    return sent, kept


def add_kernel(kept_ref, *refs):
    *arrived_refs, out_ref, mine_ref = refs
    half = kept_ref.shape[0] // 2
    start = 0
    for arrived_ref in arrived_refs:
        rows = pl.ds(start, arrived_ref.shape[1])
        for i in range(half):
            mine_ref[i, rows, :] = kept_ref[i, rows, :] + arrived_ref[i]
            out_ref[i, rows, :] = kept_ref[half + i, rows, :] + arrived_ref[half + i]
        start += arrived_ref.shape[1]


def add_halves(kept, arrived):
    count, rows, width = kept.shape
    out = jax.ShapeDtypeStruct((count // 2, rows, width), jnp.float32)
    return pl.pallas_call(
        add_kernel,
        out_shape=[out, out],
        compiler_params=PARAMS,
        cost_estimate=NO_COST,
    )(kept, *arrived)


def base_sum(tokens, weight, width, after):
    size = lax.axis_size("tensor")
    kept_order = [k for k in range(size) if not k & 1]
    kept_order.sort(key=lambda k: [k >> bit & 1 for bit in range(1, size.bit_length())])
    sent, kept = base_chunks(tokens, weight, [k ^ 1 for k in kept_order] + kept_order, width, after)
    arrived = [swap(piece, "tensor", 1) for piece in sent]
    distance = 2
    while distance < size:
        sent, kept = add_halves(kept, arrived)
        arrived = [swap(sent, "tensor", distance)]
        distance *= 2
    return kept[0], arrived[0][0]


def pick(names_ref, table_ref, holder, holder_slots, count):
    blocks = [jnp.int32(0)] * count
    slots = [jnp.int32(0)] * count
    seen = jnp.int32(0)
    for j in range(names_ref.shape[1]):
        slot = table_ref[names_ref[0, j]]
        hit = lax.div(slot, jnp.int32(holder_slots)) == holder
        for k in range(count):
            chosen = hit & (seen == k)
            blocks[k] = jnp.where(chosen, jnp.int32(j), blocks[k])
            slots[k] = jnp.where(chosen, lax.rem(slot, jnp.int32(holder_slots)), slots[k])
        seen = seen + hit.astype(jnp.int32)
    return blocks, slots


def panel_copies(k, slot, down_ref, up_ref, out_ref, sems):
    depth = down_ref.shape[2]
    width = up_ref.shape[2]
    return [
        pltpu.make_async_copy(down_ref.at[slot], out_ref.at[k, :, pl.ds(0, depth)], sems.at[k, 0]),
        pltpu.make_async_copy(up_ref.at[slot], out_ref.at[k, :, pl.ds(depth, width)], sems.at[k, 1]),
    ]


def run_copies(copies):
    for copy in copies:
        copy.start()
    return copies


def plan_kernel(capacity, *refs):
    sources, down_ref, up_ref, near_ref, plan_ref = refs[:6], *refs[6:10]
    scalars, scalar_sems, sems = refs[10:16], *refs[16:]
    loads = [
        pltpu.make_async_copy(source, scalar, scalar_sems.at[i])
        for i, (source, scalar) in enumerate(zip(sources, scalars))
    ]
    for load in run_copies(loads):
        load.wait()
    names_ref, first_ref, second_ref, third_ref, table_ref, live_ref = scalars
    here = lax.axis_index("pool")
    holder_slots = down_ref.shape[0]
    find = functools.partial(
        pick, table_ref=table_ref, holder_slots=holder_slots, count=capacity
    )
    copies = []
    for k, slot in enumerate(find(first_ref, holder=here)[1]):
        copies += run_copies(panel_copies(k, slot, down_ref, up_ref, near_ref, sems))
    inner = (here == 1) | (here == 2)
    own = find(names_ref, holder=here)
    near = find(names_ref, holder=here ^ 1)
    early = find(names_ref, holder=here ^ jnp.where(inner, 3, 2))
    late = find(names_ref, holder=here ^ jnp.where(inner, 2, 3))
    rows = [
        own[0],
        near[0],
        early[0],
        late[0],
        own[1],
        early[1],
        find(second_ref, holder=here)[1],
        find(third_ref, holder=here)[1],
        find(first_ref, holder=here ^ 3)[1],
        [inner.astype(jnp.int32)] * capacity,
        *[[live_ref[0, block] for block in phase[0]] for phase in (own, near, early, late)],
    ]
    for number, row in enumerate(rows):
        for k in range(capacity):
            plan_ref[number * capacity + k] = row[k]
    for copy in copies:
        copy.wait()


OWN, EARLY, TO_INNER, TO_OUTER, FORWARD, INNER, LIVE, PLAN_ROWS = 4, 5, 6, 7, 8, 9, 10, 14


def make_plan(names, others, table, live, down, up, capacity):
    rank, depth = down.shape[1:]
    width = up.shape[2]
    return pl.pallas_call(
        functools.partial(plan_kernel, capacity),
        in_specs=[ANY] * 8,
        out_specs=[ANY, SMEM],
        out_shape=[
            jax.ShapeDtypeStruct((capacity, rank, depth + width), down.dtype),
            jax.ShapeDtypeStruct((PLAN_ROWS * capacity,), jnp.int32),
        ],
        scratch_shapes=[pltpu.SMEM(names.shape, jnp.int32)] * 4
        + [pltpu.SMEM(table.shape, jnp.int32), pltpu.SMEM(live.shape, jnp.int32)]
        + [pltpu.SemaphoreType.DMA((6,)), pltpu.SemaphoreType.DMA((capacity, 2))],
        compiler_params=PARAMS,
        cost_estimate=NO_COST,
    )(in_hbm(names), *others, *[in_hbm(a) for a in (table, live, down, up)])


def pack_kernel(starts, capacity, plan_ref, down_ref, up_ref, *rest):
    count = len(starts)
    sems = rest[-1]
    outs = rest[-1 - count : -1]
    copies = []
    for number, start in enumerate(starts):
        for k in range(capacity):
            slot = plan_ref[start + k]
            copies += run_copies(
                panel_copies(k, slot, down_ref, up_ref, outs[number], sems.at[number])
            )
    for copy in copies:
        copy.wait()


def pack_panels(plan, starts, capacity, down, up, after=(), cost=None):
    rank, depth = down.shape[1:]
    width = up.shape[2]
    out = jax.ShapeDtypeStruct((capacity, rank, depth + width), down.dtype)
    return pl.pallas_call(
        functools.partial(pack_kernel, starts, capacity),
        in_specs=[SMEM] + [ANY] * (2 + len(after)),
        out_specs=[ANY] * len(starts),
        out_shape=[out] * len(starts),
        scratch_shapes=[pltpu.SemaphoreType.DMA((len(starts), capacity, 2))],
        compiler_params=PARAMS,
        cost_estimate=cost or NO_COST,
    )(plan, down, up, *after)


def step_of(i, start, count):
    return jnp.clip(i - start, 0, count - 1)


def source_specs(phases, shape, columns):
    specs, operands, start = [], [], 0
    for (_, count, sources), places in zip(phases, columns):
        for (panels, row), column in zip(sources, places):

            def index(i, plan, *_, start=start, count=count, row=row, column=column):
                k = step_of(i, start, count)
                return (k if row is None else plan[row + k], 0, column)

            specs.append(pl.BlockSpec(shape, index))
            operands.append(panels)
        start += count
    return specs, operands


def block_index(phases):
    def index(i, plan):
        found, start = jnp.int32(0), 0
        for row, count, _ in phases:
            inside = (i >= start) & (i < start + count)
            found = jnp.where(inside, plan[row + step_of(i, start, count)], found)
            start += count
        return found

    return index


def for_phase(phases, choose, plan_ref, refs, act):
    start, at = 0, 0
    step = pl.program_id(0)
    for _, count, sources in phases:
        mine = refs[at : at + len(sources)]

        @pl.when((step >= start) & (step < start + count))
        def _(mine=mine):
            if len(mine) == 1:
                act(mine[0])
            else:
                first = plan_ref[choose] != 0
                pl.when(first)(lambda: act(mine[0]))
                pl.when(jnp.logical_not(first))(lambda: act(mine[1]))

        start += count
        at += len(sources)


def shrink_kernel(phases, choose, plan_ref, token_ref, *refs):
    out_ref = refs[-1]

    def act(panel_ref):
        out_ref[0] = lax.dot_general(
            panel_ref[0],
            token_ref[0],
            (((1,), (1,)), ((), ())),
            preferred_element_type=jnp.float32,
        )

    for_phase(phases, choose, plan_ref, refs, act)


def shrink(plan, row_blocks, phases, choose, after=()):
    rows, depth = row_blocks.shape[1:]
    rank = phases[0][2][0][0].shape[1]
    total = sum(count for _, count, _ in phases)
    columns = [[0] * len(sources) for _, _, sources in phases]
    specs, operands = source_specs(phases, (1, rank, depth), columns)
    block = block_index(phases)
    shapes = [(row, count, [None] * len(sources)) for row, count, sources in phases]
    return pl.pallas_call(
        functools.partial(shrink_kernel, shapes, choose),
        grid_spec=pltpu.PrefetchScalarGridSpec(
            num_scalar_prefetch=1,
            grid=(total,),
            in_specs=[pl.BlockSpec((1, rows, depth), lambda i, plan: (block(i, plan), 0, 0))]
            + specs
            + [ANY] * len(after),
            out_specs=pl.BlockSpec((1, rank, rows), lambda i, plan: (i, 0, 0)),
        ),
        out_shape=jax.ShapeDtypeStruct((total, rank, rows), jnp.float32),
        compiler_params=PARAMS,
        cost_estimate=NO_COST,
    )(plan, row_blocks, *operands, *after)


def exchange(part):
    return [part] + [swap(part, "tensor", m) for m in range(1, lax.axis_size("tensor"))]


def combine_kernel(phases, choose, part_count, live_row, plan_ref, *refs):
    parts = refs[:part_count]
    mine_ref, far_ref = refs[part_count : part_count + 2]
    out_ref = refs[-1]
    total = parts[0][0]
    for part in parts[1:]:
        total = total + part[0]
    shrunk = total.astype(jnp.bfloat16)
    live = plan_ref[live_row + pl.program_id(0)]

    def act(up_ref):
        delta = lax.dot_general(
            shrunk, up_ref[0], (((0,), (0,)), ((), ())), preferred_element_type=jnp.float32
        )
        row = lax.broadcasted_iota(jnp.int32, delta.shape, 0)
        value = mine_ref[...] + far_ref[...] + ADAPTER_SCALE * delta
        out_ref[...] = jnp.where(row < live, value, 0.0).astype(out_ref.dtype)

    for_phase(phases, choose, plan_ref, refs[part_count + 2 :], act)


def combine(plan, live_row, parts, base, phases, columns, choose, out=None, after=()):
    rank, block_rows = parts[0].shape[1:]
    rows, width = base[0].shape
    total = sum(count for _, count, _ in phases)
    block = block_index(phases)
    specs = [pl.BlockSpec((1, rank, block_rows), lambda i, plan: (i, 0, 0))] * len(parts)
    specs += [pl.BlockSpec((block_rows, width), lambda i, plan: (block(i, plan), 0))] * 2
    more, operands = source_specs(phases, (1, rank, width), columns)
    specs += more + [ANY] * len(after)
    operands = [*parts, *base, *operands, *after]
    aliases = {}
    if out is not None:
        specs.append(ANY)
        operands.append(out)
        aliases = {len(operands): 0}
    shapes = [(row, count, [None] * len(sources)) for row, count, sources in phases]
    return pl.pallas_call(
        functools.partial(combine_kernel, shapes, choose, len(parts), live_row),
        grid_spec=pltpu.PrefetchScalarGridSpec(
            num_scalar_prefetch=1,
            grid=(total,),
            in_specs=specs,
            out_specs=pl.BlockSpec((block_rows, width), lambda i, plan: (block(i, plan), 0)),
        ),
        out_shape=jax.ShapeDtypeStruct((rows, width), jnp.bfloat16),
        input_output_aliases=aliases,
        compiler_params=PARAMS,
        cost_estimate=NO_COST,
    )(plan, *operands)


def on_line_of_four(tokens, weight, row_blocks, down, up, names, table, live, capacity):
    up_column = down.shape[2] // up.shape[2]

    def across(value, pairs):
        return lax.ppermute(value, "pool", pairs)

    others = [swap(names, "pool", m) for m in range(1, 4)]
    inner_down = across(down, [(1, 2), (2, 1)])
    inner_up = across(up, [(1, 2), (2, 1)])
    near_out, plan = make_plan(names, others, table, live, down, up, capacity)
    near = across(near_out, [(0, 1), (1, 0), (2, 3), (3, 2)])
    base = base_sum(tokens, weight, up.shape[2], [near_out])
    inner_out, outer_out = pack_panels(
        plan,
        [TO_INNER * capacity, TO_OUTER * capacity],
        capacity,
        in_hbm(down),
        in_hbm(up),
        [base[0]],
    )
    to_inner = across(inner_out, [(0, 2), (3, 1)])
    to_outer = across(outer_out, [(0, 3), (3, 0)])
    forward_out = pack_panels(
        plan,
        [FORWARD * capacity + k for k in range(capacity)],
        1,
        inner_down,
        inner_up,
        [outer_out, near],
        LONG,
    )
    forwarded = [across(panel, [(1, 0), (2, 3)]) for panel in forward_out]

    choose = INNER * capacity
    first = [
        (0, capacity, [(down, OWN * capacity)]),
        (capacity, capacity, [(near, None)]),
        *[
            (2 * capacity + k, 1, [(inner_down, EARLY * capacity + k), (forwarded[k], None)])
            for k in range(capacity)
        ],
    ]
    last = [(3 * capacity, capacity, [(to_inner, None), (to_outer, None)])]
    first_up = [
        (0, capacity, [(up, OWN * capacity)]),
        (capacity, capacity, [(near, None)]),
        *[
            (2 * capacity + k, 1, [(inner_up, EARLY * capacity + k), (forwarded[k], None)])
            for k in range(capacity)
        ],
    ]
    first_columns = [[0], [up_column]] + [[0, up_column]] * capacity
    first_parts = exchange(shrink(plan, row_blocks, first, choose))
    out = combine(
        plan, LIVE * capacity, first_parts, base, first_up, first_columns, choose
    )
    last_parts = exchange(shrink(plan, row_blocks, last, choose, [out]))
    last_columns = [[up_column] * 2]
    return combine(
        plan, (LIVE + 3) * capacity, last_parts, base, last, last_columns, choose, out
    )


def on_any_pool(tokens, weight, row_blocks, down, up, names, table, live, capacity):
    pool_size = lax.axis_size("pool")
    here = lax.axis_index("pool")
    holder_slots, _, depth = down.shape
    asked = table[lax.all_gather(names[0], "pool")]
    count = jnp.arange(capacity, dtype=jnp.int32)
    arrived = []
    for distance in range(pool_size):
        slots = asked[lax.rem(here + distance, pool_size)]
        hit = slots // holder_slots == here
        chosen = hit[None, :] & (jnp.cumsum(hit.astype(jnp.int32))[None, :] == 1 + count[:, None])
        plan = jnp.sum(jnp.where(chosen, (slots % holder_slots)[None, :], 0), axis=1)
        (panels,) = pack_panels(plan, [0], capacity, down, up)
        pairs = [(i, (i + distance) % pool_size) for i in range(pool_size)]
        arrived.append(lax.ppermute(panels, "pool", pairs) if distance else panels)
    arrived = jnp.concatenate(arrived)
    owners = asked[here] // holder_slots
    blocks = jnp.arange(owners.shape[0], dtype=jnp.int32)
    earlier = (owners[:, None] == owners[None, :]) & (blocks[:, None] > blocks[None, :])
    ranks = jnp.sum(earlier.astype(jnp.int32), axis=1)
    places = lax.rem(here - owners + pool_size, pool_size) * capacity + ranks
    plan = jnp.concatenate([blocks, places, live[0]])
    base = base_sum(tokens, weight, up.shape[2], [])
    phases = [(0, blocks.shape[0], [(arrived, blocks.shape[0])])]
    parts = exchange(shrink(plan, row_blocks, phases, 0))
    live_row = 2 * blocks.shape[0]
    return combine(plan, live_row, parts, base, phases, [[depth // up.shape[2]]], 0)


def on_device(
    tokens,
    value_weight,
    adapter_down_weight,
    adapter_up_weight,
    adapter_of_block,
    adapter_pool_slot,
    live_block_tokens,
):
    pool_size = lax.axis_size("pool")
    blocks = adapter_of_block.shape[1]
    capacity = -(-blocks // pool_size)
    row_blocks = tokens.reshape(blocks, tokens.shape[0] // blocks, tokens.shape[1])
    line = pool_size == 4 and blocks == capacity * pool_size
    route = on_line_of_four if line else on_any_pool
    return route(
        tokens,
        value_weight,
        row_blocks,
        jnp.transpose(adapter_down_weight, (0, 2, 1)),
        adapter_up_weight,
        adapter_of_block,
        adapter_pool_slot,
        live_block_tokens,
        capacity,
    )


def solution(mesh):
    return jax.shard_map(
        on_device,
        mesh=mesh,
        in_specs=(
            P(("groups", "pool"), "tensor"),
            P("tensor", None),
            P(("groups", "pool"), "tensor", None),
            P(("groups", "pool"), None, "tensor"),
            P(("groups", "pool"), None),
            P("groups"),
            P(("groups", "pool"), None),
        ),
        out_specs=P(("groups", "pool"), "tensor"),
        check_vma=False,
    )
```

```python
import functools

import jax
import jax.numpy as jnp
from jax import lax
from jax.experimental import pallas as pl
from jax.experimental.pallas import tpu as pltpu
from jax.sharding import PartitionSpec as P

ADAPTER_SCALE = 0.5
ROW_TILE = 256
PARAMS = pltpu.CompilerParams(vmem_limit_bytes=16 * 1024 * 1024)
NO_COST = pl.CostEstimate(flops=0, bytes_accessed=0, transcendentals=0)
SHORT = pl.CostEstimate(flops=4 * 10**9, bytes_accessed=0, transcendentals=0)
LONG = pl.CostEstimate(flops=6 * 10**9, bytes_accessed=0, transcendentals=0)
ANY = pl.BlockSpec(memory_space=pl.ANY)
SMEM = pl.BlockSpec(memory_space=pltpu.SMEM)


def in_hbm(value):
    return pltpu.with_memory_space_constraint(value, pltpu.HBM)


def swap(value, axis, distance):
    pairs = [(i, i ^ distance) for i in range(lax.axis_size(axis))]
    return lax.ppermute(value, axis, pairs)


def piece_rows(rows):
    large = rows * 7 // 16
    return [large, large, rows - 2 * large]


def base_kernel(order, tokens_ref, weight_ref, *refs):
    kept_ref = refs[-1]
    half, tile, width = kept_ref.shape
    sizes = piece_rows(tile * pl.num_programs(0))
    sent_refs = refs[-1 - len(sizes) : -1]
    place = lax.axis_index("tensor")
    for number, offset in enumerate(order):
        columns = pl.ds(pl.multiple_of((place ^ offset) * width, width), width)
        part = jnp.dot(
            tokens_ref[...], weight_ref[:, columns], preferred_element_type=jnp.float32
        )
        if number >= half:
            kept_ref[number - half] = part
            continue
        for step in range(pl.num_programs(0)):

            @pl.when(pl.program_id(0) == step)
            def _(number=number, part=part, first=step * tile):
                start = 0
                for sent_ref, size in zip(sent_refs, sizes):
                    low, high = max(first, start), min(first + tile, start + size)
                    if low < high:
                        rows = slice(low - start, high - start)
                        sent_ref[number, rows, :] = part[low - first : high - first]
                    start += size


def base_chunks(tokens, weight, order, width, after):
    rows, depth = tokens.shape
    tile = min(ROW_TILE, rows)
    half = len(order) // 2
    pieces = [(half, size, width) for size in piece_rows(rows)]
    *sent, kept = pl.pallas_call(
        functools.partial(base_kernel, order),
        grid=(rows // tile,),
        in_specs=[
            pl.BlockSpec((tile, depth), lambda i: (i, 0)),
            pl.BlockSpec(weight.shape, lambda i: (0, 0), pipeline_mode=pl.Buffered(1)),
        ]
        + [ANY] * len(after),
        out_specs=[pl.BlockSpec(shape, lambda i: (0, 0, 0)) for shape in pieces]
        + [pl.BlockSpec((half, tile, width), lambda i: (0, i, 0))],
        out_shape=[
            jax.ShapeDtypeStruct(shape, jnp.float32) for shape in [*pieces, (half, rows, width)]
        ],
        compiler_params=PARAMS,
        cost_estimate=NO_COST,
    )(in_hbm(tokens), in_hbm(weight), *after)
    return sent, kept


def add_kernel(kept_ref, *refs):
    *arrived_refs, out_ref, mine_ref = refs
    half = kept_ref.shape[0] // 2
    start = 0
    for arrived_ref in arrived_refs:
        rows = pl.ds(start, arrived_ref.shape[1])
        for i in range(half):
            mine_ref[i, rows, :] = kept_ref[i, rows, :] + arrived_ref[i]
            out_ref[i, rows, :] = kept_ref[half + i, rows, :] + arrived_ref[half + i]
        start += arrived_ref.shape[1]


def add_halves(kept, arrived):
    count, rows, width = kept.shape
    out = jax.ShapeDtypeStruct((count // 2, rows, width), jnp.float32)
    return pl.pallas_call(
        add_kernel,
        out_shape=[out, out],
        compiler_params=PARAMS,
        cost_estimate=NO_COST,
    )(kept, *arrived)


def base_sum(tokens, weight, width, after):
    size = lax.axis_size("tensor")
    kept_order = [k for k in range(size) if not k & 1]
    kept_order.sort(key=lambda k: [k >> bit & 1 for bit in range(1, size.bit_length())])
    sent, kept = base_chunks(tokens, weight, [k ^ 1 for k in kept_order] + kept_order, width, after)
    arrived = [swap(piece, "tensor", 1) for piece in sent]
    distance = 2
    while distance < size:
        sent, kept = add_halves(kept, arrived)
        arrived = [swap(sent, "tensor", distance)]
        distance *= 2
    return kept[0], arrived[0][0]


def pick(names_ref, table_ref, holder, holder_slots, count):
    blocks = [jnp.int32(0)] * count
    slots = [jnp.int32(0)] * count
    seen = jnp.int32(0)
    for j in range(names_ref.shape[1]):
        slot = table_ref[names_ref[0, j]]
        hit = lax.div(slot, jnp.int32(holder_slots)) == holder
        for k in range(count):
            chosen = hit & (seen == k)
            blocks[k] = jnp.where(chosen, jnp.int32(j), blocks[k])
            slots[k] = jnp.where(chosen, lax.rem(slot, jnp.int32(holder_slots)), slots[k])
        seen = seen + hit.astype(jnp.int32)
    return blocks, slots


def panel_copies(k, slot, down_ref, up_ref, out_ref, sems):
    depth = down_ref.shape[2]
    width = up_ref.shape[2]
    return [
        pltpu.make_async_copy(down_ref.at[slot], out_ref.at[k, :, pl.ds(0, depth)], sems.at[k, 0]),
        pltpu.make_async_copy(up_ref.at[slot], out_ref.at[k, :, pl.ds(depth, width)], sems.at[k, 1]),
    ]


def run_copies(copies):
    for copy in copies:
        copy.start()
    return copies


def plan_kernel(capacity, *refs):
    sources, down_ref, up_ref, near_ref, plan_ref = refs[:6], *refs[6:10]
    scalars, scalar_sems, sems = refs[10:16], *refs[16:]
    loads = [
        pltpu.make_async_copy(source, scalar, scalar_sems.at[i])
        for i, (source, scalar) in enumerate(zip(sources, scalars))
    ]
    for load in run_copies(loads):
        load.wait()
    names_ref, first_ref, second_ref, third_ref, table_ref, live_ref = scalars
    here = lax.axis_index("pool")
    holder_slots = down_ref.shape[0]
    find = functools.partial(
        pick, table_ref=table_ref, holder_slots=holder_slots, count=capacity
    )
    copies = []
    for k, slot in enumerate(find(first_ref, holder=here)[1]):
        copies += run_copies(panel_copies(k, slot, down_ref, up_ref, near_ref, sems))
    inner = (here == 1) | (here == 2)
    own = find(names_ref, holder=here)
    near = find(names_ref, holder=here ^ 1)
    early = find(names_ref, holder=here ^ jnp.where(inner, 3, 2))
    late = find(names_ref, holder=here ^ jnp.where(inner, 2, 3))
    rows = [
        own[0],
        near[0],
        early[0],
        late[0],
        own[1],
        early[1],
        find(second_ref, holder=here)[1],
        find(third_ref, holder=here)[1],
        find(first_ref, holder=here ^ 3)[1],
        [inner.astype(jnp.int32)] * capacity,
        *[[live_ref[0, block] for block in phase[0]] for phase in (own, near, early, late)],
    ]
    for number, row in enumerate(rows):
        for k in range(capacity):
            plan_ref[number * capacity + k] = row[k]
    for copy in copies:
        copy.wait()


OWN, EARLY, TO_INNER, TO_OUTER, FORWARD, INNER, LIVE, PLAN_ROWS = 4, 5, 6, 7, 8, 9, 10, 14


def make_plan(names, others, table, live, down, up, capacity):
    rank, depth = down.shape[1:]
    width = up.shape[2]
    return pl.pallas_call(
        functools.partial(plan_kernel, capacity),
        in_specs=[ANY] * 8,
        out_specs=[ANY, SMEM],
        out_shape=[
            jax.ShapeDtypeStruct((capacity, rank, depth + width), down.dtype),
            jax.ShapeDtypeStruct((PLAN_ROWS * capacity,), jnp.int32),
        ],
        scratch_shapes=[pltpu.SMEM(names.shape, jnp.int32)] * 4
        + [pltpu.SMEM(table.shape, jnp.int32), pltpu.SMEM(live.shape, jnp.int32)]
        + [pltpu.SemaphoreType.DMA((6,)), pltpu.SemaphoreType.DMA((capacity, 2))],
        compiler_params=PARAMS,
        cost_estimate=SHORT,
    )(in_hbm(names), *others, *[in_hbm(a) for a in (table, live, down, up)])


def pack_kernel(starts, capacity, plan_ref, down_ref, up_ref, *rest):
    count = len(starts)
    sems = rest[-1]
    outs = rest[-1 - count : -1]
    copies = []
    for number, start in enumerate(starts):
        for k in range(capacity):
            slot = plan_ref[start + k]
            copies += run_copies(
                panel_copies(k, slot, down_ref, up_ref, outs[number], sems.at[number])
            )
    for copy in copies:
        copy.wait()


def pack_panels(plan, starts, capacity, down, up, after=(), cost=None):
    rank, depth = down.shape[1:]
    width = up.shape[2]
    out = jax.ShapeDtypeStruct((capacity, rank, depth + width), down.dtype)
    return pl.pallas_call(
        functools.partial(pack_kernel, starts, capacity),
        in_specs=[SMEM] + [ANY] * (2 + len(after)),
        out_specs=[ANY] * len(starts),
        out_shape=[out] * len(starts),
        scratch_shapes=[pltpu.SemaphoreType.DMA((len(starts), capacity, 2))],
        compiler_params=PARAMS,
        cost_estimate=cost or NO_COST,
    )(plan, down, up, *after)


def step_of(i, start, count):
    return jnp.clip(i - start, 0, count - 1)


def source_specs(phases, shape, columns):
    specs, operands, start = [], [], 0
    for (_, count, sources), places in zip(phases, columns):
        for (panels, row), column in zip(sources, places):

            def index(i, plan, *_, start=start, count=count, row=row, column=column):
                k = step_of(i, start, count)
                return (k if row is None else plan[row + k], 0, column)

            specs.append(pl.BlockSpec(shape, index))
            operands.append(panels)
        start += count
    return specs, operands


def block_index(phases):
    def index(i, plan):
        found, start = jnp.int32(0), 0
        for row, count, _ in phases:
            inside = (i >= start) & (i < start + count)
            found = jnp.where(inside, plan[row + step_of(i, start, count)], found)
            start += count
        return found

    return index


def for_phase(phases, choose, plan_ref, refs, act):
    start, at = 0, 0
    step = pl.program_id(0)
    for _, count, sources in phases:
        mine = refs[at : at + len(sources)]

        @pl.when((step >= start) & (step < start + count))
        def _(mine=mine):
            if len(mine) == 1:
                act(mine[0])
            else:
                first = plan_ref[choose] != 0
                pl.when(first)(lambda: act(mine[0]))
                pl.when(jnp.logical_not(first))(lambda: act(mine[1]))

        start += count
        at += len(sources)


def shrink_kernel(phases, choose, plan_ref, token_ref, *refs):
    out_ref = refs[-1]

    def act(panel_ref):
        out_ref[0] = lax.dot_general(
            panel_ref[0],
            token_ref[0],
            (((1,), (1,)), ((), ())),
            preferred_element_type=jnp.float32,
        ).astype(out_ref.dtype)

    for_phase(phases, choose, plan_ref, refs, act)


def shrink(plan, row_blocks, phases, choose, after=()):
    rows, depth = row_blocks.shape[1:]
    rank = phases[0][2][0][0].shape[1]
    total = sum(count for _, count, _ in phases)
    columns = [[0] * len(sources) for _, _, sources in phases]
    specs, operands = source_specs(phases, (1, rank, depth), columns)
    block = block_index(phases)
    shapes = [(row, count, [None] * len(sources)) for row, count, sources in phases]
    return pl.pallas_call(
        functools.partial(shrink_kernel, shapes, choose),
        grid_spec=pltpu.PrefetchScalarGridSpec(
            num_scalar_prefetch=1,
            grid=(total,),
            in_specs=[pl.BlockSpec((1, rows, depth), lambda i, plan: (block(i, plan), 0, 0))]
            + specs
            + [ANY] * len(after),
            out_specs=pl.BlockSpec((1, rank, rows), lambda i, plan: (i, 0, 0)),
        ),
        out_shape=jax.ShapeDtypeStruct((total, rank, rows), jnp.bfloat16),
        compiler_params=PARAMS,
        cost_estimate=NO_COST,
    )(plan, row_blocks, *operands, *after)


def exchange(part):
    return [part] + [swap(part, "tensor", m) for m in range(1, lax.axis_size("tensor"))]


def combine_kernel(phases, choose, part_count, live_row, plan_ref, *refs):
    parts = refs[:part_count]
    mine_ref, far_ref = refs[part_count : part_count + 2]
    out_ref = refs[-1]
    total = parts[0][0].astype(jnp.float32)
    for part in parts[1:]:
        total = total + part[0].astype(jnp.float32)
    shrunk = total.astype(jnp.bfloat16)
    live = plan_ref[live_row + pl.program_id(0)]

    def act(up_ref):
        delta = lax.dot_general(
            shrunk, up_ref[0], (((0,), (0,)), ((), ())), preferred_element_type=jnp.float32
        )
        row = lax.broadcasted_iota(jnp.int32, delta.shape, 0)
        value = mine_ref[...] + far_ref[...] + ADAPTER_SCALE * delta
        out_ref[...] = jnp.where(row < live, value, 0.0).astype(out_ref.dtype)

    for_phase(phases, choose, plan_ref, refs[part_count + 2 :], act)


def combine(plan, live_row, parts, base, phases, columns, choose, out=None, after=()):
    rank, block_rows = parts[0].shape[1:]
    rows, width = base[0].shape
    total = sum(count for _, count, _ in phases)
    block = block_index(phases)
    specs = [pl.BlockSpec((1, rank, block_rows), lambda i, plan: (i, 0, 0))] * len(parts)
    specs += [pl.BlockSpec((block_rows, width), lambda i, plan: (block(i, plan), 0))] * 2
    more, operands = source_specs(phases, (1, rank, width), columns)
    specs += more + [ANY] * len(after)
    operands = [*parts, *base, *operands, *after]
    aliases = {}
    if out is not None:
        specs.append(ANY)
        operands.append(out)
        aliases = {len(operands): 0}
    shapes = [(row, count, [None] * len(sources)) for row, count, sources in phases]
    return pl.pallas_call(
        functools.partial(combine_kernel, shapes, choose, len(parts), live_row),
        grid_spec=pltpu.PrefetchScalarGridSpec(
            num_scalar_prefetch=1,
            grid=(total,),
            in_specs=specs,
            out_specs=pl.BlockSpec((block_rows, width), lambda i, plan: (block(i, plan), 0)),
        ),
        out_shape=pltpu.HBM((rows, width), jnp.bfloat16),
        input_output_aliases=aliases,
        compiler_params=PARAMS,
        cost_estimate=NO_COST,
    )(plan, *operands)


def on_line_of_four(tokens, weight, row_blocks, down, up, names, table, live, capacity):
    up_column = down.shape[2] // up.shape[2]

    def across(value, pairs):
        return lax.ppermute(value, "pool", pairs)

    others = [swap(names, "pool", m) for m in range(1, 4)]
    inner_down = across(down, [(1, 2), (2, 1)])
    inner_up = across(up, [(1, 2), (2, 1)])
    near_out, plan = make_plan(names, others, table, live, down, up, capacity)
    near = across(near_out, [(0, 1), (1, 0), (2, 3), (3, 2)])
    base = base_sum(tokens, weight, up.shape[2], [near_out])
    inner_out, outer_out = pack_panels(
        plan,
        [TO_INNER * capacity, TO_OUTER * capacity],
        capacity,
        in_hbm(down),
        in_hbm(up),
        [base[0]],
    )
    to_inner = across(inner_out, [(0, 2), (3, 1)])
    to_outer = across(outer_out, [(0, 3), (3, 0)])
    forward_out = pack_panels(
        plan,
        [FORWARD * capacity + k for k in range(capacity)],
        1,
        inner_down,
        inner_up,
        [outer_out, near],
        LONG,
    )
    forwarded = [across(panel, [(1, 0), (2, 3)]) for panel in forward_out]

    choose = INNER * capacity

    def phases_of(down_panels, up_panels, place):
        early = [
            (
                2 * capacity + k,
                1,
                [(place, EARLY * capacity + k), (forwarded[k], None)],
            )
            for k in range(capacity)
        ]
        return [
            (0, capacity, [(down_panels, OWN * capacity)]),
            (capacity, capacity, [(near, None)]),
        ], early

    first, early = phases_of(down, None, inner_down)
    first_up, early_up = phases_of(up, None, inner_up)
    last = [(3 * capacity, capacity, [(to_inner, None), (to_outer, None)])]

    first_parts = exchange(shrink(plan, row_blocks, first, choose, [outer_out]))
    columns = [[0], [up_column]]
    out = combine(plan, LIVE * capacity, first_parts, base, first_up, columns, choose)
    early_part = shrink(plan, row_blocks, early, choose)
    early_parts = exchange(early_part)
    last_parts = exchange(shrink(plan, row_blocks, last, choose, [out, early_part]))
    columns = [[0, up_column]] * capacity
    out = combine(
        plan, (LIVE + 2) * capacity, early_parts, base, early_up, columns, choose, out
    )
    columns = [[up_column] * 2]
    return combine(plan, (LIVE + 3) * capacity, last_parts, base, last, columns, choose, out)


def on_any_pool(tokens, weight, row_blocks, down, up, names, table, live, capacity):
    pool_size = lax.axis_size("pool")
    here = lax.axis_index("pool")
    holder_slots, _, depth = down.shape
    asked = table[lax.all_gather(names[0], "pool")]
    count = jnp.arange(capacity, dtype=jnp.int32)
    arrived = []
    for distance in range(pool_size):
        slots = asked[lax.rem(here + distance, pool_size)]
        hit = slots // holder_slots == here
        chosen = hit[None, :] & (jnp.cumsum(hit.astype(jnp.int32))[None, :] == 1 + count[:, None])
        plan = jnp.sum(jnp.where(chosen, (slots % holder_slots)[None, :], 0), axis=1)
        (panels,) = pack_panels(plan, [0], capacity, down, up)
        pairs = [(i, (i + distance) % pool_size) for i in range(pool_size)]
        arrived.append(lax.ppermute(panels, "pool", pairs) if distance else panels)
    arrived = jnp.concatenate(arrived)
    owners = asked[here] // holder_slots
    blocks = jnp.arange(owners.shape[0], dtype=jnp.int32)
    earlier = (owners[:, None] == owners[None, :]) & (blocks[:, None] > blocks[None, :])
    ranks = jnp.sum(earlier.astype(jnp.int32), axis=1)
    places = lax.rem(here - owners + pool_size, pool_size) * capacity + ranks
    plan = jnp.concatenate([blocks, places, live[0]])
    base = base_sum(tokens, weight, up.shape[2], [])
    phases = [(0, blocks.shape[0], [(arrived, blocks.shape[0])])]
    parts = exchange(shrink(plan, row_blocks, phases, 0))
    live_row = 2 * blocks.shape[0]
    return combine(plan, live_row, parts, base, phases, [[depth // up.shape[2]]], 0)


def on_device(
    tokens,
    value_weight,
    adapter_down_weight,
    adapter_up_weight,
    adapter_of_block,
    adapter_pool_slot,
    live_block_tokens,
):
    pool_size = lax.axis_size("pool")
    blocks = adapter_of_block.shape[1]
    capacity = -(-blocks // pool_size)
    row_blocks = tokens.reshape(blocks, tokens.shape[0] // blocks, tokens.shape[1])
    line = pool_size == 4 and blocks == capacity * pool_size
    route = on_line_of_four if line else on_any_pool
    return route(
        tokens,
        value_weight,
        row_blocks,
        jnp.transpose(adapter_down_weight, (0, 2, 1)),
        adapter_up_weight,
        adapter_of_block,
        adapter_pool_slot,
        live_block_tokens,
        capacity,
    )


def solution(mesh):
    return jax.shard_map(
        on_device,
        mesh=mesh,
        in_specs=(
            P(("groups", "pool"), "tensor"),
            P("tensor", None),
            P(("groups", "pool"), "tensor", None),
            P(("groups", "pool"), None, "tensor"),
            P(("groups", "pool"), None),
            P("groups"),
            P(("groups", "pool"), None),
        ),
        out_specs=P(("groups", "pool"), "tensor"),
        check_vma=False,
    )
```

```python
import functools

import jax
import jax.numpy as jnp
from jax import lax
from jax.experimental import pallas as pl
from jax.experimental.pallas import tpu as pltpu
from jax.sharding import PartitionSpec as P

ADAPTER_SCALE = 0.5
ROW_TILE = 256
PARAMS = pltpu.CompilerParams(vmem_limit_bytes=16 * 1024 * 1024)
NO_COST = pl.CostEstimate(flops=0, bytes_accessed=0, transcendentals=0)
SHORT = pl.CostEstimate(flops=4 * 10**9, bytes_accessed=0, transcendentals=0)
MIDDLE = pl.CostEstimate(flops=0 * 10**9, bytes_accessed=0, transcendentals=0)
LONG = pl.CostEstimate(flops=6 * 10**9, bytes_accessed=0, transcendentals=0)
ANY = pl.BlockSpec(memory_space=pl.ANY)
SMEM = pl.BlockSpec(memory_space=pltpu.SMEM)


def in_hbm(value):
    return pltpu.with_memory_space_constraint(value, pltpu.HBM)


def swap(value, axis, distance):
    pairs = [(i, i ^ distance) for i in range(lax.axis_size(axis))]
    return lax.ppermute(value, axis, pairs)


def piece_rows(rows):
    large = rows * 3 // 8
    return [large, large, rows - 2 * large]


def base_kernel(half, chunks_ref, tokens_ref, weight_ref, *refs):
    del chunks_ref
    *sent_refs, kept_ref = refs[-1 - len(piece_rows(tokens_ref.shape[0])) :]

    def write(out_ref, first, size):
        for start in range(0, size, ROW_TILE):
            stop = min(start + ROW_TILE, size)
            out_ref[0, start:stop, :] = jnp.dot(
                tokens_ref[first + start : first + stop, :],
                weight_ref[...],
                preferred_element_type=jnp.float32,
            )

    @pl.when(pl.program_id(0) < half)
    def _():
        first = 0
        for sent_ref in sent_refs:
            write(sent_ref, first, sent_ref.shape[1])
            first += sent_ref.shape[1]

    @pl.when(pl.program_id(0) >= half)
    def _():
        write(kept_ref, 0, kept_ref.shape[1])


def base_chunks(tokens, weight, order, width, after):
    rows, depth = tokens.shape
    half = len(order) // 2
    sizes = piece_rows(rows)
    chunks = lax.axis_index("tensor") ^ jnp.asarray(order, jnp.int32)
    *sent, kept = pl.pallas_call(
        functools.partial(base_kernel, half),
        grid_spec=pltpu.PrefetchScalarGridSpec(
            num_scalar_prefetch=1,
            grid=(len(order),),
            in_specs=[
                pl.BlockSpec(tokens.shape, lambda i, c: (0, 0), pipeline_mode=pl.Buffered(1)),
                pl.BlockSpec((depth, width), lambda i, c: (0, c[i])),
            ]
            + [ANY] * len(after),
            out_specs=[
                pl.BlockSpec((1, size, width), lambda i, c: (jnp.minimum(i, half - 1), 0, 0))
                for size in sizes
            ]
            + [pl.BlockSpec((1, rows, width), lambda i, c: (jnp.maximum(i - half, 0), 0, 0))],
        ),
        out_shape=[
            jax.ShapeDtypeStruct((half, size, width), jnp.float32) for size in [*sizes, rows]
        ],
        compiler_params=PARAMS,
        cost_estimate=NO_COST,
    )(chunks, in_hbm(tokens), in_hbm(weight), *after)
    return sent, kept


def add_kernel(kept_ref, *refs):
    *arrived_refs, out_ref, mine_ref = refs
    half = kept_ref.shape[0] // 2
    start = 0
    for arrived_ref in arrived_refs:
        rows = pl.ds(start, arrived_ref.shape[1])
        for i in range(half):
            mine_ref[i, rows, :] = kept_ref[i, rows, :] + arrived_ref[i]
            out_ref[i, rows, :] = kept_ref[half + i, rows, :] + arrived_ref[half + i]
        start += arrived_ref.shape[1]


def add_halves(kept, arrived):
    count, rows, width = kept.shape
    out = jax.ShapeDtypeStruct((count // 2, rows, width), jnp.float32)
    return pl.pallas_call(
        add_kernel,
        out_shape=[out, out],
        compiler_params=PARAMS,
        cost_estimate=NO_COST,
    )(kept, *arrived)


def base_sum(tokens, weight, width, after):
    size = lax.axis_size("tensor")
    kept_order = [k for k in range(size) if not k & 1]
    kept_order.sort(key=lambda k: [k >> bit & 1 for bit in range(1, size.bit_length())])
    sent, kept = base_chunks(tokens, weight, [k ^ 1 for k in kept_order] + kept_order, width, after)
    arrived = [swap(piece, "tensor", 1) for piece in sent]
    distance = 2
    while distance < size:
        sent, kept = add_halves(kept, arrived)
        arrived = [swap(sent, "tensor", distance)]
        distance *= 2
    return kept[0], arrived[0][0]


def pick(names_ref, table_ref, holder, holder_slots, count):
    blocks = [jnp.int32(0)] * count
    slots = [jnp.int32(0)] * count
    seen = jnp.int32(0)
    for j in range(names_ref.shape[1]):
        slot = table_ref[names_ref[0, j]]
        hit = lax.div(slot, jnp.int32(holder_slots)) == holder
        for k in range(count):
            chosen = hit & (seen == k)
            blocks[k] = jnp.where(chosen, jnp.int32(j), blocks[k])
            slots[k] = jnp.where(chosen, lax.rem(slot, jnp.int32(holder_slots)), slots[k])
        seen = seen + hit.astype(jnp.int32)
    return blocks, slots


def panel_copies(k, slot, down_ref, up_ref, out_ref, sems):
    depth = down_ref.shape[2]
    width = up_ref.shape[2]
    return [
        pltpu.make_async_copy(down_ref.at[slot], out_ref.at[k, :, pl.ds(0, depth)], sems.at[k, 0]),
        pltpu.make_async_copy(up_ref.at[slot], out_ref.at[k, :, pl.ds(depth, width)], sems.at[k, 1]),
    ]


def run_copies(copies):
    for copy in copies:
        copy.start()
    return copies


def plan_kernel(capacity, *refs):
    sources, down_ref, up_ref, out_refs, plan_ref = refs[:6], *refs[6:8], refs[8:11], refs[11]
    scalars, scalar_sems, sems = refs[12:18], *refs[18:]
    loads = [
        pltpu.make_async_copy(source, scalar, scalar_sems.at[i])
        for i, (source, scalar) in enumerate(zip(sources, scalars))
    ]
    for load in run_copies(loads):
        load.wait()
    names_ref, first_ref, second_ref, third_ref, table_ref, live_ref = scalars
    here = lax.axis_index("pool")
    holder_slots = down_ref.shape[0]
    find = functools.partial(
        pick, table_ref=table_ref, holder_slots=holder_slots, count=capacity
    )
    copies = []
    for i, asked_ref in enumerate((third_ref, second_ref, first_ref)):
        for k, slot in enumerate(find(asked_ref, holder=here)[1]):
            copies += run_copies(panel_copies(k, slot, down_ref, up_ref, out_refs[i], sems.at[i]))
    inner = (here == 1) | (here == 2)
    own = find(names_ref, holder=here)
    near = find(names_ref, holder=here ^ 1)
    across = find(names_ref, holder=here ^ 3)
    late = find(names_ref, holder=here ^ 2)
    rows = [
        own[0],
        near[0],
        across[0],
        late[0],
        own[1],
        across[1],
        find(first_ref, holder=here ^ 3)[1],
        [inner.astype(jnp.int32)] * capacity,
        *[[live_ref[0, block] for block in phase[0]] for phase in (own, near, across, late)],
    ]
    for number, row in enumerate(rows):
        for k in range(capacity):
            plan_ref[number * capacity + k] = row[k]
    for copy in copies:
        copy.wait()


OWN, ACROSS, FORWARD, INNER, LIVE, PLAN_ROWS = 4, 5, 6, 7, 8, 12


def make_plan(names, others, table, live, down, up, capacity):
    rank, depth = down.shape[1:]
    width = up.shape[2]
    return pl.pallas_call(
        functools.partial(plan_kernel, capacity),
        in_specs=[ANY] * 8,
        out_specs=[ANY] * 3 + [SMEM],
        out_shape=[jax.ShapeDtypeStruct((capacity, rank, depth + width), down.dtype)] * 3
        + [
            jax.ShapeDtypeStruct((PLAN_ROWS * capacity,), jnp.int32),
        ],
        scratch_shapes=[pltpu.SMEM(names.shape, jnp.int32)] * 4
        + [pltpu.SMEM(table.shape, jnp.int32), pltpu.SMEM(live.shape, jnp.int32)]
        + [pltpu.SemaphoreType.DMA((6,)), pltpu.SemaphoreType.DMA((3, capacity, 2))],
        compiler_params=PARAMS,
        cost_estimate=SHORT,
    )(in_hbm(names), *others, *[in_hbm(a) for a in (table, live, down, up)])


def pack_kernel(starts, capacity, plan_ref, down_ref, up_ref, *rest):
    count = len(starts)
    sems = rest[-1]
    outs = rest[-1 - count : -1]
    copies = []
    for number, start in enumerate(starts):
        for k in range(capacity):
            slot = plan_ref[start + k]
            copies += run_copies(
                panel_copies(k, slot, down_ref, up_ref, outs[number], sems.at[number])
            )
    for copy in copies:
        copy.wait()


def pack_panels(plan, starts, capacity, down, up, after=(), cost=None):
    rank, depth = down.shape[1:]
    width = up.shape[2]
    out = jax.ShapeDtypeStruct((capacity, rank, depth + width), down.dtype)
    return pl.pallas_call(
        functools.partial(pack_kernel, starts, capacity),
        in_specs=[SMEM] + [ANY] * (2 + len(after)),
        out_specs=[ANY] * len(starts),
        out_shape=[out] * len(starts),
        scratch_shapes=[pltpu.SemaphoreType.DMA((len(starts), capacity, 2))],
        compiler_params=PARAMS,
        cost_estimate=cost or NO_COST,
    )(plan, down, up, *after)


def step_of(i, start, count):
    return jnp.clip(i - start, 0, count - 1)


def source_specs(phases, shape, columns):
    specs, operands, start = [], [], 0
    for (_, count, sources), places in zip(phases, columns):
        for (panels, row), column in zip(sources, places):

            def index(i, plan, *_, start=start, count=count, row=row, column=column):
                k = step_of(i, start, count)
                return (k if row is None else plan[row + k], 0, column)

            specs.append(pl.BlockSpec(shape, index))
            operands.append(panels)
        start += count
    return specs, operands


def block_index(phases):
    def index(i, plan):
        found, start = jnp.int32(0), 0
        for row, count, _ in phases:
            inside = (i >= start) & (i < start + count)
            found = jnp.where(inside, plan[row + step_of(i, start, count)], found)
            start += count
        return found

    return index


def for_phase(phases, choose, plan_ref, refs, act):
    start, at = 0, 0
    step = pl.program_id(0)
    for _, count, sources in phases:
        mine = refs[at : at + len(sources)]

        @pl.when((step >= start) & (step < start + count))
        def _(mine=mine):
            if len(mine) == 1:
                act(mine[0])
            else:
                first = plan_ref[choose] != 0
                pl.when(first)(lambda: act(mine[0]))
                pl.when(jnp.logical_not(first))(lambda: act(mine[1]))

        start += count
        at += len(sources)


def shrink_kernel(phases, choose, plan_ref, token_ref, *refs):
    out_ref = refs[-1]

    def act(panel_ref):
        out_ref[0] = lax.dot_general(
            panel_ref[0],
            token_ref[0],
            (((1,), (1,)), ((), ())),
            preferred_element_type=jnp.float32,
        ).astype(out_ref.dtype)

    for_phase(phases, choose, plan_ref, refs, act)


def shrink(plan, row_blocks, phases, choose, after=()):
    rows, depth = row_blocks.shape[1:]
    rank = phases[0][2][0][0].shape[1]
    total = sum(count for _, count, _ in phases)
    columns = [[0] * len(sources) for _, _, sources in phases]
    specs, operands = source_specs(phases, (1, rank, depth), columns)
    block = block_index(phases)
    shapes = [(row, count, [None] * len(sources)) for row, count, sources in phases]
    return pl.pallas_call(
        functools.partial(shrink_kernel, shapes, choose),
        grid_spec=pltpu.PrefetchScalarGridSpec(
            num_scalar_prefetch=1,
            grid=(total,),
            in_specs=[pl.BlockSpec((1, rows, depth), lambda i, plan: (block(i, plan), 0, 0))]
            + specs
            + [ANY] * len(after),
            out_specs=pl.BlockSpec((1, rank, rows), lambda i, plan: (i, 0, 0)),
        ),
        out_shape=jax.ShapeDtypeStruct((total, rank, rows), jnp.bfloat16),
        compiler_params=PARAMS,
        cost_estimate=NO_COST,
    )(plan, row_blocks, *operands, *after)


def exchange(part):
    return [part] + [swap(part, "tensor", m) for m in range(1, lax.axis_size("tensor"))]


def combine_kernel(phases, choose, part_count, live_row, plan_ref, *refs):
    parts = refs[:part_count]
    mine_ref, far_ref = refs[part_count : part_count + 2]
    out_ref = refs[-1]
    total = parts[0][0].astype(jnp.float32)
    for part in parts[1:]:
        total = total + part[0].astype(jnp.float32)
    shrunk = total.astype(jnp.bfloat16)
    live = plan_ref[live_row + pl.program_id(0)]

    def act(up_ref):
        delta = lax.dot_general(
            shrunk, up_ref[0], (((0,), (0,)), ((), ())), preferred_element_type=jnp.float32
        )
        row = lax.broadcasted_iota(jnp.int32, delta.shape, 0)
        value = mine_ref[...] + far_ref[...] + ADAPTER_SCALE * delta
        out_ref[...] = jnp.where(row < live, value, 0.0).astype(out_ref.dtype)

    for_phase(phases, choose, plan_ref, refs[part_count + 2 :], act)


def combine(
    plan, live_row, parts, base, phases, columns, choose, out=None, after=(), cost=None
):
    rank, block_rows = parts[0].shape[1:]
    rows, width = base[0].shape
    total = sum(count for _, count, _ in phases)
    block = block_index(phases)
    specs = [pl.BlockSpec((1, rank, block_rows), lambda i, plan: (i, 0, 0))] * len(parts)
    specs += [pl.BlockSpec((block_rows, width), lambda i, plan: (block(i, plan), 0))] * 2
    more, operands = source_specs(phases, (1, rank, width), columns)
    specs += more + [ANY] * len(after)
    operands = [*parts, *base, *operands, *after]
    aliases = {}
    if out is not None:
        specs.append(ANY)
        operands.append(out)
        aliases = {len(operands): 0}
    shapes = [(row, count, [None] * len(sources)) for row, count, sources in phases]
    return pl.pallas_call(
        functools.partial(combine_kernel, shapes, choose, len(parts), live_row),
        grid_spec=pltpu.PrefetchScalarGridSpec(
            num_scalar_prefetch=1,
            grid=(total,),
            in_specs=specs,
            out_specs=pl.BlockSpec((block_rows, width), lambda i, plan: (block(i, plan), 0)),
        ),
        out_shape=pltpu.HBM((rows, width), jnp.bfloat16),
        input_output_aliases=aliases,
        compiler_params=PARAMS,
        cost_estimate=cost or NO_COST,
    )(plan, *operands)


def on_line_of_four(tokens, weight, row_blocks, down, up, names, table, live, capacity):
    up_column = down.shape[2] // up.shape[2]

    def across(value, pairs):
        return lax.ppermute(value, "pool", pairs)

    others = [swap(names, "pool", m) for m in range(1, 4)]
    inner_down = across(down, [(1, 2), (2, 1)])
    inner_up = across(up, [(1, 2), (2, 1)])
    outer_out, inner_out, near_out, plan = make_plan(
        names, others, table, live, down, up, capacity
    )
    to_outer = across(outer_out, [(0, 3), (3, 0)])
    to_inner = across(inner_out, [(0, 2), (3, 1)])
    near = across(near_out, [(0, 1), (1, 0), (2, 3), (3, 2)])
    base = base_sum(tokens, weight, up.shape[2], [near_out])
    (forward_out,) = pack_panels(
        plan, [FORWARD * capacity], capacity, inner_down, inner_up, [base[0]], LONG
    )
    forwarded = across(forward_out, [(1, 0), (2, 3)])

    choose = INNER * capacity
    first = [
        (0, capacity, [(down, OWN * capacity)]),
        (capacity, capacity, [(near, None)]),
        (2 * capacity, capacity, [(inner_down, ACROSS * capacity), (to_outer, None)]),
    ]
    first_up = [
        (0, capacity, [(up, OWN * capacity)]),
        (capacity, capacity, [(near, None)]),
        (2 * capacity, capacity, [(inner_up, ACROSS * capacity), (to_outer, None)]),
    ]
    last = [(3 * capacity, capacity, [(to_inner, None), (forwarded, None)])]
    first_parts = exchange(shrink(plan, row_blocks, first, choose, [forward_out]))
    columns = [[0], [up_column], [0, up_column]]
    out = combine(plan, LIVE * capacity, first_parts, base, first_up, columns, choose, cost=MIDDLE)
    last_parts = exchange(shrink(plan, row_blocks, last, choose, [in_hbm(out)]))
    columns = [[up_column] * 2]
    return combine(plan, (LIVE + 3) * capacity, last_parts, base, last, columns, choose, out)


def on_any_pool(tokens, weight, row_blocks, down, up, names, table, live, capacity):
    pool_size = lax.axis_size("pool")
    here = lax.axis_index("pool")
    holder_slots, _, depth = down.shape
    asked = table[lax.all_gather(names[0], "pool")]
    count = jnp.arange(capacity, dtype=jnp.int32)
    arrived = []
    for distance in range(pool_size):
        slots = asked[lax.rem(here + distance, pool_size)]
        hit = slots // holder_slots == here
        chosen = hit[None, :] & (jnp.cumsum(hit.astype(jnp.int32))[None, :] == 1 + count[:, None])
        plan = jnp.sum(jnp.where(chosen, (slots % holder_slots)[None, :], 0), axis=1)
        (panels,) = pack_panels(plan, [0], capacity, down, up)
        pairs = [(i, (i + distance) % pool_size) for i in range(pool_size)]
        arrived.append(lax.ppermute(panels, "pool", pairs) if distance else panels)
    arrived = jnp.concatenate(arrived)
    owners = asked[here] // holder_slots
    blocks = jnp.arange(owners.shape[0], dtype=jnp.int32)
    earlier = (owners[:, None] == owners[None, :]) & (blocks[:, None] > blocks[None, :])
    ranks = jnp.sum(earlier.astype(jnp.int32), axis=1)
    places = lax.rem(here - owners + pool_size, pool_size) * capacity + ranks
    plan = jnp.concatenate([blocks, places, live[0]])
    base = base_sum(tokens, weight, up.shape[2], [])
    phases = [(0, blocks.shape[0], [(arrived, blocks.shape[0])])]
    parts = exchange(shrink(plan, row_blocks, phases, 0))
    live_row = 2 * blocks.shape[0]
    return combine(plan, live_row, parts, base, phases, [[depth // up.shape[2]]], 0)


def on_device(
    tokens,
    value_weight,
    adapter_down_weight,
    adapter_up_weight,
    adapter_of_block,
    adapter_pool_slot,
    live_block_tokens,
):
    pool_size = lax.axis_size("pool")
    blocks = adapter_of_block.shape[1]
    capacity = -(-blocks // pool_size)
    row_blocks = tokens.reshape(blocks, tokens.shape[0] // blocks, tokens.shape[1])
    line = pool_size == 4 and blocks == capacity * pool_size
    route = on_line_of_four if line else on_any_pool
    return route(
        tokens,
        value_weight,
        row_blocks,
        jnp.transpose(adapter_down_weight, (0, 2, 1)),
        adapter_up_weight,
        adapter_of_block,
        adapter_pool_slot,
        live_block_tokens,
        capacity,
    )


def solution(mesh):
    return jax.shard_map(
        on_device,
        mesh=mesh,
        in_specs=(
            P(("groups", "pool"), "tensor"),
            P("tensor", None),
            P(("groups", "pool"), "tensor", None),
            P(("groups", "pool"), None, "tensor"),
            P(("groups", "pool"), None),
            P("groups"),
            P(("groups", "pool"), None),
        ),
        out_specs=P(("groups", "pool"), "tensor"),
        check_vma=False,
    )
```

```python
import functools

import jax
import jax.numpy as jnp
from jax import lax
from jax.experimental import pallas as pl
from jax.experimental.pallas import tpu as pltpu
from jax.sharding import PartitionSpec as P

ADAPTER_SCALE = 0.5
ROW_TILE = 256
PARAMS = pltpu.CompilerParams(vmem_limit_bytes=16 * 1024 * 1024)
NO_COST = pl.CostEstimate(flops=0, bytes_accessed=0, transcendentals=0)
SHORT = pl.CostEstimate(flops=10 * 10**9, bytes_accessed=0, transcendentals=0)
MIDDLE = pl.CostEstimate(flops=0 * 10**9, bytes_accessed=0, transcendentals=0)
LONG = pl.CostEstimate(flops=6 * 10**9, bytes_accessed=0, transcendentals=0)
ANY = pl.BlockSpec(memory_space=pl.ANY)
SMEM = pl.BlockSpec(memory_space=pltpu.SMEM)


def in_hbm(value):
    return pltpu.with_memory_space_constraint(value, pltpu.HBM)


def swap(value, axis, distance):
    pairs = [(i, i ^ distance) for i in range(lax.axis_size(axis))]
    return lax.ppermute(value, axis, pairs)


def piece_rows(rows):
    large = rows * 3 // 8
    return [large, large, rows - 2 * large]


def base_kernel(half, chunks_ref, tokens_ref, weight_ref, *refs):
    del chunks_ref
    *sent_refs, kept_ref = refs

    def write(out_ref, first, size):
        for start in range(0, size, ROW_TILE):
            stop = min(start + ROW_TILE, size)
            out_ref[0, start:stop, :] = jnp.dot(
                tokens_ref[first + start : first + stop, :],
                weight_ref[...],
                preferred_element_type=jnp.float32,
            )

    @pl.when(pl.program_id(0) < half)
    def _():
        first = 0
        for sent_ref in sent_refs:
            write(sent_ref, first, sent_ref.shape[1])
            first += sent_ref.shape[1]

    @pl.when(pl.program_id(0) >= half)
    def _():
        write(kept_ref, 0, kept_ref.shape[1])


def base_chunks(tokens, weight, order, width):
    rows, depth = tokens.shape
    half = len(order) // 2
    sizes = piece_rows(rows)
    chunks = lax.axis_index("tensor") ^ jnp.asarray(order, jnp.int32)
    *sent, kept = pl.pallas_call(
        functools.partial(base_kernel, half),
        grid_spec=pltpu.PrefetchScalarGridSpec(
            num_scalar_prefetch=1,
            grid=(len(order),),
            in_specs=[
                pl.BlockSpec(tokens.shape, lambda i, c: (0, 0), pipeline_mode=pl.Buffered(1)),
                pl.BlockSpec((depth, width), lambda i, c: (0, c[i])),
            ],
            out_specs=[
                pl.BlockSpec((1, size, width), lambda i, c: (jnp.minimum(i, half - 1), 0, 0))
                for size in sizes
            ]
            + [pl.BlockSpec((1, rows, width), lambda i, c: (jnp.maximum(i - half, 0), 0, 0))],
        ),
        out_shape=[
            jax.ShapeDtypeStruct((half, size, width), jnp.float32) for size in [*sizes, rows]
        ],
        compiler_params=PARAMS,
        cost_estimate=NO_COST,
    )(chunks, in_hbm(tokens), in_hbm(weight))
    return sent, kept


def add_kernel(kept_ref, *refs):
    *arrived_refs, out_ref, mine_ref = refs
    half = kept_ref.shape[0] // 2
    start = 0
    for arrived_ref in arrived_refs:
        rows = pl.ds(start, arrived_ref.shape[1])
        for i in range(half):
            mine_ref[i, rows, :] = kept_ref[i, rows, :] + arrived_ref[i]
            out_ref[i, rows, :] = kept_ref[half + i, rows, :] + arrived_ref[half + i]
        start += arrived_ref.shape[1]


def add_halves(kept, arrived):
    count, rows, width = kept.shape
    out = jax.ShapeDtypeStruct((count // 2, rows, width), jnp.float32)
    return pl.pallas_call(
        add_kernel,
        out_shape=[out, out],
        compiler_params=PARAMS,
        cost_estimate=NO_COST,
    )(kept, *arrived)


def base_parts(tokens, weight, width):
    size = lax.axis_size("tensor")
    kept_order = [k for k in range(size) if not k & 1]
    kept_order.sort(key=lambda k: [k >> bit & 1 for bit in range(1, size.bit_length())])
    return base_chunks(tokens, weight, [k ^ 1 for k in kept_order] + kept_order, width)


def base_sum(sent, kept):
    arrived = [swap(piece, "tensor", 1) for piece in sent]
    distance = 2
    while distance < lax.axis_size("tensor"):
        sent, kept = add_halves(kept, arrived)
        arrived = [swap(sent, "tensor", distance)]
        distance *= 2
    return kept[0], arrived[0][0]


def pick(names_ref, table_ref, holder, holder_slots, count):
    blocks = [jnp.int32(0)] * count
    slots = [jnp.int32(0)] * count
    seen = jnp.int32(0)
    for j in range(names_ref.shape[1]):
        slot = table_ref[names_ref[0, j]]
        hit = lax.div(slot, jnp.int32(holder_slots)) == holder
        for k in range(count):
            chosen = hit & (seen == k)
            blocks[k] = jnp.where(chosen, jnp.int32(j), blocks[k])
            slots[k] = jnp.where(chosen, lax.rem(slot, jnp.int32(holder_slots)), slots[k])
        seen = seen + hit.astype(jnp.int32)
    return blocks, slots


def panel_copies(k, slot, down_ref, up_ref, out_ref, sems):
    depth = down_ref.shape[2]
    width = up_ref.shape[2]
    return [
        pltpu.make_async_copy(down_ref.at[slot], out_ref.at[k, :, pl.ds(0, depth)], sems.at[k, 0]),
        pltpu.make_async_copy(up_ref.at[slot], out_ref.at[k, :, pl.ds(depth, width)], sems.at[k, 1]),
    ]


def run_copies(copies):
    for copy in copies:
        copy.start()
    return copies


def plan_kernel(capacity, holder_slots, *refs):
    sources, plan_ref, scalars, sems = refs[:6], refs[-8], refs[-7:-1], refs[-1]
    loads = [
        pltpu.make_async_copy(source, scalar, sems.at[i])
        for i, (source, scalar) in enumerate(zip(sources, scalars))
    ]
    for load in run_copies(loads):
        load.wait()
    names_ref, first_ref, second_ref, third_ref, table_ref, live_ref = scalars
    here = lax.axis_index("pool")
    find = functools.partial(
        pick, table_ref=table_ref, holder_slots=holder_slots, count=capacity
    )
    inner = (here == 1) | (here == 2)
    own = find(names_ref, holder=here)
    near = find(names_ref, holder=here ^ 1)
    across = find(names_ref, holder=here ^ 3)
    late = find(names_ref, holder=here ^ 2)
    rows = [
        own[0],
        near[0],
        across[0],
        late[0],
        own[1],
        across[1],
        find(first_ref, holder=here)[1],
        find(second_ref, holder=here)[1],
        find(third_ref, holder=here)[1],
        find(first_ref, holder=here ^ 3)[1],
        [inner.astype(jnp.int32)] * capacity,
        *[[live_ref[0, block] for block in phase[0]] for phase in (own, near, across, late)],
    ]
    for number, row in enumerate(rows):
        for k in range(capacity):
            plan_ref[number * capacity + k] = row[k]


OWN, ACROSS, NEAR, TO_INNER, TO_OUTER, FORWARD, INNER, LIVE, PLAN_ROWS = 4, 5, 6, 7, 8, 9, 10, 11, 15


def make_plan(names, others, table, live, holder_slots, capacity, after):
    return pl.pallas_call(
        functools.partial(plan_kernel, capacity, holder_slots),
        in_specs=[ANY] * (6 + len(after)),
        out_specs=SMEM,
        out_shape=jax.ShapeDtypeStruct((PLAN_ROWS * capacity,), jnp.int32),
        scratch_shapes=[pltpu.SMEM(names.shape, jnp.int32)] * 4
        + [pltpu.SMEM(table.shape, jnp.int32), pltpu.SMEM(live.shape, jnp.int32)]
        + [pltpu.SemaphoreType.DMA((6,))],
        compiler_params=PARAMS,
        cost_estimate=SHORT,
    )(in_hbm(names), *others, in_hbm(table), in_hbm(live), *after)


def pack_kernel(starts, capacity, plan_ref, down_ref, up_ref, *rest):
    count = len(starts)
    sems = rest[-1]
    outs = rest[-1 - count : -1]
    copies = []
    for number, start in enumerate(starts):
        for k in range(capacity):
            slot = plan_ref[start + k]
            copies += run_copies(
                panel_copies(k, slot, down_ref, up_ref, outs[number], sems.at[number])
            )
    for copy in copies:
        copy.wait()


def pack_panels(plan, starts, capacity, down, up, after=(), cost=None):
    rank, depth = down.shape[1:]
    width = up.shape[2]
    out = jax.ShapeDtypeStruct((capacity, rank, depth + width), down.dtype)
    return pl.pallas_call(
        functools.partial(pack_kernel, starts, capacity),
        in_specs=[SMEM] + [ANY] * (2 + len(after)),
        out_specs=[ANY] * len(starts),
        out_shape=[out] * len(starts),
        scratch_shapes=[pltpu.SemaphoreType.DMA((len(starts), capacity, 2))],
        compiler_params=PARAMS,
        cost_estimate=cost or NO_COST,
    )(plan, down, up, *after)


def step_of(i, start, count):
    return jnp.clip(i - start, 0, count - 1)


def source_specs(phases, shape, columns):
    specs, operands, start = [], [], 0
    for (_, count, sources), places in zip(phases, columns):
        for (panels, row), column in zip(sources, places):

            def index(i, plan, *_, start=start, count=count, row=row, column=column):
                k = step_of(i, start, count)
                return (k if row is None else plan[row + k], 0, column)

            specs.append(pl.BlockSpec(shape, index))
            operands.append(panels)
        start += count
    return specs, operands


def block_index(phases):
    def index(i, plan):
        found, start = jnp.int32(0), 0
        for row, count, _ in phases:
            inside = (i >= start) & (i < start + count)
            found = jnp.where(inside, plan[row + step_of(i, start, count)], found)
            start += count
        return found

    return index


def for_phase(phases, choose, plan_ref, refs, act):
    start, at = 0, 0
    step = pl.program_id(0)
    for _, count, sources in phases:
        mine = refs[at : at + len(sources)]

        @pl.when((step >= start) & (step < start + count))
        def _(mine=mine):
            if len(mine) == 1:
                act(mine[0])
            else:
                first = plan_ref[choose] != 0
                pl.when(first)(lambda: act(mine[0]))
                pl.when(jnp.logical_not(first))(lambda: act(mine[1]))

        start += count
        at += len(sources)


def shrink_kernel(phases, choose, plan_ref, token_ref, *refs):
    out_ref = refs[-1]

    def act(panel_ref):
        out_ref[0] = lax.dot_general(
            panel_ref[0],
            token_ref[0],
            (((1,), (1,)), ((), ())),
            preferred_element_type=jnp.float32,
        ).astype(out_ref.dtype)

    for_phase(phases, choose, plan_ref, refs, act)


def shrink(plan, row_blocks, phases, choose, after=()):
    rows, depth = row_blocks.shape[1:]
    rank = phases[0][2][0][0].shape[1]
    total = sum(count for _, count, _ in phases)
    columns = [[0] * len(sources) for _, _, sources in phases]
    specs, operands = source_specs(phases, (1, rank, depth), columns)
    block = block_index(phases)
    shapes = [(row, count, [None] * len(sources)) for row, count, sources in phases]
    return pl.pallas_call(
        functools.partial(shrink_kernel, shapes, choose),
        grid_spec=pltpu.PrefetchScalarGridSpec(
            num_scalar_prefetch=1,
            grid=(total,),
            in_specs=[pl.BlockSpec((1, rows, depth), lambda i, plan: (block(i, plan), 0, 0))]
            + specs
            + [ANY] * len(after),
            out_specs=pl.BlockSpec((1, rank, rows), lambda i, plan: (i, 0, 0)),
        ),
        out_shape=jax.ShapeDtypeStruct((total, rank, rows), jnp.bfloat16),
        compiler_params=PARAMS,
        cost_estimate=NO_COST,
    )(plan, row_blocks, *operands, *after)


def exchange(part):
    return [part] + [swap(part, "tensor", m) for m in range(1, lax.axis_size("tensor"))]


def combine_kernel(phases, choose, part_count, live_row, plan_ref, *refs):
    parts = refs[:part_count]
    mine_ref, far_ref = refs[part_count : part_count + 2]
    out_ref = refs[-1]
    total = parts[0][0].astype(jnp.float32)
    for part in parts[1:]:
        total = total + part[0].astype(jnp.float32)
    shrunk = total.astype(jnp.bfloat16)
    live = plan_ref[live_row + pl.program_id(0)]

    def act(up_ref):
        delta = lax.dot_general(
            shrunk, up_ref[0], (((0,), (0,)), ((), ())), preferred_element_type=jnp.float32
        )
        row = lax.broadcasted_iota(jnp.int32, delta.shape, 0)
        value = mine_ref[...] + far_ref[...] + ADAPTER_SCALE * delta
        out_ref[...] = jnp.where(row < live, value, 0.0).astype(out_ref.dtype)

    for_phase(phases, choose, plan_ref, refs[part_count + 2 :], act)


def combine(
    plan, live_row, parts, base, phases, columns, choose, out=None, after=(), cost=None
):
    rank, block_rows = parts[0].shape[1:]
    rows, width = base[0].shape
    total = sum(count for _, count, _ in phases)
    block = block_index(phases)
    specs = [pl.BlockSpec((1, rank, block_rows), lambda i, plan: (i, 0, 0))] * len(parts)
    specs += [pl.BlockSpec((block_rows, width), lambda i, plan: (block(i, plan), 0))] * 2
    more, operands = source_specs(phases, (1, rank, width), columns)
    specs += more + [ANY] * len(after)
    operands = [*parts, *base, *operands, *after]
    aliases = {}
    if out is not None:
        specs.append(ANY)
        operands.append(out)
        aliases = {len(operands): 0}
    shapes = [(row, count, [None] * len(sources)) for row, count, sources in phases]
    return pl.pallas_call(
        functools.partial(combine_kernel, shapes, choose, len(parts), live_row),
        grid_spec=pltpu.PrefetchScalarGridSpec(
            num_scalar_prefetch=1,
            grid=(total,),
            in_specs=specs,
            out_specs=pl.BlockSpec((block_rows, width), lambda i, plan: (block(i, plan), 0)),
        ),
        out_shape=pltpu.HBM((rows, width), jnp.bfloat16),
        input_output_aliases=aliases,
        compiler_params=PARAMS,
        cost_estimate=cost or NO_COST,
    )(plan, *operands)


def on_line_of_four(tokens, weight, row_blocks, down, up, names, table, live, capacity):
    up_column = down.shape[2] // up.shape[2]

    def across(value, pairs):
        return lax.ppermute(value, "pool", pairs)

    others = [swap(names, "pool", m) for m in range(1, 4)]
    inner_down = across(down, [(1, 2), (2, 1)])
    inner_up = across(up, [(1, 2), (2, 1)])
    sent, kept = base_parts(tokens, weight, up.shape[2])
    plan = make_plan(names, others, table, live, down.shape[0], capacity, [inner_up])
    near_out, outer_out, inner_out = pack_panels(
        plan,
        [NEAR * capacity, TO_OUTER * capacity, TO_INNER * capacity],
        capacity,
        in_hbm(down),
        in_hbm(up),
        sent[-1:],
    )
    near = across(near_out, [(0, 1), (1, 0), (2, 3), (3, 2)])
    to_outer = across(outer_out, [(0, 3), (3, 0)])
    to_inner = across(inner_out, [(0, 2), (3, 1)])
    base = base_sum(sent, kept)
    (forward_out,) = pack_panels(
        plan, [FORWARD * capacity], capacity, inner_down, inner_up, [base[0]], LONG
    )
    forwarded = across(forward_out, [(1, 0), (2, 3)])

    choose = INNER * capacity
    first = [(0, capacity, [(down, OWN * capacity)]), (capacity, capacity, [(near, None)])]
    first_up = [(0, capacity, [(up, OWN * capacity)]), first[1]]
    middle = [(2 * capacity, capacity, [(inner_down, ACROSS * capacity), (to_outer, None)])]
    middle_up = [(2 * capacity, capacity, [(inner_up, ACROSS * capacity), (to_outer, None)])]
    last = [(3 * capacity, capacity, [(to_inner, None), (forwarded, None)])]

    def write(number, parts, phases, columns, out, cost=None):
        live_row = (LIVE + number) * capacity
        return combine(plan, live_row, parts, base, phases, columns, choose, out, cost=cost)

    first_parts = exchange(shrink(plan, row_blocks, first, choose, [forward_out]))
    out = write(0, first_parts, first_up, [[0], [up_column]], None, MIDDLE)
    middle_part = shrink(plan, row_blocks, middle, choose, [in_hbm(out)])
    middle_parts = exchange(middle_part)
    last_parts = exchange(shrink(plan, row_blocks, last, choose, [middle_part]))
    out = write(2, middle_parts, middle_up, [[0, up_column]], out)
    return write(3, last_parts, last, [[up_column] * 2], out)


def on_any_pool(tokens, weight, row_blocks, down, up, names, table, live, capacity):
    pool_size = lax.axis_size("pool")
    here = lax.axis_index("pool")
    holder_slots, _, depth = down.shape
    asked = table[lax.all_gather(names[0], "pool")]
    count = jnp.arange(capacity, dtype=jnp.int32)
    arrived = []
    for distance in range(pool_size):
        slots = asked[lax.rem(here + distance, pool_size)]
        hit = slots // holder_slots == here
        chosen = hit[None, :] & (jnp.cumsum(hit.astype(jnp.int32))[None, :] == 1 + count[:, None])
        plan = jnp.sum(jnp.where(chosen, (slots % holder_slots)[None, :], 0), axis=1)
        (panels,) = pack_panels(plan, [0], capacity, down, up)
        pairs = [(i, (i + distance) % pool_size) for i in range(pool_size)]
        arrived.append(lax.ppermute(panels, "pool", pairs) if distance else panels)
    arrived = jnp.concatenate(arrived)
    owners = asked[here] // holder_slots
    blocks = jnp.arange(owners.shape[0], dtype=jnp.int32)
    earlier = (owners[:, None] == owners[None, :]) & (blocks[:, None] > blocks[None, :])
    ranks = jnp.sum(earlier.astype(jnp.int32), axis=1)
    places = lax.rem(here - owners + pool_size, pool_size) * capacity + ranks
    plan = jnp.concatenate([blocks, places, live[0]])
    base = base_sum(*base_parts(tokens, weight, up.shape[2]))
    phases = [(0, blocks.shape[0], [(arrived, blocks.shape[0])])]
    parts = exchange(shrink(plan, row_blocks, phases, 0))
    live_row = 2 * blocks.shape[0]
    return combine(plan, live_row, parts, base, phases, [[depth // up.shape[2]]], 0)


def on_device(
    tokens,
    value_weight,
    adapter_down_weight,
    adapter_up_weight,
    adapter_of_block,
    adapter_pool_slot,
    live_block_tokens,
):
    pool_size = lax.axis_size("pool")
    blocks = adapter_of_block.shape[1]
    capacity = -(-blocks // pool_size)
    row_blocks = tokens.reshape(blocks, tokens.shape[0] // blocks, tokens.shape[1])
    line = pool_size == 4 and blocks == capacity * pool_size
    route = on_line_of_four if line else on_any_pool
    return route(
        tokens,
        value_weight,
        row_blocks,
        jnp.transpose(adapter_down_weight, (0, 2, 1)),
        adapter_up_weight,
        adapter_of_block,
        adapter_pool_slot,
        live_block_tokens,
        capacity,
    )


def solution(mesh):
    return jax.shard_map(
        on_device,
        mesh=mesh,
        in_specs=(
            P(("groups", "pool"), "tensor"),
            P("tensor", None),
            P(("groups", "pool"), "tensor", None),
            P(("groups", "pool"), None, "tensor"),
            P(("groups", "pool"), None),
            P("groups"),
            P(("groups", "pool"), None),
        ),
        out_specs=P(("groups", "pool"), "tensor"),
        check_vma=False,
    )
```

```python
import functools

import jax
import jax.numpy as jnp
from jax import lax
from jax.experimental import pallas as pl
from jax.experimental.pallas import tpu as pltpu
from jax.sharding import PartitionSpec as P

ADAPTER_SCALE = 0.5
ROW_TILE = 256
PARAMS = pltpu.CompilerParams(vmem_limit_bytes=16 * 1024 * 1024)
NO_COST = pl.CostEstimate(flops=0, bytes_accessed=0, transcendentals=0)
SHORT = pl.CostEstimate(flops=10 * 10**9, bytes_accessed=0, transcendentals=0)
MIDDLE = pl.CostEstimate(flops=0 * 10**9, bytes_accessed=0, transcendentals=0)
LONG = pl.CostEstimate(flops=6 * 10**9, bytes_accessed=0, transcendentals=0)
ANY = pl.BlockSpec(memory_space=pl.ANY)
SMEM = pl.BlockSpec(memory_space=pltpu.SMEM)


def in_hbm(value):
    return pltpu.with_memory_space_constraint(value, pltpu.HBM)


def swap(value, axis, distance):
    pairs = [(i, i ^ distance) for i in range(lax.axis_size(axis))]
    return lax.ppermute(value, axis, pairs)


def run_copies(copies):
    for copy in copies:
        copy.start()
    return copies


def piece_rows(rows):
    large = rows * 3 // 8
    return [large, large, rows - 2 * large]


def base_kernel(half, chunks_ref, tokens_ref, weight_ref, *refs):
    del chunks_ref
    *sent_refs, kept_ref, held_ref, sems = refs
    step = pl.program_id(0)
    tiles = sems.shape[0]
    tile = held_ref.shape[0] // tiles
    copies = []
    for i in range(tiles):
        rows = pl.ds(i * tile, tile)
        copies.append(pltpu.make_async_copy(tokens_ref.at[rows], held_ref.at[rows], sems.at[i]))

    def write(out_refs, arriving=()):
        first = 0
        for out_ref in out_refs:
            for start in range(0, out_ref.shape[1], ROW_TILE):
                stop = min(start + ROW_TILE, out_ref.shape[1])
                while arriving and (tiles - len(arriving)) * tile < first + stop:
                    arriving.pop(0).wait()
                out_ref[0, start:stop, :] = jnp.dot(
                    held_ref[first + start : first + stop, :],
                    weight_ref[...],
                    preferred_element_type=jnp.float32,
                )
            first += out_ref.shape[1]

    @pl.when(step == 0)
    def _():
        write(sent_refs, run_copies(copies))

    @pl.when((step > 0) & (step < half))
    def _():
        write(sent_refs)

    @pl.when(step >= half)
    def _():
        write([kept_ref])


def base_chunks(tokens, weight, order, width):
    rows, depth = tokens.shape
    half = len(order) // 2
    sizes = piece_rows(rows)
    chunks = lax.axis_index("tensor") ^ jnp.asarray(order, jnp.int32)
    *sent, kept = pl.pallas_call(
        functools.partial(base_kernel, half),
        grid_spec=pltpu.PrefetchScalarGridSpec(
            num_scalar_prefetch=1,
            grid=(len(order),),
            in_specs=[
                ANY,
                pl.BlockSpec((depth, width), lambda i, c: (0, c[i])),
            ],
            out_specs=[
                pl.BlockSpec((1, size, width), lambda i, c: (jnp.minimum(i, half - 1), 0, 0))
                for size in sizes
            ]
            + [pl.BlockSpec((1, rows, width), lambda i, c: (jnp.maximum(i - half, 0), 0, 0))],
            scratch_shapes=[
                pltpu.VMEM(tokens.shape, tokens.dtype),
                pltpu.SemaphoreType.DMA((4,)),
            ],
        ),
        out_shape=[
            jax.ShapeDtypeStruct((half, size, width), jnp.float32) for size in [*sizes, rows]
        ],
        compiler_params=PARAMS,
        cost_estimate=NO_COST,
    )(chunks, in_hbm(tokens), in_hbm(weight))
    return sent, kept


def add_kernel(kept_ref, *refs):
    *arrived_refs, out_ref, mine_ref = refs
    half = kept_ref.shape[0] // 2
    start = 0
    for arrived_ref in arrived_refs:
        rows = pl.ds(start, arrived_ref.shape[1])
        for i in range(half):
            mine_ref[i, rows, :] = kept_ref[i, rows, :] + arrived_ref[i]
            out_ref[i, rows, :] = kept_ref[half + i, rows, :] + arrived_ref[half + i]
        start += arrived_ref.shape[1]


def add_halves(kept, arrived):
    count, rows, width = kept.shape
    out = jax.ShapeDtypeStruct((count // 2, rows, width), jnp.float32)
    return pl.pallas_call(
        add_kernel,
        out_shape=[out, out],
        compiler_params=PARAMS,
        cost_estimate=NO_COST,
    )(kept, *arrived)


def base_parts(tokens, weight, width):
    size = lax.axis_size("tensor")
    kept_order = [k for k in range(size) if not k & 1]
    kept_order.sort(key=lambda k: [k >> bit & 1 for bit in range(1, size.bit_length())])
    return base_chunks(tokens, weight, [k ^ 1 for k in kept_order] + kept_order, width)


def base_sum(sent, kept):
    arrived = [swap(piece, "tensor", 1) for piece in sent]
    distance = 2
    while distance < lax.axis_size("tensor"):
        sent, kept = add_halves(kept, arrived)
        arrived = [swap(sent, "tensor", distance)]
        distance *= 2
    return kept[0], arrived[0][0]


def pick(names_ref, table_ref, holder, holder_slots, count):
    blocks = [jnp.int32(0)] * count
    slots = [jnp.int32(0)] * count
    seen = jnp.int32(0)
    for j in range(names_ref.shape[1]):
        slot = table_ref[names_ref[0, j]]
        hit = lax.div(slot, jnp.int32(holder_slots)) == holder
        for k in range(count):
            chosen = hit & (seen == k)
            blocks[k] = jnp.where(chosen, jnp.int32(j), blocks[k])
            slots[k] = jnp.where(chosen, lax.rem(slot, jnp.int32(holder_slots)), slots[k])
        seen = seen + hit.astype(jnp.int32)
    return blocks, slots


def panel_copies(k, slot, down_ref, up_ref, out_ref, sems):
    depth = down_ref.shape[2]
    width = up_ref.shape[2]
    return [
        pltpu.make_async_copy(down_ref.at[slot], out_ref.at[k, :, pl.ds(0, depth)], sems.at[k, 0]),
        pltpu.make_async_copy(up_ref.at[slot], out_ref.at[k, :, pl.ds(depth, width)], sems.at[k, 1]),
    ]


def plan_kernel(capacity, holder_slots, *refs):
    sources, plan_ref, scalars, sems = refs[:6], refs[-8], refs[-7:-1], refs[-1]
    loads = [
        pltpu.make_async_copy(source, scalar, sems.at[i])
        for i, (source, scalar) in enumerate(zip(sources, scalars))
    ]
    for load in run_copies(loads):
        load.wait()
    names_ref, first_ref, second_ref, third_ref, table_ref, live_ref = scalars
    here = lax.axis_index("pool")
    find = functools.partial(
        pick, table_ref=table_ref, holder_slots=holder_slots, count=capacity
    )
    inner = (here == 1) | (here == 2)
    own = find(names_ref, holder=here)
    near = find(names_ref, holder=here ^ 1)
    across = find(names_ref, holder=here ^ 3)
    late = find(names_ref, holder=here ^ 2)
    rows = [
        own[0],
        near[0],
        across[0],
        late[0],
        own[1],
        across[1],
        find(first_ref, holder=here)[1],
        find(second_ref, holder=here)[1],
        find(third_ref, holder=here)[1],
        find(first_ref, holder=here ^ 3)[1],
        [inner.astype(jnp.int32)] * capacity,
        *[[live_ref[0, block] for block in phase[0]] for phase in (own, near, across, late)],
    ]
    for number, row in enumerate(rows):
        for k in range(capacity):
            plan_ref[number * capacity + k] = row[k]


OWN, ACROSS, NEAR, TO_INNER, TO_OUTER, FORWARD, INNER, LIVE, PLAN_ROWS = 4, 5, 6, 7, 8, 9, 10, 11, 15


def make_plan(names, others, table, live, holder_slots, capacity, after):
    return pl.pallas_call(
        functools.partial(plan_kernel, capacity, holder_slots),
        in_specs=[ANY] * (6 + len(after)),
        out_specs=SMEM,
        out_shape=jax.ShapeDtypeStruct((PLAN_ROWS * capacity,), jnp.int32),
        scratch_shapes=[pltpu.SMEM(names.shape, jnp.int32)] * 4
        + [pltpu.SMEM(table.shape, jnp.int32), pltpu.SMEM(live.shape, jnp.int32)]
        + [pltpu.SemaphoreType.DMA((6,))],
        compiler_params=PARAMS,
        cost_estimate=SHORT,
    )(in_hbm(names), *others, in_hbm(table), in_hbm(live), *after)


def pack_kernel(starts, capacity, plan_ref, down_ref, up_ref, *rest):
    count = len(starts)
    sems = rest[-1]
    outs = rest[-1 - count : -1]
    copies = []
    for number, start in enumerate(starts):
        for k in range(capacity):
            slot = plan_ref[start + k]
            copies += run_copies(
                panel_copies(k, slot, down_ref, up_ref, outs[number], sems.at[number])
            )
    for copy in copies:
        copy.wait()


def pack_panels(plan, starts, capacity, down, up, after=(), cost=None):
    rank, depth = down.shape[1:]
    width = up.shape[2]
    out = jax.ShapeDtypeStruct((capacity, rank, depth + width), down.dtype)
    return pl.pallas_call(
        functools.partial(pack_kernel, starts, capacity),
        in_specs=[SMEM] + [ANY] * (2 + len(after)),
        out_specs=[ANY] * len(starts),
        out_shape=[out] * len(starts),
        scratch_shapes=[pltpu.SemaphoreType.DMA((len(starts), capacity, 2))],
        compiler_params=PARAMS,
        cost_estimate=cost or NO_COST,
    )(plan, down, up, *after)


def step_of(i, start, count):
    return jnp.clip(i - start, 0, count - 1)


def source_specs(phases, shape, columns):
    specs, operands, start = [], [], 0
    for (_, count, sources), places in zip(phases, columns):
        for (panels, row), column in zip(sources, places):

            def index(i, plan, *_, start=start, count=count, row=row, column=column):
                k = step_of(i, start, count)
                return (k if row is None else plan[row + k], 0, column)

            specs.append(pl.BlockSpec(shape, index))
            operands.append(panels)
        start += count
    return specs, operands


def block_index(phases):
    def index(i, plan):
        found, start = jnp.int32(0), 0
        for row, count, _ in phases:
            inside = (i >= start) & (i < start + count)
            found = jnp.where(inside, plan[row + step_of(i, start, count)], found)
            start += count
        return found

    return index


def for_phase(phases, choose, plan_ref, refs, act):
    start, at = 0, 0
    step = pl.program_id(0)
    for _, count, sources in phases:
        mine = refs[at : at + len(sources)]

        @pl.when((step >= start) & (step < start + count))
        def _(mine=mine):
            if len(mine) == 1:
                act(mine[0])
            else:
                first = plan_ref[choose] != 0
                pl.when(first)(lambda: act(mine[0]))
                pl.when(jnp.logical_not(first))(lambda: act(mine[1]))

        start += count
        at += len(sources)


def shrink_kernel(phases, choose, plan_ref, token_ref, *refs):
    out_ref = refs[-1]

    def act(panel_ref):
        out_ref[0] = lax.dot_general(
            panel_ref[0],
            token_ref[0],
            (((1,), (1,)), ((), ())),
            preferred_element_type=jnp.float32,
        ).astype(out_ref.dtype)

    for_phase(phases, choose, plan_ref, refs, act)


def shrink(plan, row_blocks, phases, choose, after=()):
    rows, depth = row_blocks.shape[1:]
    rank = phases[0][2][0][0].shape[1]
    total = sum(count for _, count, _ in phases)
    columns = [[0] * len(sources) for _, _, sources in phases]
    specs, operands = source_specs(phases, (1, rank, depth), columns)
    block = block_index(phases)
    shapes = [(row, count, [None] * len(sources)) for row, count, sources in phases]
    return pl.pallas_call(
        functools.partial(shrink_kernel, shapes, choose),
        grid_spec=pltpu.PrefetchScalarGridSpec(
            num_scalar_prefetch=1,
            grid=(total,),
            in_specs=[pl.BlockSpec((1, rows, depth), lambda i, plan: (block(i, plan), 0, 0))]
            + specs
            + [ANY] * len(after),
            out_specs=pl.BlockSpec((1, rank, rows), lambda i, plan: (i, 0, 0)),
        ),
        out_shape=jax.ShapeDtypeStruct((total, rank, rows), jnp.bfloat16),
        compiler_params=PARAMS,
        cost_estimate=NO_COST,
    )(plan, row_blocks, *operands, *after)


def exchange(part):
    return [part] + [swap(part, "tensor", m) for m in range(1, lax.axis_size("tensor"))]


def combine_kernel(phases, choose, part_count, live_row, plan_ref, *refs):
    parts = refs[:part_count]
    mine_ref, far_ref = refs[part_count : part_count + 2]
    out_ref = refs[-1]
    total = parts[0][0].astype(jnp.float32)
    for part in parts[1:]:
        total = total + part[0].astype(jnp.float32)
    shrunk = total.astype(jnp.bfloat16)
    live = plan_ref[live_row + pl.program_id(0)]

    def act(up_ref):
        delta = lax.dot_general(
            shrunk, up_ref[0], (((0,), (0,)), ((), ())), preferred_element_type=jnp.float32
        )
        row = lax.broadcasted_iota(jnp.int32, delta.shape, 0)
        value = mine_ref[...] + far_ref[...] + ADAPTER_SCALE * delta
        out_ref[...] = jnp.where(row < live, value, 0.0).astype(out_ref.dtype)

    for_phase(phases, choose, plan_ref, refs[part_count + 2 :], act)


def combine(
    plan, live_row, parts, base, phases, columns, choose, out=None, after=(), cost=None
):
    rank, block_rows = parts[0].shape[1:]
    rows, width = base[0].shape
    total = sum(count for _, count, _ in phases)
    block = block_index(phases)
    specs = [pl.BlockSpec((1, rank, block_rows), lambda i, plan: (i, 0, 0))] * len(parts)
    specs += [pl.BlockSpec((block_rows, width), lambda i, plan: (block(i, plan), 0))] * 2
    more, operands = source_specs(phases, (1, rank, width), columns)
    specs += more + [ANY] * len(after)
    operands = [*parts, *base, *operands, *after]
    aliases = {}
    if out is not None:
        specs.append(ANY)
        operands.append(out)
        aliases = {len(operands): 0}
    shapes = [(row, count, [None] * len(sources)) for row, count, sources in phases]
    return pl.pallas_call(
        functools.partial(combine_kernel, shapes, choose, len(parts), live_row),
        grid_spec=pltpu.PrefetchScalarGridSpec(
            num_scalar_prefetch=1,
            grid=(total,),
            in_specs=specs,
            out_specs=pl.BlockSpec((block_rows, width), lambda i, plan: (block(i, plan), 0)),
        ),
        out_shape=pltpu.HBM((rows, width), jnp.bfloat16),
        input_output_aliases=aliases,
        compiler_params=PARAMS,
        cost_estimate=cost or NO_COST,
    )(plan, *operands)


def on_line_of_four(tokens, weight, row_blocks, down, up, names, table, live, capacity):
    up_column = down.shape[2] // up.shape[2]

    def across(value, pairs):
        return lax.ppermute(value, "pool", pairs)

    others = [swap(names, "pool", m) for m in range(1, 4)]
    inner_down = across(down, [(1, 2), (2, 1)])
    inner_up = across(up, [(1, 2), (2, 1)])
    sent, kept = base_parts(tokens, weight, up.shape[2])
    plan = make_plan(names, others, table, live, down.shape[0], capacity, [inner_up])
    near_out, outer_out, inner_out = pack_panels(
        plan,
        [NEAR * capacity, TO_OUTER * capacity, TO_INNER * capacity],
        capacity,
        in_hbm(down),
        in_hbm(up),
        sent[-1:],
    )
    near = across(near_out, [(0, 1), (1, 0), (2, 3), (3, 2)])
    to_outer = across(outer_out, [(0, 3), (3, 0)])
    to_inner = across(inner_out, [(0, 2), (3, 1)])
    base = base_sum(sent, kept)
    (forward_out,) = pack_panels(
        plan, [FORWARD * capacity], capacity, inner_down, inner_up, [base[0]], LONG
    )
    forwarded = across(forward_out, [(1, 0), (2, 3)])

    choose = INNER * capacity
    first = [(0, capacity, [(down, OWN * capacity)]), (capacity, capacity, [(near, None)])]
    first_up = [(0, capacity, [(up, OWN * capacity)]), first[1]]
    middle = [(2 * capacity, capacity, [(inner_down, ACROSS * capacity), (to_outer, None)])]
    middle_up = [(2 * capacity, capacity, [(inner_up, ACROSS * capacity), (to_outer, None)])]
    last = [(3 * capacity, capacity, [(to_inner, None), (forwarded, None)])]

    def write(number, parts, phases, columns, out, cost=None):
        live_row = (LIVE + number) * capacity
        return combine(plan, live_row, parts, base, phases, columns, choose, out, cost=cost)

    first_parts = exchange(shrink(plan, row_blocks, first, choose, [forward_out]))
    out = write(0, first_parts, first_up, [[0], [up_column]], None, MIDDLE)
    middle_part = shrink(plan, row_blocks, middle, choose, [in_hbm(out)])
    middle_parts = exchange(middle_part)
    last_parts = exchange(shrink(plan, row_blocks, last, choose, [middle_part]))
    out = write(2, middle_parts, middle_up, [[0, up_column]], out)
    return write(3, last_parts, last, [[up_column] * 2], out)


def on_any_pool(tokens, weight, row_blocks, down, up, names, table, live, capacity):
    pool_size = lax.axis_size("pool")
    here = lax.axis_index("pool")
    holder_slots, _, depth = down.shape
    asked = table[lax.all_gather(names[0], "pool")]
    count = jnp.arange(capacity, dtype=jnp.int32)
    arrived = []
    for distance in range(pool_size):
        slots = asked[lax.rem(here + distance, pool_size)]
        hit = slots // holder_slots == here
        chosen = hit[None, :] & (jnp.cumsum(hit.astype(jnp.int32))[None, :] == 1 + count[:, None])
        plan = jnp.sum(jnp.where(chosen, (slots % holder_slots)[None, :], 0), axis=1)
        (panels,) = pack_panels(plan, [0], capacity, down, up)
        pairs = [(i, (i + distance) % pool_size) for i in range(pool_size)]
        arrived.append(lax.ppermute(panels, "pool", pairs) if distance else panels)
    arrived = jnp.concatenate(arrived)
    owners = asked[here] // holder_slots
    blocks = jnp.arange(owners.shape[0], dtype=jnp.int32)
    earlier = (owners[:, None] == owners[None, :]) & (blocks[:, None] > blocks[None, :])
    ranks = jnp.sum(earlier.astype(jnp.int32), axis=1)
    places = lax.rem(here - owners + pool_size, pool_size) * capacity + ranks
    plan = jnp.concatenate([blocks, places, live[0]])
    base = base_sum(*base_parts(tokens, weight, up.shape[2]))
    phases = [(0, blocks.shape[0], [(arrived, blocks.shape[0])])]
    parts = exchange(shrink(plan, row_blocks, phases, 0))
    live_row = 2 * blocks.shape[0]
    return combine(plan, live_row, parts, base, phases, [[depth // up.shape[2]]], 0)


def on_device(
    tokens,
    value_weight,
    adapter_down_weight,
    adapter_up_weight,
    adapter_of_block,
    adapter_pool_slot,
    live_block_tokens,
):
    pool_size = lax.axis_size("pool")
    blocks = adapter_of_block.shape[1]
    capacity = -(-blocks // pool_size)
    row_blocks = tokens.reshape(blocks, tokens.shape[0] // blocks, tokens.shape[1])
    line = pool_size == 4 and blocks == capacity * pool_size
    route = on_line_of_four if line else on_any_pool
    return route(
        tokens,
        value_weight,
        row_blocks,
        jnp.transpose(adapter_down_weight, (0, 2, 1)),
        adapter_up_weight,
        adapter_of_block,
        adapter_pool_slot,
        live_block_tokens,
        capacity,
    )


def solution(mesh):
    return jax.shard_map(
        on_device,
        mesh=mesh,
        in_specs=(
            P(("groups", "pool"), "tensor"),
            P("tensor", None),
            P(("groups", "pool"), "tensor", None),
            P(("groups", "pool"), None, "tensor"),
            P(("groups", "pool"), None),
            P("groups"),
            P(("groups", "pool"), None),
        ),
        out_specs=P(("groups", "pool"), "tensor"),
        check_vma=False,
    )
```

```python
import functools

import jax
import jax.numpy as jnp
from jax import lax
from jax.experimental import pallas as pl
from jax.experimental.pallas import tpu as pltpu
from jax.sharding import PartitionSpec as P

ADAPTER_SCALE = 0.5
ROW_TILE = 256
PARAMS = pltpu.CompilerParams(vmem_limit_bytes=20 * 1024 * 1024)
NO_COST = pl.CostEstimate(flops=0, bytes_accessed=0, transcendentals=0)
BASE = pl.CostEstimate(flops=4 * 10**9, bytes_accessed=0, transcendentals=0)
SHORT = pl.CostEstimate(flops=10 * 10**9, bytes_accessed=0, transcendentals=0)
MIDDLE = pl.CostEstimate(flops=0 * 10**9, bytes_accessed=0, transcendentals=0)
LONG = pl.CostEstimate(flops=6 * 10**9, bytes_accessed=0, transcendentals=0)
ANY = pl.BlockSpec(memory_space=pl.ANY)
SMEM = pl.BlockSpec(memory_space=pltpu.SMEM)


def in_hbm(value):
    return pltpu.with_memory_space_constraint(value, pltpu.HBM)


def swap(value, axis, distance):
    pairs = [(i, i ^ distance) for i in range(lax.axis_size(axis))]
    return lax.ppermute(value, axis, pairs)


def run_copies(copies):
    for copy in copies:
        copy.start()
    return copies


def piece_rows(rows):
    large = rows * 3 // 8
    return [large, large, rows - 2 * large]


def base_kernel(order, tokens_ref, weight_ref, *refs):
    *sent_refs, kept_ref, tokens, weight, sems = refs
    half, rows, width = kept_ref.shape
    place = lax.axis_index("tensor")
    copies = []
    for number, (source, held) in enumerate(((weight_ref, weight), (tokens_ref, tokens))):
        tile = held.shape[0] // sems.shape[1]
        for i in range(sems.shape[1]):
            part = pl.ds(i * tile, tile)
            copies.append(
                pltpu.make_async_copy(source.at[part], held.at[part], sems.at[number, i])
            )
    run_copies(copies)
    for copy in copies[: sems.shape[1]]:
        copy.wait()
    tile = rows // sems.shape[1]
    for first in range(0, rows, tile):
        copies[sems.shape[1] + first // tile].wait()
        for number, offset in enumerate(order):
            columns = pl.ds(pl.multiple_of((place ^ offset) * width, width), width)
            part = jnp.dot(
                tokens[first : first + tile, :],
                weight[:, columns],
                preferred_element_type=jnp.float32,
            )
            if number >= half:
                kept_ref[number - half, first : first + tile, :] = part
                continue
            start = 0
            for sent_ref in sent_refs:
                stop = start + sent_ref.shape[1]
                low, high = max(first, start), min(first + tile, stop)
                if low < high:
                    sent_ref[number, low - start : high - start, :] = part[
                        low - first : high - first
                    ]
                start = stop


def base_chunks(tokens, weight, order, width):
    rows = tokens.shape[0]
    half = len(order) // 2
    sizes = [*piece_rows(rows), rows]
    *sent, kept = pl.pallas_call(
        functools.partial(base_kernel, order),
        in_specs=[ANY] * 2,
        out_specs=[pl.BlockSpec(memory_space=pltpu.VMEM)] * len(sizes),
        out_shape=[jax.ShapeDtypeStruct((half, size, width), jnp.float32) for size in sizes],
        scratch_shapes=[
            pltpu.VMEM(tokens.shape, tokens.dtype),
            pltpu.VMEM(weight.shape, weight.dtype),
            pltpu.SemaphoreType.DMA((2, 4)),
        ],
        compiler_params=PARAMS,
        cost_estimate=BASE,
    )(in_hbm(tokens), in_hbm(weight))
    return sent, kept


def add_kernel(kept_ref, *refs):
    *arrived_refs, out_ref, mine_ref = refs
    half = kept_ref.shape[0] // 2
    start = 0
    for arrived_ref in arrived_refs:
        rows = pl.ds(start, arrived_ref.shape[1])
        for i in range(half):
            mine_ref[i, rows, :] = kept_ref[i, rows, :] + arrived_ref[i]
            out = kept_ref[half + i, rows, :] + arrived_ref[half + i]
            out_ref[i, rows, :] = out.astype(out_ref.dtype)
        start += arrived_ref.shape[1]


def add_halves(kept, arrived, sent_type):
    count, rows, width = kept.shape
    shape = (count // 2, rows, width)
    return pl.pallas_call(
        add_kernel,
        out_shape=[
            jax.ShapeDtypeStruct(shape, sent_type),
            jax.ShapeDtypeStruct(shape, jnp.float32),
        ],
        compiler_params=PARAMS,
        cost_estimate=NO_COST,
    )(kept, *arrived)


def base_parts(tokens, weight, width):
    size = lax.axis_size("tensor")
    kept_order = [k for k in range(size) if not k & 1]
    kept_order.sort(key=lambda k: [k >> bit & 1 for bit in range(1, size.bit_length())])
    return base_chunks(tokens, weight, [k ^ 1 for k in kept_order] + kept_order, width)


def base_sum(sent, kept):
    arrived = [swap(piece, "tensor", 1) for piece in sent]
    distance = 2
    size = lax.axis_size("tensor")
    while distance < size:
        sent_type = jnp.bfloat16 if 2 * distance == size else jnp.float32
        sent, kept = add_halves(kept, arrived, sent_type)
        arrived = [swap(sent, "tensor", distance)]
        distance *= 2
    return kept[0], arrived[0][0]


def pick(names_ref, table_ref, holder, holder_slots, count):
    blocks = [jnp.int32(0)] * count
    slots = [jnp.int32(0)] * count
    seen = jnp.int32(0)
    for j in range(names_ref.shape[1]):
        slot = table_ref[names_ref[0, j]]
        hit = lax.div(slot, jnp.int32(holder_slots)) == holder
        for k in range(count):
            chosen = hit & (seen == k)
            blocks[k] = jnp.where(chosen, jnp.int32(j), blocks[k])
            slots[k] = jnp.where(chosen, lax.rem(slot, jnp.int32(holder_slots)), slots[k])
        seen = seen + hit.astype(jnp.int32)
    return blocks, slots


def panel_copies(k, slot, down_ref, up_ref, out_ref, sems):
    depth = down_ref.shape[2]
    width = up_ref.shape[2]
    return [
        pltpu.make_async_copy(down_ref.at[slot], out_ref.at[k, :, pl.ds(0, depth)], sems.at[k, 0]),
        pltpu.make_async_copy(up_ref.at[slot], out_ref.at[k, :, pl.ds(depth, width)], sems.at[k, 1]),
    ]


def plan_kernel(capacity, holder_slots, *refs):
    sources, plan_ref, scalars, sems = refs[:6], refs[-8], refs[-7:-1], refs[-1]
    loads = [
        pltpu.make_async_copy(source, scalar, sems.at[i])
        for i, (source, scalar) in enumerate(zip(sources, scalars))
    ]
    for load in run_copies(loads):
        load.wait()
    names_ref, first_ref, second_ref, third_ref, table_ref, live_ref = scalars
    here = lax.axis_index("pool")
    find = functools.partial(
        pick, table_ref=table_ref, holder_slots=holder_slots, count=capacity
    )
    inner = (here == 1) | (here == 2)
    own = find(names_ref, holder=here)
    near = find(names_ref, holder=here ^ 1)
    across = find(names_ref, holder=here ^ 3)
    late = find(names_ref, holder=here ^ 2)
    rows = [
        own[0],
        near[0],
        across[0],
        late[0],
        own[1],
        across[1],
        find(first_ref, holder=here)[1],
        find(second_ref, holder=here)[1],
        find(third_ref, holder=here)[1],
        find(first_ref, holder=here ^ 3)[1],
        [inner.astype(jnp.int32)] * capacity,
        *[[live_ref[0, block] for block in phase[0]] for phase in (own, near, across, late)],
    ]
    for number, row in enumerate(rows):
        for k in range(capacity):
            plan_ref[number * capacity + k] = row[k]


OWN, ACROSS, NEAR, TO_INNER, TO_OUTER, FORWARD, INNER, LIVE, PLAN_ROWS = 4, 5, 6, 7, 8, 9, 10, 11, 15


def make_plan(names, others, table, live, holder_slots, capacity, after):
    return pl.pallas_call(
        functools.partial(plan_kernel, capacity, holder_slots),
        in_specs=[ANY] * (6 + len(after)),
        out_specs=SMEM,
        out_shape=jax.ShapeDtypeStruct((PLAN_ROWS * capacity,), jnp.int32),
        scratch_shapes=[pltpu.SMEM(names.shape, jnp.int32)] * 4
        + [pltpu.SMEM(table.shape, jnp.int32), pltpu.SMEM(live.shape, jnp.int32)]
        + [pltpu.SemaphoreType.DMA((6,))],
        compiler_params=PARAMS,
        cost_estimate=SHORT,
    )(in_hbm(names), *others, in_hbm(table), in_hbm(live), *after)


def pack_kernel(starts, capacity, plan_ref, down_ref, up_ref, *rest):
    count = len(starts)
    sems = rest[-1]
    outs = rest[-1 - count : -1]
    copies = []
    for number, start in enumerate(starts):
        for k in range(capacity):
            slot = plan_ref[start + k]
            copies += run_copies(
                panel_copies(k, slot, down_ref, up_ref, outs[number], sems.at[number])
            )
    for copy in copies:
        copy.wait()


def pack_panels(plan, starts, capacity, down, up, after=(), cost=None):
    rank, depth = down.shape[1:]
    width = up.shape[2]
    out = jax.ShapeDtypeStruct((capacity, rank, depth + width), down.dtype)
    return pl.pallas_call(
        functools.partial(pack_kernel, starts, capacity),
        in_specs=[SMEM] + [ANY] * (2 + len(after)),
        out_specs=[ANY] * len(starts),
        out_shape=[out] * len(starts),
        scratch_shapes=[pltpu.SemaphoreType.DMA((len(starts), capacity, 2))],
        compiler_params=PARAMS,
        cost_estimate=cost or NO_COST,
    )(plan, down, up, *after)


def step_of(i, start, count):
    return jnp.clip(i - start, 0, count - 1)


def source_specs(phases, shape, columns):
    specs, operands, start = [], [], 0
    for (_, count, sources), places in zip(phases, columns):
        for (panels, row), column in zip(sources, places):

            def index(i, plan, *_, start=start, count=count, row=row, column=column):
                k = step_of(i, start, count)
                return (k if row is None else plan[row + k], 0, column)

            specs.append(pl.BlockSpec(shape, index))
            operands.append(panels)
        start += count
    return specs, operands


def block_index(phases):
    def index(i, plan):
        found, start = jnp.int32(0), 0
        for row, count, _ in phases:
            inside = (i >= start) & (i < start + count)
            found = jnp.where(inside, plan[row + step_of(i, start, count)], found)
            start += count
        return found

    return index


def for_phase(phases, choose, plan_ref, refs, act):
    start, at = 0, 0
    step = pl.program_id(0)
    for _, count, sources in phases:
        mine = refs[at : at + len(sources)]

        @pl.when((step >= start) & (step < start + count))
        def _(mine=mine):
            if len(mine) == 1:
                act(mine[0])
            else:
                first = plan_ref[choose] != 0
                pl.when(first)(lambda: act(mine[0]))
                pl.when(jnp.logical_not(first))(lambda: act(mine[1]))

        start += count
        at += len(sources)


def shrink_kernel(phases, choose, plan_ref, token_ref, *refs):
    out_ref = refs[-1]

    def act(panel_ref):
        out_ref[0] = lax.dot_general(
            panel_ref[0],
            token_ref[0],
            (((1,), (1,)), ((), ())),
            preferred_element_type=jnp.float32,
        ).astype(out_ref.dtype)

    for_phase(phases, choose, plan_ref, refs, act)


def shrink(plan, row_blocks, phases, choose, after=(), kind=jnp.float32):
    rows, depth = row_blocks.shape[1:]
    rank = phases[0][2][0][0].shape[1]
    total = sum(count for _, count, _ in phases)
    columns = [[0] * len(sources) for _, _, sources in phases]
    specs, operands = source_specs(phases, (1, rank, depth), columns)
    block = block_index(phases)
    shapes = [(row, count, [None] * len(sources)) for row, count, sources in phases]
    return pl.pallas_call(
        functools.partial(shrink_kernel, shapes, choose),
        grid_spec=pltpu.PrefetchScalarGridSpec(
            num_scalar_prefetch=1,
            grid=(total,),
            in_specs=[pl.BlockSpec((1, rows, depth), lambda i, plan: (block(i, plan), 0, 0))]
            + specs
            + [ANY] * len(after),
            out_specs=pl.BlockSpec((1, rank, rows), lambda i, plan: (i, 0, 0)),
        ),
        out_shape=jax.ShapeDtypeStruct((total, rank, rows), kind),
        compiler_params=PARAMS,
        cost_estimate=NO_COST,
    )(plan, row_blocks, *operands, *after)


def exchange(part):
    return [part] + [swap(part, "tensor", m) for m in range(1, lax.axis_size("tensor"))]


def combine_kernel(phases, choose, part_count, live_row, plan_ref, *refs):
    parts = refs[:part_count]
    mine_ref, far_ref = refs[part_count : part_count + 2]
    out_ref = refs[-1]
    total = parts[0][0].astype(jnp.float32)
    for part in parts[1:]:
        total = total + part[0].astype(jnp.float32)
    shrunk = total.astype(jnp.bfloat16)
    live = plan_ref[live_row + pl.program_id(0)]

    def act(up_ref):
        delta = lax.dot_general(
            shrunk, up_ref[0], (((0,), (0,)), ((), ())), preferred_element_type=jnp.float32
        )
        row = lax.broadcasted_iota(jnp.int32, delta.shape, 0)
        value = mine_ref[...] + far_ref[...] + ADAPTER_SCALE * delta
        out_ref[...] = jnp.where(row < live, value, 0.0).astype(out_ref.dtype)

    for_phase(phases, choose, plan_ref, refs[part_count + 2 :], act)


def combine(
    plan, live_row, parts, base, phases, columns, choose, out=None, after=(), cost=None
):
    rank, block_rows = parts[0].shape[1:]
    rows, width = base[0].shape
    total = sum(count for _, count, _ in phases)
    block = block_index(phases)
    specs = [pl.BlockSpec((1, rank, block_rows), lambda i, plan: (i, 0, 0))] * len(parts)
    specs += [pl.BlockSpec((block_rows, width), lambda i, plan: (block(i, plan), 0))] * 2
    more, operands = source_specs(phases, (1, rank, width), columns)
    specs += more + [ANY] * len(after)
    operands = [*parts, *base, *operands, *after]
    aliases = {}
    if out is not None:
        specs.append(ANY)
        operands.append(out)
        aliases = {len(operands): 0}
    shapes = [(row, count, [None] * len(sources)) for row, count, sources in phases]
    return pl.pallas_call(
        functools.partial(combine_kernel, shapes, choose, len(parts), live_row),
        grid_spec=pltpu.PrefetchScalarGridSpec(
            num_scalar_prefetch=1,
            grid=(total,),
            in_specs=specs,
            out_specs=pl.BlockSpec((block_rows, width), lambda i, plan: (block(i, plan), 0)),
        ),
        out_shape=pltpu.HBM((rows, width), jnp.bfloat16),
        input_output_aliases=aliases,
        compiler_params=PARAMS,
        cost_estimate=cost or NO_COST,
    )(plan, *operands)


def on_line_of_four(tokens, weight, row_blocks, down, up, names, table, live, capacity):
    up_column = down.shape[2] // up.shape[2]

    def across(value, pairs):
        return lax.ppermute(value, "pool", pairs)

    others = [swap(names, "pool", m) for m in range(1, 4)]
    inner_down = across(down, [(1, 2), (2, 1)])
    inner_up = across(up, [(1, 2), (2, 1)])
    sent, kept = base_parts(tokens, weight, up.shape[2])
    plan = make_plan(names, others, table, live, down.shape[0], capacity, [inner_up])
    near_out, outer_out, inner_out = pack_panels(
        plan,
        [NEAR * capacity, TO_OUTER * capacity, TO_INNER * capacity],
        capacity,
        in_hbm(down),
        in_hbm(up),
        sent[-1:],
    )
    near = across(near_out, [(0, 1), (1, 0), (2, 3), (3, 2)])
    to_outer = across(outer_out, [(0, 3), (3, 0)])
    to_inner = across(inner_out, [(0, 2), (3, 1)])
    base = base_sum(sent, kept)
    (forward_out,) = pack_panels(
        plan, [FORWARD * capacity], capacity, inner_down, inner_up, [base[0]], LONG
    )
    forwarded = across(forward_out, [(1, 0), (2, 3)])

    choose = INNER * capacity
    first = [(0, capacity, [(down, OWN * capacity)]), (capacity, capacity, [(near, None)])]
    first_up = [(0, capacity, [(up, OWN * capacity)]), first[1]]
    middle = [(2 * capacity, capacity, [(inner_down, ACROSS * capacity), (to_outer, None)])]
    middle_up = [(2 * capacity, capacity, [(inner_up, ACROSS * capacity), (to_outer, None)])]
    last = [(3 * capacity, capacity, [(to_inner, None), (forwarded, None)])]

    def write(number, parts, phases, columns, out, cost=None):
        live_row = (LIVE + number) * capacity
        return combine(plan, live_row, parts, base, phases, columns, choose, out, cost=cost)

    first_parts = exchange(shrink(plan, row_blocks, first, choose, [forward_out]))
    out = write(0, first_parts, first_up, [[0], [up_column]], None, MIDDLE)
    middle_part = shrink(plan, row_blocks, middle, choose, [in_hbm(out)])
    middle_parts = exchange(middle_part)
    last_parts = exchange(shrink(plan, row_blocks, last, choose, [middle_part], jnp.bfloat16))
    out = write(2, middle_parts, middle_up, [[0, up_column]], out)
    return write(3, last_parts, last, [[up_column] * 2], out)


def on_any_pool(tokens, weight, row_blocks, down, up, names, table, live, capacity):
    pool_size = lax.axis_size("pool")
    here = lax.axis_index("pool")
    holder_slots, _, depth = down.shape
    asked = table[lax.all_gather(names[0], "pool")]
    count = jnp.arange(capacity, dtype=jnp.int32)
    arrived = []
    for distance in range(pool_size):
        slots = asked[lax.rem(here + distance, pool_size)]
        hit = slots // holder_slots == here
        chosen = hit[None, :] & (jnp.cumsum(hit.astype(jnp.int32))[None, :] == 1 + count[:, None])
        plan = jnp.sum(jnp.where(chosen, (slots % holder_slots)[None, :], 0), axis=1)
        (panels,) = pack_panels(plan, [0], capacity, down, up)
        pairs = [(i, (i + distance) % pool_size) for i in range(pool_size)]
        arrived.append(lax.ppermute(panels, "pool", pairs) if distance else panels)
    arrived = jnp.concatenate(arrived)
    owners = asked[here] // holder_slots
    blocks = jnp.arange(owners.shape[0], dtype=jnp.int32)
    earlier = (owners[:, None] == owners[None, :]) & (blocks[:, None] > blocks[None, :])
    ranks = jnp.sum(earlier.astype(jnp.int32), axis=1)
    places = lax.rem(here - owners + pool_size, pool_size) * capacity + ranks
    plan = jnp.concatenate([blocks, places, live[0]])
    base = base_sum(*base_parts(tokens, weight, up.shape[2]))
    phases = [(0, blocks.shape[0], [(arrived, blocks.shape[0])])]
    parts = exchange(shrink(plan, row_blocks, phases, 0))
    live_row = 2 * blocks.shape[0]
    return combine(plan, live_row, parts, base, phases, [[depth // up.shape[2]]], 0)


def on_device(
    tokens,
    value_weight,
    adapter_down_weight,
    adapter_up_weight,
    adapter_of_block,
    adapter_pool_slot,
    live_block_tokens,
):
    pool_size = lax.axis_size("pool")
    blocks = adapter_of_block.shape[1]
    capacity = -(-blocks // pool_size)
    row_blocks = tokens.reshape(blocks, tokens.shape[0] // blocks, tokens.shape[1])
    line = pool_size == 4 and blocks == capacity * pool_size
    route = on_line_of_four if line else on_any_pool
    return route(
        tokens,
        value_weight,
        row_blocks,
        jnp.transpose(adapter_down_weight, (0, 2, 1)),
        adapter_up_weight,
        adapter_of_block,
        adapter_pool_slot,
        live_block_tokens,
        capacity,
    )


def solution(mesh):
    return jax.shard_map(
        on_device,
        mesh=mesh,
        in_specs=(
            P(("groups", "pool"), "tensor"),
            P("tensor", None),
            P(("groups", "pool"), "tensor", None),
            P(("groups", "pool"), None, "tensor"),
            P(("groups", "pool"), None),
            P("groups"),
            P(("groups", "pool"), None),
        ),
        out_specs=P(("groups", "pool"), "tensor"),
        check_vma=False,
    )
```

```python
import functools

import jax
import jax.numpy as jnp
from jax import lax
from jax.experimental import pallas as pl
from jax.experimental.pallas import tpu as pltpu
from jax.sharding import PartitionSpec as P

ADAPTER_SCALE = 0.5
ROW_TILE = 256
PARAMS = pltpu.CompilerParams(vmem_limit_bytes=20 * 1024 * 1024)
NO_COST = pl.CostEstimate(flops=0, bytes_accessed=0, transcendentals=0)
BASE = pl.CostEstimate(flops=0 * 10**9, bytes_accessed=0, transcendentals=0)
SHORT = pl.CostEstimate(flops=2 * 10**9, bytes_accessed=0, transcendentals=0)
PACK = pl.CostEstimate(flops=3 * 10**9, bytes_accessed=0, transcendentals=0)
FIRST = pl.CostEstimate(flops=3 * 10**9, bytes_accessed=0, transcendentals=0)
MIDDLE = pl.CostEstimate(flops=0 * 10**9, bytes_accessed=0, transcendentals=0)
LONG = pl.CostEstimate(flops=6 * 10**9, bytes_accessed=0, transcendentals=0)
ANY = pl.BlockSpec(memory_space=pl.ANY)
SMEM = pl.BlockSpec(memory_space=pltpu.SMEM)
VMEM = pl.BlockSpec(memory_space=pltpu.VMEM)


def in_hbm(value):
    return pltpu.with_memory_space_constraint(value, pltpu.HBM)


def swap(value, axis, distance):
    pairs = [(i, i ^ distance) for i in range(lax.axis_size(axis))]
    return lax.ppermute(value, axis, pairs)


def run_copies(copies):
    for copy in copies:
        copy.start()
    return copies


def piece_rows(rows):
    large = rows * 3 // 8
    return [large, large, rows - 2 * large]


def base_kernel(order, tokens_ref, weight_ref, *refs):
    *refs, kept_ref, tokens, weight, sems = refs
    sent_refs = refs[-len(piece_rows(kept_ref.shape[1])) :]
    half, rows, width = kept_ref.shape
    place = lax.axis_index("tensor")
    copies = []
    for number, (source, held) in enumerate(((weight_ref, weight), (tokens_ref, tokens))):
        tile = held.shape[0] // sems.shape[1]
        for i in range(sems.shape[1]):
            part = pl.ds(i * tile, tile)
            copies.append(
                pltpu.make_async_copy(source.at[part], held.at[part], sems.at[number, i])
            )
    run_copies(copies)
    for copy in copies[: sems.shape[1]]:
        copy.wait()
    tile = rows // sems.shape[1]
    for first in range(0, rows, tile):
        copies[sems.shape[1] + first // tile].wait()
        for number, offset in enumerate(order):
            columns = pl.ds(pl.multiple_of((place ^ offset) * width, width), width)
            part = jnp.dot(
                tokens[first : first + tile, :],
                weight[:, columns],
                preferred_element_type=jnp.float32,
            )
            if number >= half:
                kept_ref[number - half, first : first + tile, :] = part
                continue
            start = 0
            for sent_ref in sent_refs:
                stop = start + sent_ref.shape[1]
                low, high = max(first, start), min(first + tile, stop)
                if low < high:
                    sent_ref[number, low - start : high - start, :] = part[
                        low - first : high - first
                    ]
                start = stop


def base_chunks(tokens, weight, order, width, after):
    rows = tokens.shape[0]
    half = len(order) // 2
    sizes = [*piece_rows(rows), rows]
    *sent, kept = pl.pallas_call(
        functools.partial(base_kernel, order),
        in_specs=[ANY] * (2 + len(after)),
        out_specs=[VMEM] * len(sizes),
        out_shape=[jax.ShapeDtypeStruct((half, size, width), jnp.float32) for size in sizes],
        scratch_shapes=[
            pltpu.VMEM(tokens.shape, tokens.dtype),
            pltpu.VMEM(weight.shape, weight.dtype),
            pltpu.SemaphoreType.DMA((2, 4)),
        ],
        compiler_params=PARAMS,
        cost_estimate=BASE,
    )(in_hbm(tokens), in_hbm(weight), *after)
    return sent, kept


def add_kernel(pieces, kept_ref, *refs):
    arrived_refs, out_ref, mine_ref = refs[:pieces], *refs[-2:]
    half = kept_ref.shape[0] // 2
    start = 0
    for arrived_ref in arrived_refs:
        rows = pl.ds(start, arrived_ref.shape[1])
        for i in range(half):
            mine_ref[i, rows, :] = kept_ref[i, rows, :] + arrived_ref[i]
            out = kept_ref[half + i, rows, :] + arrived_ref[half + i]
            out_ref[i, rows, :] = out.astype(out_ref.dtype)
        start += arrived_ref.shape[1]


def add_halves(kept, arrived, sent_type, after):
    count, rows, width = kept.shape
    shape = (count // 2, rows, width)
    return pl.pallas_call(
        functools.partial(add_kernel, len(arrived)),
        in_specs=[VMEM] * (1 + len(arrived)) + [ANY] * len(after),
        out_shape=[
            jax.ShapeDtypeStruct(shape, sent_type),
            jax.ShapeDtypeStruct(shape, jnp.float32),
        ],
        compiler_params=PARAMS,
        cost_estimate=NO_COST,
    )(kept, *arrived, *after)


def base_parts(tokens, weight, width, after=()):
    size = lax.axis_size("tensor")
    kept_order = [k for k in range(size) if not k & 1]
    kept_order.sort(key=lambda k: [k >> bit & 1 for bit in range(1, size.bit_length())])
    return base_chunks(tokens, weight, [k ^ 1 for k in kept_order] + kept_order, width, after)


def base_sum(sent, kept, after=()):
    arrived = [swap(piece, "tensor", 1) for piece in sent]
    distance = 2
    size = lax.axis_size("tensor")
    while distance < size:
        sent_type = jnp.bfloat16 if 2 * distance == size else jnp.float32
        sent, kept = add_halves(kept, arrived, sent_type, after)
        arrived = [swap(sent, "tensor", distance)]
        distance *= 2
    return kept[0], arrived[0][0]


def pick(names_ref, table_ref, holder, holder_slots, count):
    blocks = [jnp.int32(0)] * count
    slots = [jnp.int32(0)] * count
    seen = jnp.int32(0)
    for j in range(names_ref.shape[1]):
        slot = table_ref[names_ref[0, j]]
        hit = lax.div(slot, jnp.int32(holder_slots)) == holder
        for k in range(count):
            chosen = hit & (seen == k)
            blocks[k] = jnp.where(chosen, jnp.int32(j), blocks[k])
            slots[k] = jnp.where(chosen, lax.rem(slot, jnp.int32(holder_slots)), slots[k])
        seen = seen + hit.astype(jnp.int32)
    return blocks, slots


def panel_copies(k, slot, down_ref, up_ref, out_ref, sems):
    depth = down_ref.shape[2]
    width = up_ref.shape[2]
    return [
        pltpu.make_async_copy(down_ref.at[slot], out_ref.at[k, :, pl.ds(0, depth)], sems.at[k, 0]),
        pltpu.make_async_copy(up_ref.at[slot], out_ref.at[k, :, pl.ds(depth, width)], sems.at[k, 1]),
    ]


def plan_kernel(capacity, holder_slots, *refs):
    sources, plan_ref, scalars, sems = refs[:6], refs[-8], refs[-7:-1], refs[-1]
    loads = [
        pltpu.make_async_copy(source, scalar, sems.at[i])
        for i, (source, scalar) in enumerate(zip(sources, scalars))
    ]
    for load in run_copies(loads):
        load.wait()
    names_ref, first_ref, second_ref, third_ref, table_ref, live_ref = scalars
    here = lax.axis_index("pool")
    find = functools.partial(
        pick, table_ref=table_ref, holder_slots=holder_slots, count=capacity
    )
    inner = (here == 1) | (here == 2)
    own = find(names_ref, holder=here)
    near = find(names_ref, holder=here ^ 1)
    across = find(names_ref, holder=here ^ 3)
    late = find(names_ref, holder=here ^ 2)
    rows = [
        own[0],
        near[0],
        across[0],
        late[0],
        own[1],
        across[1],
        find(first_ref, holder=here)[1],
        find(second_ref, holder=here)[1],
        find(third_ref, holder=here)[1],
        find(first_ref, holder=here ^ 3)[1],
        [inner.astype(jnp.int32)] * capacity,
        *[[live_ref[0, block] for block in phase[0]] for phase in (own, near, across, late)],
    ]
    for number, row in enumerate(rows):
        for k in range(capacity):
            plan_ref[number * capacity + k] = row[k]


OWN, ACROSS, NEAR, TO_INNER, TO_OUTER, FORWARD, INNER, LIVE, PLAN_ROWS = 4, 5, 6, 7, 8, 9, 10, 11, 15


def make_plan(names, others, table, live, holder_slots, capacity):
    return pl.pallas_call(
        functools.partial(plan_kernel, capacity, holder_slots),
        in_specs=[ANY] * 6,
        out_specs=SMEM,
        out_shape=jax.ShapeDtypeStruct((PLAN_ROWS * capacity,), jnp.int32),
        scratch_shapes=[pltpu.SMEM(names.shape, jnp.int32)] * 4
        + [pltpu.SMEM(table.shape, jnp.int32), pltpu.SMEM(live.shape, jnp.int32)]
        + [pltpu.SemaphoreType.DMA((6,))],
        compiler_params=PARAMS,
        cost_estimate=SHORT,
    )(in_hbm(names), *others, in_hbm(table), in_hbm(live))


def pack_kernel(starts, capacity, plan_ref, down_ref, up_ref, *rest):
    count = len(starts)
    sems = rest[-1]
    outs = rest[-1 - count : -1]
    copies = []
    for number, start in enumerate(starts):
        for k in range(capacity):
            slot = plan_ref[start + k]
            copies += run_copies(
                panel_copies(k, slot, down_ref, up_ref, outs[number], sems.at[number])
            )
    for copy in copies:
        copy.wait()


def pack_panels(plan, starts, capacity, down, up, after=(), cost=None):
    rank, depth = down.shape[1:]
    width = up.shape[2]
    out = jax.ShapeDtypeStruct((capacity, rank, depth + width), down.dtype)
    return pl.pallas_call(
        functools.partial(pack_kernel, starts, capacity),
        in_specs=[SMEM] + [ANY] * (2 + len(after)),
        out_specs=[ANY] * len(starts),
        out_shape=[out] * len(starts),
        scratch_shapes=[pltpu.SemaphoreType.DMA((len(starts), capacity, 2))],
        compiler_params=PARAMS,
        cost_estimate=cost or NO_COST,
    )(plan, down, up, *after)


def each_block(phases, choose, plan_ref, refs, act):
    number = 0
    for row, count, rows in phases:
        mine, refs = refs[: len(rows)], refs[len(rows) :]

        def run(ref, row_of, number=number, row=row, count=count):
            for k in range(count):
                panel = ref.at[k if row_of is None else plan_ref[row_of + k]]
                act(number + k, plan_ref[row + k], panel)

        if len(rows) == 1:
            run(mine[0], rows[0])
        else:
            first = plan_ref[choose] != 0
            pl.when(first)(functools.partial(run, mine[0], rows[0]))
            pl.when(jnp.logical_not(first))(functools.partial(run, mine[1], rows[1]))
        number += count


def split_phases(phases):
    shapes = [(row, count, [source[1] for source in sources]) for row, count, sources in phases]
    return shapes, [source[0] for _, _, sources in phases for source in sources]


def shrink_kernel(phases, choose, plan_ref, token_ref, *refs):
    out_ref = refs[-1]
    depth = token_ref.shape[2]

    def act(number, block, panel_ref):
        out_ref[number] = lax.dot_general(
            panel_ref[:, :depth],
            token_ref[block],
            (((1,), (1,)), ((), ())),
            preferred_element_type=jnp.float32,
        ).astype(out_ref.dtype)

    each_block(phases, choose, plan_ref, refs, act)


def shrink(plan, row_blocks, phases, choose, after=(), kind=jnp.float32, cost=None):
    shapes, panels = split_phases(phases)
    total = sum(count for _, count, _ in phases)
    shape = (total, panels[0].shape[1], row_blocks.shape[1])
    return pl.pallas_call(
        functools.partial(shrink_kernel, shapes, choose),
        in_specs=[SMEM] + [VMEM] * (1 + len(panels)) + [ANY] * len(after),
        out_specs=VMEM,
        out_shape=jax.ShapeDtypeStruct(shape, kind),
        compiler_params=PARAMS,
        cost_estimate=cost or NO_COST,
    )(plan, row_blocks, *panels, *after)


def exchange(part):
    return [part] + [swap(part, "tensor", m) for m in range(1, lax.axis_size("tensor"))]


def combine_kernel(phases, choose, part_count, live_row, plan_ref, *refs):
    parts = refs[:part_count]
    mine_ref, far_ref = refs[part_count : part_count + 2]
    out_ref, held_ref, sems = refs[-3:]
    total, block_rows, width = held_ref.shape

    def copy_of(number, block):
        rows = pl.ds(pl.multiple_of(block * block_rows, block_rows), block_rows)
        return pltpu.make_async_copy(held_ref.at[number], out_ref.at[rows], sems.at[number])

    def act(number, block, panel_ref):
        shrunk = parts[0][number].astype(jnp.float32)
        for part in parts[1:]:
            shrunk = shrunk + part[number].astype(jnp.float32)
        start = panel_ref.shape[1] - width
        delta = lax.dot_general(
            shrunk.astype(jnp.bfloat16),
            panel_ref[:, start : start + width],
            (((0,), (0,)), ((), ())),
            preferred_element_type=jnp.float32,
        )
        rows = pl.ds(pl.multiple_of(block * block_rows, block_rows), block_rows)
        row = lax.broadcasted_iota(jnp.int32, delta.shape, 0)
        value = mine_ref[rows, :] + far_ref[rows, :].astype(jnp.float32) + ADAPTER_SCALE * delta
        value = jnp.where(row < plan_ref[live_row + number], value, 0.0)
        held_ref[number] = value.astype(held_ref.dtype)
        copy_of(number, block).start()

    each_block(phases, choose, plan_ref, refs[part_count + 2 :], act)
    number = 0
    for row, count, _ in phases:
        for k in range(count):
            copy_of(number, plan_ref[row + k]).wait()
            number += 1


def combine(plan, live_row, parts, base, phases, choose, out=None, cost=None):
    block_rows = parts[0].shape[2]
    rows, width = base[0].shape
    shapes, panels = split_phases(phases)
    total = sum(count for _, count, _ in phases)
    operands = [*parts, *base, *panels]
    specs = [VMEM] * len(operands)
    aliases = {}
    if out is not None:
        specs.append(ANY)
        operands.append(out)
        aliases = {len(operands): 0}
    return pl.pallas_call(
        functools.partial(combine_kernel, shapes, choose, len(parts), live_row),
        in_specs=[SMEM] + specs,
        out_specs=ANY,
        out_shape=pltpu.HBM((rows, width), jnp.bfloat16),
        input_output_aliases=aliases,
        scratch_shapes=[
            pltpu.VMEM((total, block_rows, width), jnp.bfloat16),
            pltpu.SemaphoreType.DMA((total,)),
        ],
        compiler_params=PARAMS,
        cost_estimate=cost or NO_COST,
    )(plan, *operands)


def on_line_of_four(tokens, weight, row_blocks, down, up, names, table, live, capacity):
    def across(value, pairs):
        return lax.ppermute(value, "pool", pairs)

    others = [swap(names, "pool", m) for m in range(1, 4)]
    inner_down = across(down, [(1, 2), (2, 1)])
    inner_up = across(up, [(1, 2), (2, 1)])
    plan = make_plan(names, others, table, live, down.shape[0], capacity)
    near_out, outer_out, inner_out = pack_panels(
        plan,
        [NEAR * capacity, TO_OUTER * capacity, TO_INNER * capacity],
        capacity,
        in_hbm(down),
        in_hbm(up),
        [inner_up],
        PACK,
    )
    near = across(near_out, [(0, 1), (1, 0), (2, 3), (3, 2)])
    to_outer = across(outer_out, [(0, 3), (3, 0)])
    to_inner = across(inner_out, [(0, 2), (3, 1)])
    sent, kept = base_parts(tokens, weight, up.shape[2], [near_out])

    choose = INNER * capacity
    first = [(0, capacity, [(down, OWN * capacity)]), (capacity, capacity, [(near, None)])]
    first_up = [(0, capacity, [(up, OWN * capacity)]), first[1]]
    first_part = shrink(plan, row_blocks, first, choose, cost=FIRST)
    base = base_sum(sent, kept, [first_part])
    (forward_out,) = pack_panels(
        plan, [FORWARD * capacity], capacity, inner_down, inner_up, [base[0]], LONG
    )
    forwarded = across(forward_out, [(1, 0), (2, 3)])
    middle = [(2 * capacity, capacity, [(inner_down, ACROSS * capacity), (to_outer, None)])]
    middle_up = [(2 * capacity, capacity, [(inner_up, ACROSS * capacity), (to_outer, None)])]
    last = [(3 * capacity, capacity, [(to_inner, None), (forwarded, None)])]

    def write(number, parts, phases, out, cost=None):
        live_row = (LIVE + number) * capacity
        return combine(plan, live_row, parts, base, phases, choose, out, cost)

    first_parts = exchange(first_part)
    out = write(0, first_parts, first_up, None, MIDDLE)
    middle_part = shrink(plan, row_blocks, middle, choose, [in_hbm(out)])
    middle_parts = exchange(middle_part)
    last_parts = exchange(shrink(plan, row_blocks, last, choose, [middle_part], jnp.bfloat16))
    out = write(2, middle_parts, middle_up, out)
    return write(3, last_parts, last, out)


def on_any_pool(tokens, weight, row_blocks, down, up, names, table, live, capacity):
    pool_size = lax.axis_size("pool")
    here = lax.axis_index("pool")
    holder_slots = down.shape[0]
    asked = table[lax.all_gather(names[0], "pool")]
    count = jnp.arange(capacity, dtype=jnp.int32)
    arrived = []
    for distance in range(pool_size):
        slots = asked[lax.rem(here + distance, pool_size)]
        hit = slots // holder_slots == here
        chosen = hit[None, :] & (jnp.cumsum(hit.astype(jnp.int32))[None, :] == 1 + count[:, None])
        plan = jnp.sum(jnp.where(chosen, (slots % holder_slots)[None, :], 0), axis=1)
        (panels,) = pack_panels(plan, [0], capacity, down, up)
        pairs = [(i, (i + distance) % pool_size) for i in range(pool_size)]
        arrived.append(lax.ppermute(panels, "pool", pairs) if distance else panels)
    arrived = jnp.concatenate(arrived)
    owners = asked[here] // holder_slots
    blocks = jnp.arange(owners.shape[0], dtype=jnp.int32)
    earlier = (owners[:, None] == owners[None, :]) & (blocks[:, None] > blocks[None, :])
    ranks = jnp.sum(earlier.astype(jnp.int32), axis=1)
    places = lax.rem(here - owners + pool_size, pool_size) * capacity + ranks
    plan = jnp.concatenate([blocks, places, live[0]])
    base = base_sum(*base_parts(tokens, weight, up.shape[2]))
    phases = [(0, blocks.shape[0], [(arrived, blocks.shape[0])])]
    parts = exchange(shrink(plan, row_blocks, phases, 0))
    live_row = 2 * blocks.shape[0]
    return combine(plan, live_row, parts, base, phases, 0)


def on_device(
    tokens,
    value_weight,
    adapter_down_weight,
    adapter_up_weight,
    adapter_of_block,
    adapter_pool_slot,
    live_block_tokens,
):
    pool_size = lax.axis_size("pool")
    blocks = adapter_of_block.shape[1]
    capacity = -(-blocks // pool_size)
    row_blocks = tokens.reshape(blocks, tokens.shape[0] // blocks, tokens.shape[1])
    line = pool_size == 4 and blocks == capacity * pool_size
    route = on_line_of_four if line else on_any_pool
    return route(
        tokens,
        value_weight,
        row_blocks,
        jnp.transpose(adapter_down_weight, (0, 2, 1)),
        adapter_up_weight,
        adapter_of_block,
        adapter_pool_slot,
        live_block_tokens,
        capacity,
    )


def solution(mesh):
    return jax.shard_map(
        on_device,
        mesh=mesh,
        in_specs=(
            P(("groups", "pool"), "tensor"),
            P("tensor", None),
            P(("groups", "pool"), "tensor", None),
            P(("groups", "pool"), None, "tensor"),
            P(("groups", "pool"), None),
            P("groups"),
            P(("groups", "pool"), None),
        ),
        out_specs=P(("groups", "pool"), "tensor"),
        check_vma=False,
    )
```

```python
import functools

import jax
import jax.numpy as jnp
from jax import lax
from jax.experimental import pallas as pl
from jax.experimental.pallas import tpu as pltpu
from jax.sharding import PartitionSpec as P

ADAPTER_SCALE = 0.5
ROW_TILE = 256
PARAMS = pltpu.CompilerParams(vmem_limit_bytes=20 * 1024 * 1024)
NO_COST = pl.CostEstimate(flops=0, bytes_accessed=0, transcendentals=0)
BASE = pl.CostEstimate(flops=4 * 10**9, bytes_accessed=0, transcendentals=0)
SHORT = pl.CostEstimate(flops=10 * 10**9, bytes_accessed=0, transcendentals=0)
MIDDLE = pl.CostEstimate(flops=0 * 10**9, bytes_accessed=0, transcendentals=0)
LONG = pl.CostEstimate(flops=6 * 10**9, bytes_accessed=0, transcendentals=0)
ANY = pl.BlockSpec(memory_space=pl.ANY)
SMEM = pl.BlockSpec(memory_space=pltpu.SMEM)
VMEM = pl.BlockSpec(memory_space=pltpu.VMEM)


def in_hbm(value):
    return pltpu.with_memory_space_constraint(value, pltpu.HBM)


def swap(value, axis, distance):
    pairs = [(i, i ^ distance) for i in range(lax.axis_size(axis))]
    return lax.ppermute(value, axis, pairs)


def run_copies(copies):
    for copy in copies:
        copy.start()
    return copies


def piece_rows(rows):
    large = rows * 3 // 8
    return [large, large, rows - 2 * large]


def base_kernel(order, tokens_ref, weight_ref, *refs):
    *sent_refs, kept_ref, tokens, weight, sems = refs
    half, rows, width = kept_ref.shape
    place = lax.axis_index("tensor")
    copies = []
    for number, (source, held) in enumerate(((weight_ref, weight), (tokens_ref, tokens))):
        tile = held.shape[0] // sems.shape[1]
        for i in range(sems.shape[1]):
            part = pl.ds(i * tile, tile)
            copies.append(
                pltpu.make_async_copy(source.at[part], held.at[part], sems.at[number, i])
            )
    run_copies(copies)
    for copy in copies[: sems.shape[1]]:
        copy.wait()
    tile = rows // sems.shape[1]
    for first in range(0, rows, tile):
        copies[sems.shape[1] + first // tile].wait()
        for number, offset in enumerate(order):
            columns = pl.ds(pl.multiple_of((place ^ offset) * width, width), width)
            part = jnp.dot(
                tokens[first : first + tile, :],
                weight[:, columns],
                preferred_element_type=jnp.float32,
            )
            if number >= half:
                kept_ref[number - half, first : first + tile, :] = part
                continue
            start = 0
            for sent_ref in sent_refs:
                stop = start + sent_ref.shape[1]
                low, high = max(first, start), min(first + tile, stop)
                if low < high:
                    sent_ref[number, low - start : high - start, :] = part[
                        low - first : high - first
                    ]
                start = stop


def base_chunks(tokens, weight, order, width):
    rows = tokens.shape[0]
    half = len(order) // 2
    sizes = [*piece_rows(rows), rows]
    *sent, kept = pl.pallas_call(
        functools.partial(base_kernel, order),
        in_specs=[ANY] * 2,
        out_specs=[VMEM] * len(sizes),
        out_shape=[jax.ShapeDtypeStruct((half, size, width), jnp.float32) for size in sizes],
        scratch_shapes=[
            pltpu.VMEM(tokens.shape, tokens.dtype),
            pltpu.VMEM(weight.shape, weight.dtype),
            pltpu.SemaphoreType.DMA((2, 4)),
        ],
        compiler_params=PARAMS,
        cost_estimate=BASE,
    )(in_hbm(tokens), in_hbm(weight))
    return sent, kept


def add_kernel(kept_ref, *refs):
    *arrived_refs, out_ref, mine_ref = refs
    half = kept_ref.shape[0] // 2
    start = 0
    for arrived_ref in arrived_refs:
        rows = pl.ds(start, arrived_ref.shape[1])
        for i in range(half):
            mine_ref[i, rows, :] = kept_ref[i, rows, :] + arrived_ref[i]
            out = kept_ref[half + i, rows, :] + arrived_ref[half + i]
            out_ref[i, rows, :] = out.astype(out_ref.dtype)
        start += arrived_ref.shape[1]


def add_halves(kept, arrived, sent_type):
    count, rows, width = kept.shape
    shape = (count // 2, rows, width)
    return pl.pallas_call(
        add_kernel,
        in_specs=[VMEM] * (1 + len(arrived)),
        out_shape=[
            jax.ShapeDtypeStruct(shape, sent_type),
            jax.ShapeDtypeStruct(shape, jnp.float32),
        ],
        compiler_params=PARAMS,
        cost_estimate=NO_COST,
    )(kept, *arrived)


def base_parts(tokens, weight, width):
    size = lax.axis_size("tensor")
    kept_order = [k for k in range(size) if not k & 1]
    kept_order.sort(key=lambda k: [k >> bit & 1 for bit in range(1, size.bit_length())])
    return base_chunks(tokens, weight, [k ^ 1 for k in kept_order] + kept_order, width)


def base_sum(sent, kept):
    arrived = [swap(piece, "tensor", 1) for piece in sent]
    distance = 2
    size = lax.axis_size("tensor")
    while distance < size:
        sent_type = jnp.bfloat16 if 2 * distance == size else jnp.float32
        sent, kept = add_halves(kept, arrived, sent_type)
        arrived = [swap(sent, "tensor", distance)]
        distance *= 2
    return kept[0], arrived[0][0]


def pick(names_ref, table_ref, holder, holder_slots, count):
    blocks = [jnp.int32(0)] * count
    slots = [jnp.int32(0)] * count
    seen = jnp.int32(0)
    for j in range(names_ref.shape[1]):
        slot = table_ref[names_ref[0, j]]
        hit = lax.div(slot, jnp.int32(holder_slots)) == holder
        for k in range(count):
            chosen = hit & (seen == k)
            blocks[k] = jnp.where(chosen, jnp.int32(j), blocks[k])
            slots[k] = jnp.where(chosen, lax.rem(slot, jnp.int32(holder_slots)), slots[k])
        seen = seen + hit.astype(jnp.int32)
    return blocks, slots


def panel_copies(k, slot, down_ref, up_ref, out_ref, sems):
    depth = down_ref.shape[2]
    width = up_ref.shape[2]
    return [
        pltpu.make_async_copy(down_ref.at[slot], out_ref.at[k, :, pl.ds(0, depth)], sems.at[k, 0]),
        pltpu.make_async_copy(up_ref.at[slot], out_ref.at[k, :, pl.ds(depth, width)], sems.at[k, 1]),
    ]


def plan_kernel(capacity, holder_slots, *refs):
    sources, plan_ref, scalars, sems = refs[:6], refs[-8], refs[-7:-1], refs[-1]
    loads = [
        pltpu.make_async_copy(source, scalar, sems.at[i])
        for i, (source, scalar) in enumerate(zip(sources, scalars))
    ]
    for load in run_copies(loads):
        load.wait()
    names_ref, first_ref, second_ref, third_ref, table_ref, live_ref = scalars
    here = lax.axis_index("pool")
    find = functools.partial(
        pick, table_ref=table_ref, holder_slots=holder_slots, count=capacity
    )
    inner = (here == 1) | (here == 2)
    own = find(names_ref, holder=here)
    near = find(names_ref, holder=here ^ 1)
    across = find(names_ref, holder=here ^ 3)
    late = find(names_ref, holder=here ^ 2)
    rows = [
        own[0],
        near[0],
        across[0],
        late[0],
        own[1],
        across[1],
        find(first_ref, holder=here)[1],
        find(second_ref, holder=here)[1],
        find(third_ref, holder=here)[1],
        find(first_ref, holder=here ^ 3)[1],
        [inner.astype(jnp.int32)] * capacity,
        *[[live_ref[0, block] for block in phase[0]] for phase in (own, near, across, late)],
    ]
    for number, row in enumerate(rows):
        for k in range(capacity):
            plan_ref[number * capacity + k] = row[k]


OWN, ACROSS, NEAR, TO_INNER, TO_OUTER, FORWARD, INNER, LIVE, PLAN_ROWS = 4, 5, 6, 7, 8, 9, 10, 11, 15


def make_plan(names, others, table, live, holder_slots, capacity, after):
    return pl.pallas_call(
        functools.partial(plan_kernel, capacity, holder_slots),
        in_specs=[ANY] * (6 + len(after)),
        out_specs=SMEM,
        out_shape=jax.ShapeDtypeStruct((PLAN_ROWS * capacity,), jnp.int32),
        scratch_shapes=[pltpu.SMEM(names.shape, jnp.int32)] * 4
        + [pltpu.SMEM(table.shape, jnp.int32), pltpu.SMEM(live.shape, jnp.int32)]
        + [pltpu.SemaphoreType.DMA((6,))],
        compiler_params=PARAMS,
        cost_estimate=SHORT,
    )(in_hbm(names), *others, in_hbm(table), in_hbm(live), *after)


def pack_kernel(starts, capacity, plan_ref, down_ref, up_ref, *rest):
    count = len(starts)
    sems = rest[-1]
    outs = rest[-1 - count : -1]
    copies = []
    for number, start in enumerate(starts):
        for k in range(capacity):
            slot = plan_ref[start + k]
            copies += run_copies(
                panel_copies(k, slot, down_ref, up_ref, outs[number], sems.at[number])
            )
    for copy in copies:
        copy.wait()


def pack_panels(plan, starts, capacity, down, up, after=(), cost=None):
    rank, depth = down.shape[1:]
    width = up.shape[2]
    out = jax.ShapeDtypeStruct((capacity, rank, depth + width), down.dtype)
    return pl.pallas_call(
        functools.partial(pack_kernel, starts, capacity),
        in_specs=[SMEM] + [ANY] * (2 + len(after)),
        out_specs=[ANY] * len(starts),
        out_shape=[out] * len(starts),
        scratch_shapes=[pltpu.SemaphoreType.DMA((len(starts), capacity, 2))],
        compiler_params=PARAMS,
        cost_estimate=cost or NO_COST,
    )(plan, down, up, *after)


def each_block(phases, choose, plan_ref, refs, act):
    number = 0
    for row, count, rows in phases:
        mine, refs = refs[: len(rows)], refs[len(rows) :]

        def run(ref, row_of, number=number, row=row, count=count):
            for k in range(count):
                panel = ref.at[k if row_of is None else plan_ref[row_of + k]]
                act(number + k, plan_ref[row + k], panel)

        if len(rows) == 1:
            run(mine[0], rows[0])
        else:
            first = plan_ref[choose] != 0
            pl.when(first)(functools.partial(run, mine[0], rows[0]))
            pl.when(jnp.logical_not(first))(functools.partial(run, mine[1], rows[1]))
        number += count


def split_phases(phases):
    shapes = [(row, count, [source[1] for source in sources]) for row, count, sources in phases]
    return shapes, [source[0] for _, _, sources in phases for source in sources]


def shrink_kernel(phases, choose, plan_ref, token_ref, *refs):
    out_ref = refs[-1]
    depth = token_ref.shape[2]

    def act(number, block, panel_ref):
        out_ref[number] = lax.dot_general(
            panel_ref[:, :depth],
            token_ref[block],
            (((1,), (1,)), ((), ())),
            preferred_element_type=jnp.float32,
        ).astype(out_ref.dtype)

    each_block(phases, choose, plan_ref, refs, act)


def shrink(plan, row_blocks, phases, choose, after=(), kind=jnp.float32, cost=None):
    shapes, panels = split_phases(phases)
    total = sum(count for _, count, _ in phases)
    shape = (total, panels[0].shape[1], row_blocks.shape[1])
    return pl.pallas_call(
        functools.partial(shrink_kernel, shapes, choose),
        in_specs=[SMEM] + [VMEM] * (1 + len(panels)) + [ANY] * len(after),
        out_specs=VMEM,
        out_shape=jax.ShapeDtypeStruct(shape, kind),
        compiler_params=PARAMS,
        cost_estimate=cost or NO_COST,
    )(plan, row_blocks, *panels, *after)


def exchange(part):
    return [part] + [swap(part, "tensor", m) for m in range(1, lax.axis_size("tensor"))]


def combine_kernel(phases, choose, part_count, live_row, plan_ref, *refs):
    parts = refs[:part_count]
    mine_ref, far_ref = refs[part_count : part_count + 2]
    out_ref, held_ref, sems = refs[-3:]
    total, block_rows, width = held_ref.shape

    def copy_of(number, block):
        rows = pl.ds(pl.multiple_of(block * block_rows, block_rows), block_rows)
        return pltpu.make_async_copy(held_ref.at[number], out_ref.at[rows], sems.at[number])

    def act(number, block, panel_ref):
        shrunk = parts[0][number].astype(jnp.float32)
        for part in parts[1:]:
            shrunk = shrunk + part[number].astype(jnp.float32)
        start = panel_ref.shape[1] - width
        delta = lax.dot_general(
            shrunk.astype(jnp.bfloat16),
            panel_ref[:, start : start + width],
            (((0,), (0,)), ((), ())),
            preferred_element_type=jnp.float32,
        )
        rows = pl.ds(pl.multiple_of(block * block_rows, block_rows), block_rows)
        row = lax.broadcasted_iota(jnp.int32, delta.shape, 0)
        value = mine_ref[rows, :] + far_ref[rows, :].astype(jnp.float32) + ADAPTER_SCALE * delta
        value = jnp.where(row < plan_ref[live_row + number], value, 0.0)
        held_ref[number] = value.astype(held_ref.dtype)
        copy_of(number, block).start()

    each_block(phases, choose, plan_ref, refs[part_count + 2 :], act)
    number = 0
    for row, count, _ in phases:
        for k in range(count):
            copy_of(number, plan_ref[row + k]).wait()
            number += 1


def combine(plan, live_row, parts, base, phases, choose, out=None, cost=None):
    block_rows = parts[0].shape[2]
    rows, width = base[0].shape
    shapes, panels = split_phases(phases)
    total = sum(count for _, count, _ in phases)
    operands = [*parts, *base, *panels]
    specs = [VMEM] * len(operands)
    aliases = {}
    if out is not None:
        specs.append(ANY)
        operands.append(out)
        aliases = {len(operands): 0}
    return pl.pallas_call(
        functools.partial(combine_kernel, shapes, choose, len(parts), live_row),
        in_specs=[SMEM] + specs,
        out_specs=ANY,
        out_shape=pltpu.HBM((rows, width), jnp.bfloat16),
        input_output_aliases=aliases,
        scratch_shapes=[
            pltpu.VMEM((total, block_rows, width), jnp.bfloat16),
            pltpu.SemaphoreType.DMA((total,)),
        ],
        compiler_params=PARAMS,
        cost_estimate=cost or NO_COST,
    )(plan, *operands)


def on_line_of_four(tokens, weight, row_blocks, down, up, names, table, live, capacity):
    def across(value, pairs):
        return lax.ppermute(value, "pool", pairs)

    others = [swap(names, "pool", m) for m in range(1, 4)]
    inner_down = across(down, [(1, 2), (2, 1)])
    inner_up = across(up, [(1, 2), (2, 1)])
    sent, kept = base_parts(tokens, weight, up.shape[2])
    plan = make_plan(names, others, table, live, down.shape[0], capacity, [inner_up])
    held = in_hbm(down), in_hbm(up)
    (near_out,) = pack_panels(plan, [NEAR * capacity], capacity, *held, sent[-1:])
    near = across(near_out, [(0, 1), (1, 0), (2, 3), (3, 2)])
    outer_out, inner_out = pack_panels(
        plan, [TO_OUTER * capacity, TO_INNER * capacity], capacity, *held, [near_out]
    )
    to_outer = across(outer_out, [(0, 3), (3, 0)])
    to_inner = across(inner_out, [(0, 2), (3, 1)])
    choose = INNER * capacity
    first = [(0, capacity, [(down, OWN * capacity)]), (capacity, capacity, [(near, None)])]
    first_up = [(0, capacity, [(up, OWN * capacity)]), first[1]]
    base = base_sum(sent, kept)
    (forward_out,) = pack_panels(
        plan, [FORWARD * capacity], capacity, inner_down, inner_up, [base[0]], LONG
    )
    forwarded = across(forward_out, [(1, 0), (2, 3)])
    middle = [(2 * capacity, capacity, [(inner_down, ACROSS * capacity), (to_outer, None)])]
    middle_up = [(2 * capacity, capacity, [(inner_up, ACROSS * capacity), (to_outer, None)])]
    last = [(3 * capacity, capacity, [(to_inner, None), (forwarded, None)])]

    def write(number, parts, phases, out, cost=None):
        live_row = (LIVE + number) * capacity
        return combine(plan, live_row, parts, base, phases, choose, out, cost)

    first_parts = exchange(shrink(plan, row_blocks, first, choose, [forward_out]))
    out = write(0, first_parts, first_up, None, MIDDLE)
    middle_part = shrink(plan, row_blocks, middle, choose, [in_hbm(out)])
    middle_parts = exchange(middle_part)
    last_parts = exchange(shrink(plan, row_blocks, last, choose, [middle_part], jnp.bfloat16))
    out = write(2, middle_parts, middle_up, out)
    return write(3, last_parts, last, out)


def on_any_pool(tokens, weight, row_blocks, down, up, names, table, live, capacity):
    pool_size = lax.axis_size("pool")
    here = lax.axis_index("pool")
    holder_slots = down.shape[0]
    asked = table[lax.all_gather(names[0], "pool")]
    count = jnp.arange(capacity, dtype=jnp.int32)
    arrived = []
    for distance in range(pool_size):
        slots = asked[lax.rem(here + distance, pool_size)]
        hit = slots // holder_slots == here
        chosen = hit[None, :] & (jnp.cumsum(hit.astype(jnp.int32))[None, :] == 1 + count[:, None])
        plan = jnp.sum(jnp.where(chosen, (slots % holder_slots)[None, :], 0), axis=1)
        (panels,) = pack_panels(plan, [0], capacity, down, up)
        pairs = [(i, (i + distance) % pool_size) for i in range(pool_size)]
        arrived.append(lax.ppermute(panels, "pool", pairs) if distance else panels)
    arrived = jnp.concatenate(arrived)
    owners = asked[here] // holder_slots
    blocks = jnp.arange(owners.shape[0], dtype=jnp.int32)
    earlier = (owners[:, None] == owners[None, :]) & (blocks[:, None] > blocks[None, :])
    ranks = jnp.sum(earlier.astype(jnp.int32), axis=1)
    places = lax.rem(here - owners + pool_size, pool_size) * capacity + ranks
    plan = jnp.concatenate([blocks, places, live[0]])
    base = base_sum(*base_parts(tokens, weight, up.shape[2]))
    phases = [(0, blocks.shape[0], [(arrived, blocks.shape[0])])]
    parts = exchange(shrink(plan, row_blocks, phases, 0))
    live_row = 2 * blocks.shape[0]
    return combine(plan, live_row, parts, base, phases, 0)


def on_device(
    tokens,
    value_weight,
    adapter_down_weight,
    adapter_up_weight,
    adapter_of_block,
    adapter_pool_slot,
    live_block_tokens,
):
    pool_size = lax.axis_size("pool")
    blocks = adapter_of_block.shape[1]
    capacity = -(-blocks // pool_size)
    row_blocks = tokens.reshape(blocks, tokens.shape[0] // blocks, tokens.shape[1])
    line = pool_size == 4 and blocks == capacity * pool_size
    route = on_line_of_four if line else on_any_pool
    return route(
        tokens,
        value_weight,
        row_blocks,
        jnp.transpose(adapter_down_weight, (0, 2, 1)),
        adapter_up_weight,
        adapter_of_block,
        adapter_pool_slot,
        live_block_tokens,
        capacity,
    )


def solution(mesh):
    return jax.shard_map(
        on_device,
        mesh=mesh,
        in_specs=(
            P(("groups", "pool"), "tensor"),
            P("tensor", None),
            P(("groups", "pool"), "tensor", None),
            P(("groups", "pool"), None, "tensor"),
            P(("groups", "pool"), None),
            P("groups"),
            P(("groups", "pool"), None),
        ),
        out_specs=P(("groups", "pool"), "tensor"),
        check_vma=False,
    )
```

```python
import functools

import jax
import jax.numpy as jnp
from jax import lax
from jax.experimental import pallas as pl
from jax.experimental.pallas import tpu as pltpu
from jax.sharding import PartitionSpec as P

ADAPTER_SCALE = 0.5
ROW_TILE = 256
PARAMS = pltpu.CompilerParams(vmem_limit_bytes=20 * 1024 * 1024)
NO_COST = pl.CostEstimate(flops=0, bytes_accessed=0, transcendentals=0)
BASE = pl.CostEstimate(flops=4 * 10**9, bytes_accessed=0, transcendentals=0)
SHORT = pl.CostEstimate(flops=10 * 10**9, bytes_accessed=0, transcendentals=0)
MIDDLE = pl.CostEstimate(flops=0 * 10**9, bytes_accessed=0, transcendentals=0)
LONG = pl.CostEstimate(flops=6 * 10**9, bytes_accessed=0, transcendentals=0)
ANY = pl.BlockSpec(memory_space=pl.ANY)
SMEM = pl.BlockSpec(memory_space=pltpu.SMEM)
VMEM = pl.BlockSpec(memory_space=pltpu.VMEM)


def in_hbm(value):
    return pltpu.with_memory_space_constraint(value, pltpu.HBM)


def swap(value, axis, distance):
    pairs = [(i, i ^ distance) for i in range(lax.axis_size(axis))]
    return lax.ppermute(value, axis, pairs)


def run_copies(copies):
    for copy in copies:
        copy.start()
    return copies


def piece_rows(rows):
    large = rows * 3 // 8
    return [large, large, rows - 2 * large]


def base_kernel(order, tokens_ref, weight_ref, *refs):
    *sent_refs, kept_ref, tokens, weight, sems = refs
    half, rows, width = kept_ref.shape
    parts = sems.shape[1]
    tile, slab = rows // parts, weight.shape[0] // parts
    place = lax.axis_index("tensor")

    def copy_of(number, source, held, size, i):
        span = pl.ds(i * size, size)
        return pltpu.make_async_copy(source.at[span], held.at[span], sems.at[number, i])

    token_copies = [copy_of(0, tokens_ref, tokens, tile, i) for i in range(parts)]
    weight_copies = [copy_of(1, weight_ref, weight, slab, i) for i in range(parts)]

    def add(first, low, high, fresh):
        for number, offset in enumerate(order):
            columns = pl.ds(pl.multiple_of((place ^ offset) * width, width), width)
            part = jnp.dot(
                tokens[first : first + tile, low:high],
                weight[low:high, columns],
                preferred_element_type=jnp.float32,
            )
            if number >= half:
                targets = [(kept_ref, number - half, first, 0, tile)]
            else:
                targets, start = [], 0
                for sent_ref in sent_refs:
                    stop = start + sent_ref.shape[1]
                    above, below = max(first, start), min(first + tile, stop)
                    if above < below:
                        targets.append(
                            (sent_ref, number, above - start, above - first, below - above)
                        )
                    start = stop
            for ref, index, at, source, size in targets:
                value = part[source : source + size]
                if not fresh:
                    value = value + ref[index, at : at + size, :]
                ref[index, at : at + size, :] = value

    run_copies([token_copies[0], *weight_copies])
    token_copies[0].wait()
    for i, copy in enumerate(weight_copies):
        copy.wait()
        if i == 0:
            run_copies(token_copies[1:])
        add(0, i * slab, (i + 1) * slab, i == 0)
    for i in range(1, parts):
        token_copies[i].wait()
        add(i * tile, 0, weight.shape[0], True)


def base_chunks(tokens, weight, order, width):
    rows = tokens.shape[0]
    half = len(order) // 2
    sizes = [*piece_rows(rows), rows]
    *sent, kept = pl.pallas_call(
        functools.partial(base_kernel, order),
        in_specs=[ANY] * 2,
        out_specs=[VMEM] * len(sizes),
        out_shape=[jax.ShapeDtypeStruct((half, size, width), jnp.float32) for size in sizes],
        scratch_shapes=[
            pltpu.VMEM(tokens.shape, tokens.dtype),
            pltpu.VMEM(weight.shape, weight.dtype),
            pltpu.SemaphoreType.DMA((2, 4)),
        ],
        compiler_params=PARAMS,
        cost_estimate=BASE,
    )(in_hbm(tokens), in_hbm(weight))
    return sent, kept


def add_kernel(kept_ref, *refs):
    *arrived_refs, out_ref, mine_ref = refs
    half = kept_ref.shape[0] // 2
    start = 0
    for arrived_ref in arrived_refs:
        rows = pl.ds(start, arrived_ref.shape[1])
        for i in range(half):
            mine_ref[i, rows, :] = kept_ref[i, rows, :] + arrived_ref[i]
            out = kept_ref[half + i, rows, :] + arrived_ref[half + i]
            out_ref[i, rows, :] = out.astype(out_ref.dtype)
        start += arrived_ref.shape[1]


def add_halves(kept, arrived, sent_type):
    count, rows, width = kept.shape
    shape = (count // 2, rows, width)
    return pl.pallas_call(
        add_kernel,
        in_specs=[VMEM] * (1 + len(arrived)),
        out_shape=[
            jax.ShapeDtypeStruct(shape, sent_type),
            jax.ShapeDtypeStruct(shape, jnp.float32),
        ],
        compiler_params=PARAMS,
        cost_estimate=NO_COST,
    )(kept, *arrived)


def base_parts(tokens, weight, width):
    size = lax.axis_size("tensor")
    kept_order = [k for k in range(size) if not k & 1]
    kept_order.sort(key=lambda k: [k >> bit & 1 for bit in range(1, size.bit_length())])
    return base_chunks(tokens, weight, [k ^ 1 for k in kept_order] + kept_order, width)


def base_sum(sent, kept):
    arrived = [swap(piece, "tensor", 1) for piece in sent]
    distance = 2
    size = lax.axis_size("tensor")
    while distance < size:
        sent_type = jnp.bfloat16 if 2 * distance == size else jnp.float32
        sent, kept = add_halves(kept, arrived, sent_type)
        arrived = [swap(sent, "tensor", distance)]
        distance *= 2
    return kept[0], arrived[0][0]


def pick(names_ref, table_ref, holder, holder_slots, count):
    blocks = [jnp.int32(0)] * count
    slots = [jnp.int32(0)] * count
    seen = jnp.int32(0)
    for j in range(names_ref.shape[1]):
        slot = table_ref[names_ref[0, j]]
        hit = lax.div(slot, jnp.int32(holder_slots)) == holder
        for k in range(count):
            chosen = hit & (seen == k)
            blocks[k] = jnp.where(chosen, jnp.int32(j), blocks[k])
            slots[k] = jnp.where(chosen, lax.rem(slot, jnp.int32(holder_slots)), slots[k])
        seen = seen + hit.astype(jnp.int32)
    return blocks, slots


def panel_copies(k, slot, down_ref, up_ref, out_ref, sems):
    depth = down_ref.shape[2]
    width = up_ref.shape[2]
    return [
        pltpu.make_async_copy(down_ref.at[slot], out_ref.at[k, :, pl.ds(0, depth)], sems.at[k, 0]),
        pltpu.make_async_copy(up_ref.at[slot], out_ref.at[k, :, pl.ds(depth, width)], sems.at[k, 1]),
    ]


def plan_kernel(capacity, holder_slots, *refs):
    sources, plan_ref, scalars, sems = refs[:6], refs[-8], refs[-7:-1], refs[-1]
    loads = [
        pltpu.make_async_copy(source, scalar, sems.at[i])
        for i, (source, scalar) in enumerate(zip(sources, scalars))
    ]
    for load in run_copies(loads):
        load.wait()
    names_ref, first_ref, second_ref, third_ref, table_ref, live_ref = scalars
    here = lax.axis_index("pool")
    find = functools.partial(
        pick, table_ref=table_ref, holder_slots=holder_slots, count=capacity
    )
    inner = (here == 1) | (here == 2)
    own = find(names_ref, holder=here)
    near = find(names_ref, holder=here ^ 1)
    across = find(names_ref, holder=here ^ 3)
    late = find(names_ref, holder=here ^ 2)
    rows = [
        own[0],
        near[0],
        across[0],
        late[0],
        own[1],
        across[1],
        find(first_ref, holder=here)[1],
        find(second_ref, holder=here)[1],
        find(third_ref, holder=here)[1],
        find(first_ref, holder=here ^ 3)[1],
        [inner.astype(jnp.int32)] * capacity,
        *[[live_ref[0, block] for block in phase[0]] for phase in (own, near, across, late)],
    ]
    for number, row in enumerate(rows):
        for k in range(capacity):
            plan_ref[number * capacity + k] = row[k]


OWN, ACROSS, NEAR, TO_INNER, TO_OUTER, FORWARD, INNER, LIVE, PLAN_ROWS = 4, 5, 6, 7, 8, 9, 10, 11, 15


def make_plan(names, others, table, live, holder_slots, capacity, after):
    return pl.pallas_call(
        functools.partial(plan_kernel, capacity, holder_slots),
        in_specs=[ANY] * (6 + len(after)),
        out_specs=SMEM,
        out_shape=jax.ShapeDtypeStruct((PLAN_ROWS * capacity,), jnp.int32),
        scratch_shapes=[pltpu.SMEM(names.shape, jnp.int32)] * 4
        + [pltpu.SMEM(table.shape, jnp.int32), pltpu.SMEM(live.shape, jnp.int32)]
        + [pltpu.SemaphoreType.DMA((6,))],
        compiler_params=PARAMS,
        cost_estimate=SHORT,
    )(in_hbm(names), *others, in_hbm(table), in_hbm(live), *after)


def pack_kernel(starts, choose, capacity, plan_ref, *refs):
    out_ref, sems = refs[-2:]

    def run(start, down_ref, up_ref):
        copies = []
        for k in range(capacity):
            slot = plan_ref[start + k]
            copies += run_copies(panel_copies(k, slot, down_ref, up_ref, out_ref, sems))
        for copy in copies:
            copy.wait()

    if len(starts) == 1:
        run(starts[0], *refs[:2])
    else:
        first = plan_ref[choose] != 0
        pl.when(first)(functools.partial(run, starts[0], *refs[:2]))
        pl.when(jnp.logical_not(first))(functools.partial(run, starts[1], *refs[2:4]))


def pack_panels(plan, choices, choose, capacity, after=(), cost=None):
    sources = [a for _, *pair in choices for a in pair]
    rank, depth = sources[0].shape[1:]
    width = sources[1].shape[2]
    return pl.pallas_call(
        functools.partial(pack_kernel, [start for start, *_ in choices], choose, capacity),
        in_specs=[SMEM] + [ANY] * (len(sources) + len(after)),
        out_specs=ANY,
        out_shape=jax.ShapeDtypeStruct((capacity, rank, depth + width), sources[0].dtype),
        scratch_shapes=[pltpu.SemaphoreType.DMA((capacity, 2))],
        compiler_params=PARAMS,
        cost_estimate=cost or NO_COST,
    )(plan, *sources, *after)


def each_block(phases, choose, plan_ref, refs, act):
    number = 0
    for row, count, rows in phases:
        mine, refs = refs[: len(rows)], refs[len(rows) :]

        def run(ref, row_of, number=number, row=row, count=count):
            for k in range(count):
                panel = ref.at[k if row_of is None else plan_ref[row_of + k]]
                act(number + k, plan_ref[row + k], panel)

        if len(rows) == 1:
            run(mine[0], rows[0])
        else:
            first = plan_ref[choose] != 0
            pl.when(first)(functools.partial(run, mine[0], rows[0]))
            pl.when(jnp.logical_not(first))(functools.partial(run, mine[1], rows[1]))
        number += count


def split_phases(phases):
    shapes = [(row, count, [source[1] for source in sources]) for row, count, sources in phases]
    return shapes, [source[0] for _, _, sources in phases for source in sources]


def shrink_kernel(phases, choose, plan_ref, token_ref, *refs):
    out_ref = refs[-1]
    depth = token_ref.shape[2]

    def act(number, block, panel_ref):
        out_ref[number] = lax.dot_general(
            panel_ref[:, :depth],
            token_ref[block],
            (((1,), (1,)), ((), ())),
            preferred_element_type=jnp.float32,
        ).astype(out_ref.dtype)

    each_block(phases, choose, plan_ref, refs, act)


def shrink(plan, row_blocks, phases, choose, after=(), kind=jnp.float32, cost=None):
    shapes, panels = split_phases(phases)
    total = sum(count for _, count, _ in phases)
    shape = (total, panels[0].shape[1], row_blocks.shape[1])
    return pl.pallas_call(
        functools.partial(shrink_kernel, shapes, choose),
        in_specs=[SMEM] + [VMEM] * (1 + len(panels)) + [ANY] * len(after),
        out_specs=VMEM,
        out_shape=jax.ShapeDtypeStruct(shape, kind),
        compiler_params=PARAMS,
        cost_estimate=cost or NO_COST,
    )(plan, row_blocks, *panels, *after)


def exchange(part):
    return [part] + [swap(part, "tensor", m) for m in range(1, lax.axis_size("tensor"))]


def combine_kernel(phases, choose, part_count, live_row, plan_ref, *refs):
    parts = refs[:part_count]
    mine_ref, far_ref = refs[part_count : part_count + 2]
    out_ref, held_ref, sems = refs[-3:]
    total, block_rows, width = held_ref.shape

    def copy_of(number, block):
        rows = pl.ds(pl.multiple_of(block * block_rows, block_rows), block_rows)
        return pltpu.make_async_copy(held_ref.at[number], out_ref.at[rows], sems.at[number])

    def act(number, block, panel_ref):
        shrunk = parts[0][number].astype(jnp.float32)
        for part in parts[1:]:
            shrunk = shrunk + part[number].astype(jnp.float32)
        start = panel_ref.shape[1] - width
        delta = lax.dot_general(
            shrunk.astype(jnp.bfloat16),
            panel_ref[:, start : start + width],
            (((0,), (0,)), ((), ())),
            preferred_element_type=jnp.float32,
        )
        rows = pl.ds(pl.multiple_of(block * block_rows, block_rows), block_rows)
        row = lax.broadcasted_iota(jnp.int32, delta.shape, 0)
        value = mine_ref[rows, :] + far_ref[rows, :].astype(jnp.float32) + ADAPTER_SCALE * delta
        value = jnp.where(row < plan_ref[live_row + number], value, 0.0)
        held_ref[number] = value.astype(held_ref.dtype)
        copy_of(number, block).start()

    each_block(phases, choose, plan_ref, refs[part_count + 2 :], act)
    number = 0
    for row, count, _ in phases:
        for k in range(count):
            copy_of(number, plan_ref[row + k]).wait()
            number += 1


def combine(plan, live_row, parts, base, phases, choose, out=None, cost=None):
    block_rows = parts[0].shape[2]
    rows, width = base[0].shape
    shapes, panels = split_phases(phases)
    total = sum(count for _, count, _ in phases)
    operands = [*parts, *base, *panels]
    specs = [VMEM] * len(operands)
    aliases = {}
    if out is not None:
        specs.append(ANY)
        operands.append(out)
        aliases = {len(operands): 0}
    return pl.pallas_call(
        functools.partial(combine_kernel, shapes, choose, len(parts), live_row),
        in_specs=[SMEM] + specs,
        out_specs=ANY,
        out_shape=pltpu.HBM((rows, width), jnp.bfloat16),
        input_output_aliases=aliases,
        scratch_shapes=[
            pltpu.VMEM((total, block_rows, width), jnp.bfloat16),
            pltpu.SemaphoreType.DMA((total,)),
        ],
        compiler_params=PARAMS,
        cost_estimate=cost or NO_COST,
    )(plan, *operands)


def on_line_of_four(tokens, weight, row_blocks, down, up, names, table, live, capacity):
    def across(value, pairs):
        return lax.ppermute(value, "pool", pairs)

    others = [swap(names, "pool", m) for m in range(1, 4)]
    inner_up = across(up, [(0, 0), (1, 2), (2, 1), (3, 3)])
    inner_down = across(down, [(0, 0), (1, 2), (2, 1), (3, 3)])
    sent, kept = base_parts(tokens, weight, up.shape[2])
    plan = make_plan(names, others, table, live, down.shape[0], capacity, [inner_up])
    choose = INNER * capacity
    held = in_hbm(down), in_hbm(up)

    def pack(choices, after, cost=None):
        choices = [(row * capacity, *panels) for row, *panels in choices]
        return pack_panels(plan, choices, choose, capacity, after, cost)

    near_out = pack([(NEAR, *held)], sent[-1:])
    near = across(near_out, [(0, 1), (1, 0), (2, 3), (3, 2)])
    outer_out = pack([(TO_OUTER, *held)], [near_out])
    to_outer = across(outer_out, [(0, 3), (1, 1), (2, 2), (3, 0)])
    base = base_sum(sent, kept)
    late_out = pack(
        [(FORWARD, inner_down, inner_up), (TO_INNER, *held)], [base[0], outer_out], LONG
    )
    late = across(late_out, [(0, 2), (1, 0), (2, 3), (3, 1)])

    first = [(0, capacity, [(down, OWN * capacity)]), (capacity, capacity, [(near, None)])]
    first_up = [(0, capacity, [(up, OWN * capacity)]), first[1]]
    middle = [(2 * capacity, capacity, [(inner_down, ACROSS * capacity), (to_outer, None)])]
    middle_up = [(2 * capacity, capacity, [(inner_up, ACROSS * capacity), (to_outer, None)])]
    last = [(3 * capacity, capacity, [(late, None)])]

    def write(number, parts, phases, out, cost=None):
        live_row = (LIVE + number) * capacity
        return combine(plan, live_row, parts, base, phases, choose, out, cost)

    first_parts = exchange(shrink(plan, row_blocks, first, choose, [late_out]))
    out = write(0, first_parts, first_up, None, MIDDLE)
    middle_part = shrink(plan, row_blocks, middle, choose, [in_hbm(out)])
    middle_parts = exchange(middle_part)
    last_parts = exchange(shrink(plan, row_blocks, last, choose, [middle_part], jnp.bfloat16))
    out = write(2, middle_parts, middle_up, out)
    return write(3, last_parts, last, out)


def on_any_pool(tokens, weight, row_blocks, down, up, names, table, live, capacity):
    pool_size = lax.axis_size("pool")
    here = lax.axis_index("pool")
    holder_slots = down.shape[0]
    asked = table[lax.all_gather(names[0], "pool")]
    count = jnp.arange(capacity, dtype=jnp.int32)
    arrived = []
    for distance in range(pool_size):
        slots = asked[lax.rem(here + distance, pool_size)]
        hit = slots // holder_slots == here
        chosen = hit[None, :] & (jnp.cumsum(hit.astype(jnp.int32))[None, :] == 1 + count[:, None])
        plan = jnp.sum(jnp.where(chosen, (slots % holder_slots)[None, :], 0), axis=1)
        panels = pack_panels(plan, [(0, down, up)], 0, capacity)
        pairs = [(i, (i + distance) % pool_size) for i in range(pool_size)]
        arrived.append(lax.ppermute(panels, "pool", pairs) if distance else panels)
    arrived = jnp.concatenate(arrived)
    owners = asked[here] // holder_slots
    blocks = jnp.arange(owners.shape[0], dtype=jnp.int32)
    earlier = (owners[:, None] == owners[None, :]) & (blocks[:, None] > blocks[None, :])
    ranks = jnp.sum(earlier.astype(jnp.int32), axis=1)
    places = lax.rem(here - owners + pool_size, pool_size) * capacity + ranks
    plan = jnp.concatenate([blocks, places, live[0]])
    base = base_sum(*base_parts(tokens, weight, up.shape[2]))
    phases = [(0, blocks.shape[0], [(arrived, blocks.shape[0])])]
    parts = exchange(shrink(plan, row_blocks, phases, 0))
    live_row = 2 * blocks.shape[0]
    return combine(plan, live_row, parts, base, phases, 0)


def on_device(
    tokens,
    value_weight,
    adapter_down_weight,
    adapter_up_weight,
    adapter_of_block,
    adapter_pool_slot,
    live_block_tokens,
):
    pool_size = lax.axis_size("pool")
    blocks = adapter_of_block.shape[1]
    capacity = -(-blocks // pool_size)
    row_blocks = tokens.reshape(blocks, tokens.shape[0] // blocks, tokens.shape[1])
    line = pool_size == 4 and blocks == capacity * pool_size
    route = on_line_of_four if line else on_any_pool
    return route(
        tokens,
        value_weight,
        row_blocks,
        jnp.transpose(adapter_down_weight, (0, 2, 1)),
        adapter_up_weight,
        adapter_of_block,
        adapter_pool_slot,
        live_block_tokens,
        capacity,
    )


def solution(mesh):
    return jax.shard_map(
        on_device,
        mesh=mesh,
        in_specs=(
            P(("groups", "pool"), "tensor"),
            P("tensor", None),
            P(("groups", "pool"), "tensor", None),
            P(("groups", "pool"), None, "tensor"),
            P(("groups", "pool"), None),
            P("groups"),
            P(("groups", "pool"), None),
        ),
        out_specs=P(("groups", "pool"), "tensor"),
        check_vma=False,
    )
```

```python
import functools

import jax
import jax.numpy as jnp
from jax import lax
from jax.experimental import pallas as pl
from jax.experimental.pallas import tpu as pltpu
from jax.sharding import PartitionSpec as P

ADAPTER_SCALE = 0.5
ROW_TILE = 256
PARAMS = pltpu.CompilerParams(vmem_limit_bytes=20 * 1024 * 1024)
NO_COST = pl.CostEstimate(flops=0, bytes_accessed=0, transcendentals=0)
BASE = pl.CostEstimate(flops=4 * 10**9, bytes_accessed=0, transcendentals=0)
SHORT = pl.CostEstimate(flops=10 * 10**9, bytes_accessed=0, transcendentals=0)
MIDDLE = pl.CostEstimate(flops=0 * 10**9, bytes_accessed=0, transcendentals=0)
LONG = pl.CostEstimate(flops=6 * 10**9, bytes_accessed=0, transcendentals=0)
ANY = pl.BlockSpec(memory_space=pl.ANY)
SMEM = pl.BlockSpec(memory_space=pltpu.SMEM)
VMEM = pl.BlockSpec(memory_space=pltpu.VMEM)


def in_hbm(value):
    return pltpu.with_memory_space_constraint(value, pltpu.HBM)


def swap(value, axis, distance):
    pairs = [(i, i ^ distance) for i in range(lax.axis_size(axis))]
    return lax.ppermute(value, axis, pairs)


def run_copies(copies):
    for copy in copies:
        copy.start()
    return copies


def piece_rows(rows):
    large = rows * 3 // 8
    return [large, large, rows - 2 * large]


def base_kernel(order, tokens_ref, weight_ref, *refs):
    *sent_refs, kept_ref, tokens, weight, sems = refs
    half, rows, width = kept_ref.shape
    parts = sems.shape[1]
    tile, slab = rows // parts, weight.shape[0] // parts
    place = lax.axis_index("tensor")

    def copy_of(number, source, held, size, i):
        span = pl.ds(i * size, size)
        return pltpu.make_async_copy(source.at[span], held.at[span], sems.at[number, i])

    token_copies = [copy_of(0, tokens_ref, tokens, tile, i) for i in range(parts)]
    weight_copies = [copy_of(1, weight_ref, weight, slab, i) for i in range(parts)]

    def add(first, low, high, fresh):
        for number, offset in enumerate(order):
            columns = pl.ds(pl.multiple_of((place ^ offset) * width, width), width)
            part = jnp.dot(
                tokens[first : first + tile, low:high],
                weight[low:high, columns],
                preferred_element_type=jnp.float32,
            )
            if number >= half:
                targets = [(kept_ref, number - half, first, 0, tile)]
            else:
                targets, start = [], 0
                for sent_ref in sent_refs:
                    stop = start + sent_ref.shape[1]
                    above, below = max(first, start), min(first + tile, stop)
                    if above < below:
                        targets.append(
                            (sent_ref, number, above - start, above - first, below - above)
                        )
                    start = stop
            for ref, index, at, source, size in targets:
                value = part[source : source + size]
                if not fresh:
                    value = value + ref[index, at : at + size, :]
                ref[index, at : at + size, :] = value

    run_copies([token_copies[0], *weight_copies])
    token_copies[0].wait()
    for i, copy in enumerate(weight_copies):
        copy.wait()
        if i == 0:
            run_copies(token_copies[1:])
        add(0, i * slab, (i + 1) * slab, i == 0)
    for i in range(1, parts):
        token_copies[i].wait()
        add(i * tile, 0, weight.shape[0], True)


def base_chunks(tokens, weight, order, width):
    rows = tokens.shape[0]
    half = len(order) // 2
    sizes = [*piece_rows(rows), rows]
    *sent, kept = pl.pallas_call(
        functools.partial(base_kernel, order),
        in_specs=[ANY] * 2,
        out_specs=[VMEM] * len(sizes),
        out_shape=[jax.ShapeDtypeStruct((half, size, width), jnp.float32) for size in sizes],
        scratch_shapes=[
            pltpu.VMEM(tokens.shape, tokens.dtype),
            pltpu.VMEM(weight.shape, weight.dtype),
            pltpu.SemaphoreType.DMA((2, 4)),
        ],
        compiler_params=PARAMS,
        cost_estimate=BASE,
    )(in_hbm(tokens), in_hbm(weight))
    return sent, kept


def add_kernel(kept_ref, *refs):
    *arrived_refs, out_ref, mine_ref = refs
    half = kept_ref.shape[0] // 2
    start = 0
    for arrived_ref in arrived_refs:
        rows = pl.ds(start, arrived_ref.shape[1])
        for i in range(half):
            mine_ref[i, rows, :] = kept_ref[i, rows, :] + arrived_ref[i]
            out = kept_ref[half + i, rows, :] + arrived_ref[half + i]
            out_ref[i, rows, :] = out.astype(out_ref.dtype)
        start += arrived_ref.shape[1]


def add_halves(kept, arrived, sent_type):
    count, rows, width = kept.shape
    shape = (count // 2, rows, width)
    return pl.pallas_call(
        add_kernel,
        in_specs=[VMEM] * (1 + len(arrived)),
        out_shape=[
            jax.ShapeDtypeStruct(shape, sent_type),
            jax.ShapeDtypeStruct(shape, jnp.float32),
        ],
        compiler_params=PARAMS,
        cost_estimate=NO_COST,
    )(kept, *arrived)


def base_parts(tokens, weight, width):
    size = lax.axis_size("tensor")
    kept_order = [k for k in range(size) if not k & 1]
    kept_order.sort(key=lambda k: [k >> bit & 1 for bit in range(1, size.bit_length())])
    return base_chunks(tokens, weight, [k ^ 1 for k in kept_order] + kept_order, width)


def base_sum(sent, kept):
    arrived = [swap(piece, "tensor", 1) for piece in sent]
    distance = 2
    size = lax.axis_size("tensor")
    while distance < size:
        sent_type = jnp.bfloat16 if 2 * distance == size else jnp.float32
        sent, kept = add_halves(kept, arrived, sent_type)
        arrived = [swap(sent, "tensor", distance)]
        distance *= 2
    return kept[0], arrived[0][0]


def pick(names_ref, table_ref, holder, holder_slots, count):
    blocks = [jnp.int32(0)] * count
    slots = [jnp.int32(0)] * count
    seen = jnp.int32(0)
    for j in range(names_ref.shape[1]):
        slot = table_ref[names_ref[0, j]]
        hit = lax.div(slot, jnp.int32(holder_slots)) == holder
        for k in range(count):
            chosen = hit & (seen == k)
            blocks[k] = jnp.where(chosen, jnp.int32(j), blocks[k])
            slots[k] = jnp.where(chosen, lax.rem(slot, jnp.int32(holder_slots)), slots[k])
        seen = seen + hit.astype(jnp.int32)
    return blocks, slots


def panel_copies(k, slot, down_ref, up_ref, out_ref, sems):
    depth = down_ref.shape[2]
    width = up_ref.shape[2]
    return [
        pltpu.make_async_copy(down_ref.at[slot], out_ref.at[k, :, pl.ds(0, depth)], sems.at[k, 0]),
        pltpu.make_async_copy(up_ref.at[slot], out_ref.at[k, :, pl.ds(depth, width)], sems.at[k, 1]),
    ]


def plan_kernel(capacity, *refs):
    sources, down_ref, up_ref = refs[:6], *refs[6:8]
    near_ref, plan_ref, *scalars, scalar_sems, sems = refs[-10:]
    holder_slots = down_ref.shape[0]
    loads = [
        pltpu.make_async_copy(source, scalar, scalar_sems.at[i])
        for i, (source, scalar) in enumerate(zip(sources, scalars))
    ]
    for load in run_copies(loads):
        load.wait()
    names_ref, first_ref, second_ref, third_ref, table_ref, live_ref = scalars
    here = lax.axis_index("pool")
    find = functools.partial(
        pick, table_ref=table_ref, holder_slots=holder_slots, count=capacity
    )
    near_slots = find(first_ref, holder=here)[1]
    copies = []
    for k, slot in enumerate(near_slots):
        copies += run_copies(panel_copies(k, slot, down_ref, up_ref, near_ref, sems))
    inner = (here == 1) | (here == 2)
    own = find(names_ref, holder=here)
    near = find(names_ref, holder=here ^ 1)
    across = find(names_ref, holder=here ^ 3)
    late = find(names_ref, holder=here ^ 2)
    rows = [
        own[0],
        near[0],
        across[0],
        late[0],
        own[1],
        across[1],
        find(second_ref, holder=here)[1],
        find(third_ref, holder=here)[1],
        find(first_ref, holder=here ^ 3)[1],
        [inner.astype(jnp.int32)] * capacity,
        *[[live_ref[0, block] for block in phase[0]] for phase in (own, near, across, late)],
    ]
    for number, row in enumerate(rows):
        for k in range(capacity):
            plan_ref[number * capacity + k] = row[k]
    for copy in copies:
        copy.wait()


OWN, ACROSS, TO_INNER, TO_OUTER, FORWARD, INNER, LIVE, PLAN_ROWS = 4, 5, 6, 7, 8, 9, 10, 14


def make_plan(names, others, table, live, down, up, capacity, after):
    rank, depth = down.shape[1:]
    return pl.pallas_call(
        functools.partial(plan_kernel, capacity),
        in_specs=[ANY] * (8 + len(after)),
        out_specs=[ANY, SMEM],
        out_shape=[
            jax.ShapeDtypeStruct((capacity, rank, depth + up.shape[2]), down.dtype),
            jax.ShapeDtypeStruct((PLAN_ROWS * capacity,), jnp.int32),
        ],
        scratch_shapes=[pltpu.SMEM(names.shape, jnp.int32)] * 4
        + [pltpu.SMEM(table.shape, jnp.int32), pltpu.SMEM(live.shape, jnp.int32)]
        + [pltpu.SemaphoreType.DMA((6,)), pltpu.SemaphoreType.DMA((capacity, 2))],
        compiler_params=PARAMS,
        cost_estimate=SHORT,
    )(in_hbm(names), *others, in_hbm(table), in_hbm(live), down, up, *after)


def pack_kernel(starts, choose, capacity, plan_ref, *refs):
    out_ref, sems = refs[-2:]

    def run(start, down_ref, up_ref):
        copies = []
        for k in range(capacity):
            slot = plan_ref[start + k]
            copies += run_copies(panel_copies(k, slot, down_ref, up_ref, out_ref, sems))
        for copy in copies:
            copy.wait()

    if len(starts) == 1:
        run(starts[0], *refs[:2])
    else:
        first = plan_ref[choose] != 0
        pl.when(first)(functools.partial(run, starts[0], *refs[:2]))
        pl.when(jnp.logical_not(first))(functools.partial(run, starts[1], *refs[2:4]))


def pack_panels(plan, choices, choose, capacity, after=(), cost=None):
    sources = [a for _, *pair in choices for a in pair]
    rank, depth = sources[0].shape[1:]
    width = sources[1].shape[2]
    return pl.pallas_call(
        functools.partial(pack_kernel, [start for start, *_ in choices], choose, capacity),
        in_specs=[SMEM] + [ANY] * (len(sources) + len(after)),
        out_specs=ANY,
        out_shape=jax.ShapeDtypeStruct((capacity, rank, depth + width), sources[0].dtype),
        scratch_shapes=[pltpu.SemaphoreType.DMA((capacity, 2))],
        compiler_params=PARAMS,
        cost_estimate=cost or NO_COST,
    )(plan, *sources, *after)


def each_block(phases, choose, plan_ref, refs, act):
    number = 0
    for row, count, rows in phases:
        mine, refs = refs[: len(rows)], refs[len(rows) :]

        def run(ref, row_of, number=number, row=row, count=count):
            for k in range(count):
                panel = ref.at[k if row_of is None else plan_ref[row_of + k]]
                act(number + k, plan_ref[row + k], panel)

        if len(rows) == 1:
            run(mine[0], rows[0])
        else:
            first = plan_ref[choose] != 0
            pl.when(first)(functools.partial(run, mine[0], rows[0]))
            pl.when(jnp.logical_not(first))(functools.partial(run, mine[1], rows[1]))
        number += count


def split_phases(phases):
    shapes = [(row, count, [source[1] for source in sources]) for row, count, sources in phases]
    return shapes, [source[0] for _, _, sources in phases for source in sources]


def shrink_kernel(phases, choose, plan_ref, token_ref, *refs):
    out_ref = refs[-1]
    depth = token_ref.shape[2]

    def act(number, block, panel_ref):
        out_ref[number] = lax.dot_general(
            panel_ref[:, :depth],
            token_ref[block],
            (((1,), (1,)), ((), ())),
            preferred_element_type=jnp.float32,
        ).astype(out_ref.dtype)

    each_block(phases, choose, plan_ref, refs, act)


def shrink(plan, row_blocks, phases, choose, after=(), kind=jnp.float32, cost=None):
    shapes, panels = split_phases(phases)
    total = sum(count for _, count, _ in phases)
    shape = (total, panels[0].shape[1], row_blocks.shape[1])
    return pl.pallas_call(
        functools.partial(shrink_kernel, shapes, choose),
        in_specs=[SMEM] + [VMEM] * (1 + len(panels)) + [ANY] * len(after),
        out_specs=VMEM,
        out_shape=jax.ShapeDtypeStruct(shape, kind),
        compiler_params=PARAMS,
        cost_estimate=cost or NO_COST,
    )(plan, row_blocks, *panels, *after)


def exchange(part):
    return [part] + [swap(part, "tensor", m) for m in range(1, lax.axis_size("tensor"))]


def combine_kernel(phases, choose, part_count, live_row, plan_ref, *refs):
    parts = refs[:part_count]
    mine_ref, far_ref = refs[part_count : part_count + 2]
    out_ref, held_ref, sems = refs[-3:]
    total, block_rows, width = held_ref.shape

    def copy_of(number, block):
        rows = pl.ds(pl.multiple_of(block * block_rows, block_rows), block_rows)
        return pltpu.make_async_copy(held_ref.at[number], out_ref.at[rows], sems.at[number])

    def act(number, block, panel_ref):
        shrunk = parts[0][number].astype(jnp.float32)
        for part in parts[1:]:
            shrunk = shrunk + part[number].astype(jnp.float32)
        start = panel_ref.shape[1] - width
        delta = lax.dot_general(
            shrunk.astype(jnp.bfloat16),
            panel_ref[:, start : start + width],
            (((0,), (0,)), ((), ())),
            preferred_element_type=jnp.float32,
        )
        rows = pl.ds(pl.multiple_of(block * block_rows, block_rows), block_rows)
        row = lax.broadcasted_iota(jnp.int32, delta.shape, 0)
        value = mine_ref[rows, :] + far_ref[rows, :].astype(jnp.float32) + ADAPTER_SCALE * delta
        value = jnp.where(row < plan_ref[live_row + number], value, 0.0)
        held_ref[number] = value.astype(held_ref.dtype)
        copy_of(number, block).start()

    each_block(phases, choose, plan_ref, refs[part_count + 2 :], act)
    number = 0
    for row, count, _ in phases:
        for k in range(count):
            copy_of(number, plan_ref[row + k]).wait()
            number += 1


def combine(plan, live_row, parts, base, phases, choose, out=None, cost=None):
    block_rows = parts[0].shape[2]
    rows, width = base[0].shape
    shapes, panels = split_phases(phases)
    total = sum(count for _, count, _ in phases)
    operands = [*parts, *base, *panels]
    specs = [VMEM] * len(operands)
    aliases = {}
    if out is not None:
        specs.append(ANY)
        operands.append(out)
        aliases = {len(operands): 0}
    return pl.pallas_call(
        functools.partial(combine_kernel, shapes, choose, len(parts), live_row),
        in_specs=[SMEM] + specs,
        out_specs=ANY,
        out_shape=pltpu.HBM((rows, width), jnp.bfloat16),
        input_output_aliases=aliases,
        scratch_shapes=[
            pltpu.VMEM((total, block_rows, width), jnp.bfloat16),
            pltpu.SemaphoreType.DMA((total,)),
        ],
        compiler_params=PARAMS,
        cost_estimate=cost or NO_COST,
    )(plan, *operands)


def on_line_of_four(tokens, weight, row_blocks, down, up, names, table, live, capacity):
    def across(value, pairs):
        return lax.ppermute(value, "pool", pairs)

    others = [swap(names, "pool", m) for m in range(1, 4)]
    inner_up = across(up, [(0, 0), (1, 2), (2, 1), (3, 3)])
    inner_down = across(down, [(0, 0), (1, 2), (2, 1), (3, 3)])
    sent, kept = base_parts(tokens, weight, up.shape[2])
    choose = INNER * capacity
    held = in_hbm(down), in_hbm(up)
    near_out, plan = make_plan(
        names, others, table, live, *held, capacity, [inner_up, sent[-1]]
    )

    def pack(choices, after, cost=None):
        choices = [(row * capacity, *panels) for row, *panels in choices]
        return pack_panels(plan, choices, choose, capacity, after, cost)

    near = across(near_out, [(0, 1), (1, 0), (2, 3), (3, 2)])
    base = base_sum(sent, kept)
    outer_out = pack([(TO_OUTER, *held)], [base[0]])
    to_outer = across(outer_out, [(0, 3), (1, 1), (2, 2), (3, 0)])
    late_out = pack(
        [(FORWARD, inner_down, inner_up), (TO_INNER, *held)], [outer_out], LONG
    )
    late = across(late_out, [(0, 2), (1, 0), (2, 3), (3, 1)])

    first = [(0, capacity, [(down, OWN * capacity)]), (capacity, capacity, [(near, None)])]
    first_up = [(0, capacity, [(up, OWN * capacity)]), first[1]]
    middle = [(2 * capacity, capacity, [(inner_down, ACROSS * capacity), (to_outer, None)])]
    middle_up = [(2 * capacity, capacity, [(inner_up, ACROSS * capacity), (to_outer, None)])]
    last = [(3 * capacity, capacity, [(late, None)])]

    def write(number, parts, phases, out, cost=None):
        live_row = (LIVE + number) * capacity
        return combine(plan, live_row, parts, base, phases, choose, out, cost)

    first_parts = exchange(shrink(plan, row_blocks, first, choose, [late_out]))
    out = write(0, first_parts, first_up, None, MIDDLE)
    middle_part = shrink(plan, row_blocks, middle, choose, [in_hbm(out)])
    middle_parts = exchange(middle_part)
    last_parts = exchange(shrink(plan, row_blocks, last, choose, [middle_part], jnp.bfloat16))
    out = write(2, middle_parts, middle_up, out)
    return write(3, last_parts, last, out)


def on_any_pool(tokens, weight, row_blocks, down, up, names, table, live, capacity):
    pool_size = lax.axis_size("pool")
    here = lax.axis_index("pool")
    holder_slots = down.shape[0]
    asked = table[lax.all_gather(names[0], "pool")]
    count = jnp.arange(capacity, dtype=jnp.int32)
    arrived = []
    for distance in range(pool_size):
        slots = asked[lax.rem(here + distance, pool_size)]
        hit = slots // holder_slots == here
        chosen = hit[None, :] & (jnp.cumsum(hit.astype(jnp.int32))[None, :] == 1 + count[:, None])
        plan = jnp.sum(jnp.where(chosen, (slots % holder_slots)[None, :], 0), axis=1)
        panels = pack_panels(plan, [(0, down, up)], 0, capacity)
        pairs = [(i, (i + distance) % pool_size) for i in range(pool_size)]
        arrived.append(lax.ppermute(panels, "pool", pairs) if distance else panels)
    arrived = jnp.concatenate(arrived)
    owners = asked[here] // holder_slots
    blocks = jnp.arange(owners.shape[0], dtype=jnp.int32)
    earlier = (owners[:, None] == owners[None, :]) & (blocks[:, None] > blocks[None, :])
    ranks = jnp.sum(earlier.astype(jnp.int32), axis=1)
    places = lax.rem(here - owners + pool_size, pool_size) * capacity + ranks
    plan = jnp.concatenate([blocks, places, live[0]])
    base = base_sum(*base_parts(tokens, weight, up.shape[2]))
    phases = [(0, blocks.shape[0], [(arrived, blocks.shape[0])])]
    parts = exchange(shrink(plan, row_blocks, phases, 0))
    live_row = 2 * blocks.shape[0]
    return combine(plan, live_row, parts, base, phases, 0)


def on_device(
    tokens,
    value_weight,
    adapter_down_weight,
    adapter_up_weight,
    adapter_of_block,
    adapter_pool_slot,
    live_block_tokens,
):
    pool_size = lax.axis_size("pool")
    blocks = adapter_of_block.shape[1]
    capacity = -(-blocks // pool_size)
    row_blocks = tokens.reshape(blocks, tokens.shape[0] // blocks, tokens.shape[1])
    line = pool_size == 4 and blocks == capacity * pool_size
    route = on_line_of_four if line else on_any_pool
    return route(
        tokens,
        value_weight,
        row_blocks,
        jnp.transpose(adapter_down_weight, (0, 2, 1)),
        adapter_up_weight,
        adapter_of_block,
        adapter_pool_slot,
        live_block_tokens,
        capacity,
    )


def solution(mesh):
    return jax.shard_map(
        on_device,
        mesh=mesh,
        in_specs=(
            P(("groups", "pool"), "tensor"),
            P("tensor", None),
            P(("groups", "pool"), "tensor", None),
            P(("groups", "pool"), None, "tensor"),
            P(("groups", "pool"), None),
            P("groups"),
            P(("groups", "pool"), None),
        ),
        out_specs=P(("groups", "pool"), "tensor"),
        check_vma=False,
    )
```

```python
import functools

import jax
import jax.numpy as jnp
from jax import lax
from jax.experimental import pallas as pl
from jax.experimental.pallas import tpu as pltpu
from jax.sharding import PartitionSpec as P

ADAPTER_SCALE = 0.5
ROW_TILE = 256
PARAMS = pltpu.CompilerParams(vmem_limit_bytes=20 * 1024 * 1024)
NO_COST = pl.CostEstimate(flops=0, bytes_accessed=0, transcendentals=0)
BASE = pl.CostEstimate(flops=4 * 10**9, bytes_accessed=0, transcendentals=0)
SHORT = pl.CostEstimate(flops=10 * 10**9, bytes_accessed=0, transcendentals=0)
MIDDLE = pl.CostEstimate(flops=0 * 10**9, bytes_accessed=0, transcendentals=0)
LONG = pl.CostEstimate(flops=6 * 10**9, bytes_accessed=0, transcendentals=0)
ANY = pl.BlockSpec(memory_space=pl.ANY)
SMEM = pl.BlockSpec(memory_space=pltpu.SMEM)
VMEM = pl.BlockSpec(memory_space=pltpu.VMEM)


def in_hbm(value):
    return pltpu.with_memory_space_constraint(value, pltpu.HBM)


def swap(value, axis, distance):
    pairs = [(i, i ^ distance) for i in range(lax.axis_size(axis))]
    return lax.ppermute(value, axis, pairs)


def run_copies(copies):
    for copy in copies:
        copy.start()
    return copies


def piece_rows(rows):
    large = rows * 3 // 8
    return [large, large, rows - 2 * large]


def base_kernel(order, tokens_ref, weight_ref, *refs):
    *sent_refs, kept_ref, tokens, weight, sems = refs
    half, rows, width = kept_ref.shape
    parts = sems.shape[1]
    tile, slab = rows // parts, weight.shape[0] // parts
    place = lax.axis_index("tensor")

    def copy_of(number, source, held, size, i):
        span = pl.ds(i * size, size)
        return pltpu.make_async_copy(source.at[span], held.at[span], sems.at[number, i])

    token_copies = [copy_of(0, tokens_ref, tokens, tile, i) for i in range(parts)]
    weight_copies = [copy_of(1, weight_ref, weight, slab, i) for i in range(parts)]

    def add(first, low, high, fresh):
        for number, offset in enumerate(order):
            columns = pl.ds(pl.multiple_of((place ^ offset) * width, width), width)
            part = jnp.dot(
                tokens[first : first + tile, low:high],
                weight[low:high, columns],
                preferred_element_type=jnp.float32,
            )
            if number >= half:
                targets = [(kept_ref, number - half, first, 0, tile)]
            else:
                targets, start = [], 0
                for sent_ref in sent_refs:
                    stop = start + sent_ref.shape[1]
                    above, below = max(first, start), min(first + tile, stop)
                    if above < below:
                        targets.append(
                            (sent_ref, number, above - start, above - first, below - above)
                        )
                    start = stop
            for ref, index, at, source, size in targets:
                value = part[source : source + size]
                if not fresh:
                    value = value + ref[index, at : at + size, :]
                ref[index, at : at + size, :] = value

    run_copies([token_copies[0], *weight_copies])
    token_copies[0].wait()
    for i, copy in enumerate(weight_copies):
        copy.wait()
        if i == 0:
            run_copies(token_copies[1:])
        add(0, i * slab, (i + 1) * slab, i == 0)
    for i in range(1, parts):
        token_copies[i].wait()
        add(i * tile, 0, weight.shape[0], True)


def base_chunks(tokens, weight, order, width):
    rows = tokens.shape[0]
    half = len(order) // 2
    sizes = [*piece_rows(rows), rows]
    *sent, kept = pl.pallas_call(
        functools.partial(base_kernel, order),
        in_specs=[ANY] * 2,
        out_specs=[VMEM] * len(sizes),
        out_shape=[jax.ShapeDtypeStruct((half, size, width), jnp.float32) for size in sizes],
        scratch_shapes=[
            pltpu.VMEM(tokens.shape, tokens.dtype),
            pltpu.VMEM(weight.shape, weight.dtype),
            pltpu.SemaphoreType.DMA((2, 4)),
        ],
        compiler_params=PARAMS,
        cost_estimate=BASE,
    )(in_hbm(tokens), in_hbm(weight))
    return sent, kept


def add_kernel(kept_ref, *refs):
    *arrived_refs, out_ref, mine_ref = refs
    half = kept_ref.shape[0] // 2
    start = 0
    for arrived_ref in arrived_refs:
        rows = pl.ds(start, arrived_ref.shape[1])
        for i in range(half):
            mine_ref[i, rows, :] = kept_ref[i, rows, :] + arrived_ref[i]
            out = kept_ref[half + i, rows, :] + arrived_ref[half + i]
            out_ref[i, rows, :] = out.astype(out_ref.dtype)
        start += arrived_ref.shape[1]


def add_halves(kept, arrived, sent_type):
    count, rows, width = kept.shape
    shape = (count // 2, rows, width)
    return pl.pallas_call(
        add_kernel,
        in_specs=[VMEM] * (1 + len(arrived)),
        out_shape=[
            jax.ShapeDtypeStruct(shape, sent_type),
            jax.ShapeDtypeStruct(shape, jnp.float32),
        ],
        compiler_params=PARAMS,
        cost_estimate=NO_COST,
    )(kept, *arrived)


def base_parts(tokens, weight, width):
    size = lax.axis_size("tensor")
    kept_order = [k for k in range(size) if not k & 1]
    kept_order.sort(key=lambda k: [k >> bit & 1 for bit in range(1, size.bit_length())])
    return base_chunks(tokens, weight, [k ^ 1 for k in kept_order] + kept_order, width)


def base_sum(sent, kept):
    arrived = [swap(piece, "tensor", 1) for piece in sent]
    distance = 2
    size = lax.axis_size("tensor")
    while distance < size:
        sent_type = jnp.bfloat16 if 2 * distance == size else jnp.float32
        sent, kept = add_halves(kept, arrived, sent_type)
        arrived = [swap(sent, "tensor", distance)]
        distance *= 2
    return kept[0], arrived[0][0]


def pick(names_ref, table_ref, holder, holder_slots, count):
    blocks = [jnp.int32(0)] * count
    slots = [jnp.int32(0)] * count
    seen = jnp.int32(0)
    for j in range(names_ref.shape[1]):
        slot = table_ref[names_ref[0, j]]
        hit = lax.div(slot, jnp.int32(holder_slots)) == holder
        for k in range(count):
            chosen = hit & (seen == k)
            blocks[k] = jnp.where(chosen, jnp.int32(j), blocks[k])
            slots[k] = jnp.where(chosen, lax.rem(slot, jnp.int32(holder_slots)), slots[k])
        seen = seen + hit.astype(jnp.int32)
    return blocks, slots


def panel_copies(slot, down_ref, up_ref, out_ref, sems):
    depth = down_ref.shape[2]
    width = up_ref.shape[2]
    return [
        pltpu.make_async_copy(down_ref.at[slot], out_ref.at[:, pl.ds(0, depth)], sems.at[0]),
        pltpu.make_async_copy(up_ref.at[slot], out_ref.at[:, pl.ds(depth, width)], sems.at[1]),
    ]


def plan_kernel(capacity, *refs):
    sources, down_ref, up_ref = refs[:6], *refs[6:8]
    near_ref, plan_ref, *scalars, scalar_sems, sems = refs[-10:]
    holder_slots = down_ref.shape[0]
    loads = [
        pltpu.make_async_copy(source, scalar, scalar_sems.at[i])
        for i, (source, scalar) in enumerate(zip(sources, scalars))
    ]
    for load in run_copies(loads):
        load.wait()
    names_ref, first_ref, second_ref, third_ref, table_ref, live_ref = scalars
    here = lax.axis_index("pool")
    find = functools.partial(
        pick, table_ref=table_ref, holder_slots=holder_slots, count=capacity
    )
    near_slots = find(first_ref, holder=here)[1]
    copies = []
    for k, slot in enumerate(near_slots):
        copies += run_copies(panel_copies(slot, down_ref, up_ref, near_ref.at[k], sems.at[k]))
    inner = (here == 1) | (here == 2)
    own = find(names_ref, holder=here)
    near = find(names_ref, holder=here ^ 1)
    across = find(names_ref, holder=here ^ 3)
    late = find(names_ref, holder=here ^ 2)
    rows = [
        own[0],
        near[0],
        across[0],
        late[0],
        own[1],
        across[1],
        find(second_ref, holder=here)[1],
        find(third_ref, holder=here)[1],
        find(first_ref, holder=here ^ 3)[1],
        [inner.astype(jnp.int32)] * capacity,
        *[[live_ref[0, block] for block in phase[0]] for phase in (own, near, across, late)],
    ]
    for number, row in enumerate(rows):
        for k in range(capacity):
            plan_ref[number * capacity + k] = row[k]
    for copy in copies:
        copy.wait()


OWN, ACROSS, TO_INNER, TO_OUTER, FORWARD, INNER, LIVE, PLAN_ROWS = 4, 5, 6, 7, 8, 9, 10, 14


def make_plan(names, others, table, live, down, up, capacity, after):
    rank, depth = down.shape[1:]
    return pl.pallas_call(
        functools.partial(plan_kernel, capacity),
        in_specs=[ANY] * (8 + len(after)),
        out_specs=[ANY, SMEM],
        out_shape=[
            jax.ShapeDtypeStruct((capacity, rank, depth + up.shape[2]), down.dtype),
            jax.ShapeDtypeStruct((PLAN_ROWS * capacity,), jnp.int32),
        ],
        scratch_shapes=[pltpu.SMEM(names.shape, jnp.int32)] * 4
        + [pltpu.SMEM(table.shape, jnp.int32), pltpu.SMEM(live.shape, jnp.int32)]
        + [pltpu.SemaphoreType.DMA((6,)), pltpu.SemaphoreType.DMA((capacity, 2))],
        compiler_params=PARAMS,
        cost_estimate=SHORT,
    )(in_hbm(names), *others, in_hbm(table), in_hbm(live), down, up, *after)


def pack_kernel(starts, choose, capacity, outs, plan_ref, *refs):
    *out_refs, sems = refs[-1 - outs :]

    def run(start, down_ref, up_ref):
        copies = []
        for k in range(capacity):
            slot = plan_ref[start + k]
            out_ref = out_refs[k * outs // capacity].at[k % (capacity // outs)]
            copies += run_copies(panel_copies(slot, down_ref, up_ref, out_ref, sems.at[k]))
        for copy in copies:
            copy.wait()

    if len(starts) == 1:
        run(starts[0], *refs[:2])
    else:
        first = plan_ref[choose] != 0
        pl.when(first)(functools.partial(run, starts[0], *refs[:2]))
        pl.when(jnp.logical_not(first))(functools.partial(run, starts[1], *refs[2:4]))


def pack_panels(plan, choices, choose, capacity, outs=1, after=(), cost=None):
    sources = [a for _, *pair in choices for a in pair]
    rank, depth = sources[0].shape[1:]
    width = sources[1].shape[2]
    return pl.pallas_call(
        functools.partial(pack_kernel, [start for start, *_ in choices], choose, capacity, outs),
        in_specs=[SMEM] + [ANY] * (len(sources) + len(after)),
        out_specs=[ANY] * outs,
        out_shape=[jax.ShapeDtypeStruct((capacity // outs, rank, depth + width), sources[0].dtype)]
        * outs,
        scratch_shapes=[pltpu.SemaphoreType.DMA((capacity, 2))],
        compiler_params=PARAMS,
        cost_estimate=cost or NO_COST,
    )(plan, *sources, *after)


def each_block(phases, choose, plan_ref, refs, act):
    number = 0
    for row, count, rows in phases:
        mine, refs = refs[: len(rows)], refs[len(rows) :]

        def run(ref, row_of, number=number, row=row, count=count):
            for k in range(count):
                panel = ref.at[k if row_of is None else plan_ref[row_of + k]]
                act(number + k, plan_ref[row + k], panel)

        if len(rows) == 1:
            run(mine[0], rows[0])
        else:
            first = plan_ref[choose] != 0
            pl.when(first)(functools.partial(run, mine[0], rows[0]))
            pl.when(jnp.logical_not(first))(functools.partial(run, mine[1], rows[1]))
        number += count


def split_phases(phases):
    shapes = [(row, count, [source[1] for source in sources]) for row, count, sources in phases]
    return shapes, [source[0] for _, _, sources in phases for source in sources]


def shrink_kernel(phases, choose, plan_ref, token_ref, *refs):
    out_ref = refs[-1]
    depth = token_ref.shape[2]

    def act(number, block, panel_ref):
        out_ref[number] = lax.dot_general(
            panel_ref[:, :depth],
            token_ref[block],
            (((1,), (1,)), ((), ())),
            preferred_element_type=jnp.float32,
        ).astype(out_ref.dtype)

    each_block(phases, choose, plan_ref, refs, act)


def shrink(plan, row_blocks, phases, choose, after=(), kind=jnp.float32, cost=None):
    shapes, panels = split_phases(phases)
    total = sum(count for _, count, _ in phases)
    shape = (total, panels[0].shape[1], row_blocks.shape[1])
    return pl.pallas_call(
        functools.partial(shrink_kernel, shapes, choose),
        in_specs=[SMEM] + [VMEM] * (1 + len(panels)) + [ANY] * len(after),
        out_specs=VMEM,
        out_shape=jax.ShapeDtypeStruct(shape, kind),
        compiler_params=PARAMS,
        cost_estimate=cost or NO_COST,
    )(plan, row_blocks, *panels, *after)


def exchange(part):
    return [part] + [swap(part, "tensor", m) for m in range(1, lax.axis_size("tensor"))]


def combine_kernel(phases, choose, part_count, live_row, plan_ref, *refs):
    parts = refs[:part_count]
    mine_ref, far_ref = refs[part_count : part_count + 2]
    out_ref, held_ref, sems = refs[-3:]
    total, block_rows, width = held_ref.shape

    def copy_of(number, block):
        rows = pl.ds(pl.multiple_of(block * block_rows, block_rows), block_rows)
        return pltpu.make_async_copy(held_ref.at[number], out_ref.at[rows], sems.at[number])

    def act(number, block, panel_ref):
        shrunk = parts[0][number].astype(jnp.float32)
        for part in parts[1:]:
            shrunk = shrunk + part[number].astype(jnp.float32)
        start = panel_ref.shape[1] - width
        delta = lax.dot_general(
            shrunk.astype(jnp.bfloat16),
            panel_ref[:, start : start + width],
            (((0,), (0,)), ((), ())),
            preferred_element_type=jnp.float32,
        )
        rows = pl.ds(pl.multiple_of(block * block_rows, block_rows), block_rows)
        row = lax.broadcasted_iota(jnp.int32, delta.shape, 0)
        value = mine_ref[rows, :] + far_ref[rows, :].astype(jnp.float32) + ADAPTER_SCALE * delta
        value = jnp.where(row < plan_ref[live_row + number], value, 0.0)
        held_ref[number] = value.astype(held_ref.dtype)
        copy_of(number, block).start()

    each_block(phases, choose, plan_ref, refs[part_count + 2 :], act)
    number = 0
    for row, count, _ in phases:
        for k in range(count):
            copy_of(number, plan_ref[row + k]).wait()
            number += 1


def combine(plan, live_row, parts, base, phases, choose, out=None, cost=None):
    block_rows = parts[0].shape[2]
    rows, width = base[0].shape
    shapes, panels = split_phases(phases)
    total = sum(count for _, count, _ in phases)
    operands = [*parts, *base, *panels]
    specs = [VMEM] * len(operands)
    aliases = {}
    if out is not None:
        specs.append(ANY)
        operands.append(out)
        aliases = {len(operands): 0}
    return pl.pallas_call(
        functools.partial(combine_kernel, shapes, choose, len(parts), live_row),
        in_specs=[SMEM] + specs,
        out_specs=ANY,
        out_shape=pltpu.HBM((rows, width), jnp.bfloat16),
        input_output_aliases=aliases,
        scratch_shapes=[
            pltpu.VMEM((total, block_rows, width), jnp.bfloat16),
            pltpu.SemaphoreType.DMA((total,)),
        ],
        compiler_params=PARAMS,
        cost_estimate=cost or NO_COST,
    )(plan, *operands)


def on_line_of_four(tokens, weight, row_blocks, down, up, names, table, live, capacity):
    def across(value, pairs):
        return lax.ppermute(value, "pool", pairs)

    others = [swap(names, "pool", m) for m in range(1, 4)]
    inner_up = across(up, [(0, 0), (1, 2), (2, 1), (3, 3)])
    inner_down = across(down, [(0, 0), (1, 2), (2, 1), (3, 3)])
    sent, kept = base_parts(tokens, weight, up.shape[2])
    choose = INNER * capacity
    held = in_hbm(down), in_hbm(up)
    near_out, plan = make_plan(
        names, others, table, live, *held, capacity, [inner_up, sent[-1]]
    )

    def pack(choices, outs, after, cost=None):
        choices = [(row * capacity, *panels) for row, *panels in choices]
        return pack_panels(plan, choices, choose, capacity, outs, after, cost)

    near = across(near_out, [(0, 1), (1, 0), (2, 3), (3, 2)])
    base = base_sum(sent, kept)
    (outer_out,) = pack([(TO_OUTER, *held)], 1, [base[0]])
    to_outer = across(outer_out, [(0, 3), (1, 1), (2, 2), (3, 0)])
    late_out = pack(
        [(FORWARD, inner_down, inner_up), (TO_INNER, *held)], capacity, [outer_out], LONG
    )
    late = [across(panel, [(0, 2), (1, 0), (2, 3), (3, 1)]) for panel in late_out]

    first = [(0, capacity, [(down, OWN * capacity)]), (capacity, capacity, [(near, None)])]
    first_up = [(0, capacity, [(up, OWN * capacity)]), first[1]]
    middle = [(2 * capacity, capacity, [(inner_down, ACROSS * capacity), (to_outer, None)])]
    middle_up = [(2 * capacity, capacity, [(inner_up, ACROSS * capacity), (to_outer, None)])]

    def write(number, parts, phases, out, cost=None):
        live_row = LIVE * capacity + number
        return combine(plan, live_row, parts, base, phases, choose, out, cost)

    first_parts = exchange(shrink(plan, row_blocks, first, choose, late_out[:1]))
    out = write(0, first_parts, first_up, None, MIDDLE)
    number, phases = 2 * capacity, middle_up
    part = shrink(plan, row_blocks, middle, choose, [in_hbm(out)])
    parts = exchange(part)
    for k in range(capacity):
        last = [(3 * capacity + k, 1, [(late[k], None)])]
        kind = jnp.bfloat16 if k == capacity - 1 else jnp.float32
        part = shrink(plan, row_blocks, last, choose, [part, in_hbm(out)], kind)
        sums = exchange(part)
        out = write(number, parts, phases, out)
        number, parts, phases = 3 * capacity + k, sums, last
    return write(number, parts, phases, out)


def on_any_pool(tokens, weight, row_blocks, down, up, names, table, live, capacity):
    pool_size = lax.axis_size("pool")
    here = lax.axis_index("pool")
    holder_slots = down.shape[0]
    asked = table[lax.all_gather(names[0], "pool")]
    count = jnp.arange(capacity, dtype=jnp.int32)
    arrived = []
    for distance in range(pool_size):
        slots = asked[lax.rem(here + distance, pool_size)]
        hit = slots // holder_slots == here
        chosen = hit[None, :] & (jnp.cumsum(hit.astype(jnp.int32))[None, :] == 1 + count[:, None])
        plan = jnp.sum(jnp.where(chosen, (slots % holder_slots)[None, :], 0), axis=1)
        (panels,) = pack_panels(plan, [(0, down, up)], 0, capacity)
        pairs = [(i, (i + distance) % pool_size) for i in range(pool_size)]
        arrived.append(lax.ppermute(panels, "pool", pairs) if distance else panels)
    arrived = jnp.concatenate(arrived)
    owners = asked[here] // holder_slots
    blocks = jnp.arange(owners.shape[0], dtype=jnp.int32)
    earlier = (owners[:, None] == owners[None, :]) & (blocks[:, None] > blocks[None, :])
    ranks = jnp.sum(earlier.astype(jnp.int32), axis=1)
    places = lax.rem(here - owners + pool_size, pool_size) * capacity + ranks
    plan = jnp.concatenate([blocks, places, live[0]])
    base = base_sum(*base_parts(tokens, weight, up.shape[2]))
    phases = [(0, blocks.shape[0], [(arrived, blocks.shape[0])])]
    parts = exchange(shrink(plan, row_blocks, phases, 0))
    live_row = 2 * blocks.shape[0]
    return combine(plan, live_row, parts, base, phases, 0)


def on_device(
    tokens,
    value_weight,
    adapter_down_weight,
    adapter_up_weight,
    adapter_of_block,
    adapter_pool_slot,
    live_block_tokens,
):
    pool_size = lax.axis_size("pool")
    blocks = adapter_of_block.shape[1]
    capacity = -(-blocks // pool_size)
    row_blocks = tokens.reshape(blocks, tokens.shape[0] // blocks, tokens.shape[1])
    line = pool_size == 4 and blocks == capacity * pool_size
    route = on_line_of_four if line else on_any_pool
    return route(
        tokens,
        value_weight,
        row_blocks,
        jnp.transpose(adapter_down_weight, (0, 2, 1)),
        adapter_up_weight,
        adapter_of_block,
        adapter_pool_slot,
        live_block_tokens,
        capacity,
    )


def solution(mesh):
    return jax.shard_map(
        on_device,
        mesh=mesh,
        in_specs=(
            P(("groups", "pool"), "tensor"),
            P("tensor", None),
            P(("groups", "pool"), "tensor", None),
            P(("groups", "pool"), None, "tensor"),
            P(("groups", "pool"), None),
            P("groups"),
            P(("groups", "pool"), None),
        ),
        out_specs=P(("groups", "pool"), "tensor"),
        check_vma=False,
    )
```

```python
import functools

import jax
import jax.numpy as jnp
from jax import lax
from jax.experimental import pallas as pl
from jax.experimental.pallas import tpu as pltpu
from jax.sharding import PartitionSpec as P

ADAPTER_SCALE = 0.5
ROW_TILE = 256
PARAMS = pltpu.CompilerParams(vmem_limit_bytes=20 * 1024 * 1024)
NO_COST = pl.CostEstimate(flops=0, bytes_accessed=0, transcendentals=0)
BASE = pl.CostEstimate(flops=4 * 10**9, bytes_accessed=0, transcendentals=0)
SHORT = pl.CostEstimate(flops=10 * 10**9, bytes_accessed=0, transcendentals=0)
MIDDLE = pl.CostEstimate(flops=0 * 10**9, bytes_accessed=0, transcendentals=0)
LONG = pl.CostEstimate(flops=6 * 10**9, bytes_accessed=0, transcendentals=0)
ANY = pl.BlockSpec(memory_space=pl.ANY)
SMEM = pl.BlockSpec(memory_space=pltpu.SMEM)
VMEM = pl.BlockSpec(memory_space=pltpu.VMEM)


def in_hbm(value):
    return pltpu.with_memory_space_constraint(value, pltpu.HBM)


def swap(value, axis, distance):
    pairs = [(i, i ^ distance) for i in range(lax.axis_size(axis))]
    return lax.ppermute(value, axis, pairs)


def run_copies(copies):
    for copy in copies:
        copy.start()
    return copies


def piece_rows(rows):
    large = rows * 3 // 8
    return [large, large, rows - 2 * large]


def base_kernel(order, capacity, tokens_ref, weight_ref, *refs):
    if capacity:
        *asked, down_ref, up_ref = refs[:8]
        *scalars, scalar_sems, panel_sems = refs[-8:]
        near_ref, plan_ref, *held = refs[-13:-8]
        refs = [*refs[-17:-13], *held]
        loads = [
            pltpu.make_async_copy(source, scalar, scalar_sems.at[i])
            for i, (source, scalar) in enumerate(zip(asked, scalars))
        ]
        run_copies(loads)
    *sent_refs, kept_ref, tokens, weight, sems = refs
    half, rows, width = kept_ref.shape
    parts = sems.shape[1]
    tile, slab = rows // parts, weight.shape[0] // parts
    place = lax.axis_index("tensor")

    def copy_of(number, source, held, size, i):
        span = pl.ds(i * size, size)
        return pltpu.make_async_copy(source.at[span], held.at[span], sems.at[number, i])

    token_copies = [copy_of(0, tokens_ref, tokens, tile, i) for i in range(parts)]
    weight_copies = [copy_of(1, weight_ref, weight, slab, i) for i in range(parts)]

    def add(first, low, high, fresh):
        for number, offset in enumerate(order):
            columns = pl.ds(pl.multiple_of((place ^ offset) * width, width), width)
            part = jnp.dot(
                tokens[first : first + tile, low:high],
                weight[low:high, columns],
                preferred_element_type=jnp.float32,
            )
            if number >= half:
                targets = [(kept_ref, number - half, first, 0, tile)]
            else:
                targets, start = [], 0
                for sent_ref in sent_refs:
                    stop = start + sent_ref.shape[1]
                    above, below = max(first, start), min(first + tile, stop)
                    if above < below:
                        targets.append(
                            (sent_ref, number, above - start, above - first, below - above)
                        )
                    start = stop
            for ref, index, at, source, size in targets:
                value = part[source : source + size]
                if not fresh:
                    value = value + ref[index, at : at + size, :]
                ref[index, at : at + size, :] = value

    run_copies([token_copies[0], *weight_copies])
    packing = []
    if capacity:
        for load in loads:
            load.wait()
        packing = write_plan(
            capacity, scalars, down_ref, up_ref, near_ref, plan_ref, panel_sems
        )
    token_copies[0].wait()
    for i, copy in enumerate(weight_copies):
        copy.wait()
        if i == 0:
            run_copies(token_copies[1:])
        add(0, i * slab, (i + 1) * slab, i == 0)
    for i in range(1, parts):
        token_copies[i].wait()
        add(i * tile, 0, weight.shape[0], True)
    for copy in packing:
        copy.wait()


def base_chunks(tokens, weight, order, width, planning=None, after=()):
    rows = tokens.shape[0]
    half = len(order) // 2
    sizes = [*piece_rows(rows), rows]
    specs = [VMEM] * len(sizes)
    shapes = [jax.ShapeDtypeStruct((half, size, width), jnp.float32) for size in sizes]
    scratch = [
        pltpu.VMEM(tokens.shape, tokens.dtype),
        pltpu.VMEM(weight.shape, weight.dtype),
        pltpu.SemaphoreType.DMA((2, 4)),
    ]
    operands, capacity = [], 0
    if planning is not None:
        *operands, capacity = planning
        down, up = operands[-2:]
        specs += [ANY, SMEM]
        shapes += [
            jax.ShapeDtypeStruct((capacity, down.shape[1], down.shape[2] + width), down.dtype),
            jax.ShapeDtypeStruct((PLAN_ROWS * capacity,), jnp.int32),
        ]
        scratch += [pltpu.SMEM(operand.shape, operand.dtype) for operand in operands[:6]]
        scratch += [pltpu.SemaphoreType.DMA((6,)), pltpu.SemaphoreType.DMA((capacity, 2))]
    return pl.pallas_call(
        functools.partial(base_kernel, order, capacity),
        in_specs=[ANY] * (2 + len(operands) + len(after)),
        out_specs=specs,
        out_shape=shapes,
        scratch_shapes=scratch,
        compiler_params=PARAMS,
        cost_estimate=BASE,
    )(in_hbm(tokens), in_hbm(weight), *operands, *after)


def add_kernel(kept_ref, *refs):
    *arrived_refs, out_ref, mine_ref = refs
    half = kept_ref.shape[0] // 2
    start = 0
    for arrived_ref in arrived_refs:
        rows = pl.ds(start, arrived_ref.shape[1])
        for i in range(half):
            mine_ref[i, rows, :] = kept_ref[i, rows, :] + arrived_ref[i]
            out = kept_ref[half + i, rows, :] + arrived_ref[half + i]
            out_ref[i, rows, :] = out.astype(out_ref.dtype)
        start += arrived_ref.shape[1]


def add_halves(kept, arrived, sent_type):
    count, rows, width = kept.shape
    shape = (count // 2, rows, width)
    return pl.pallas_call(
        add_kernel,
        in_specs=[VMEM] * (1 + len(arrived)),
        out_shape=[
            jax.ShapeDtypeStruct(shape, sent_type),
            jax.ShapeDtypeStruct(shape, jnp.float32),
        ],
        compiler_params=PARAMS,
        cost_estimate=NO_COST,
    )(kept, *arrived)


def base_parts(tokens, weight, width, planning=None, after=()):
    size = lax.axis_size("tensor")
    kept_order = [k for k in range(size) if not k & 1]
    kept_order.sort(key=lambda k: [k >> bit & 1 for bit in range(1, size.bit_length())])
    return base_chunks(tokens, weight, [k ^ 1 for k in kept_order] + kept_order, width, planning, after)


def base_sum(sent, kept):
    arrived = [swap(piece, "tensor", 1) for piece in sent]
    distance = 2
    size = lax.axis_size("tensor")
    while distance < size:
        sent_type = jnp.bfloat16 if 2 * distance == size else jnp.float32
        sent, kept = add_halves(kept, arrived, sent_type)
        arrived = [swap(sent, "tensor", distance)]
        distance *= 2
    return kept[0], arrived[0][0]


def pick(names_ref, table_ref, holder, holder_slots, count):
    blocks = [jnp.int32(0)] * count
    slots = [jnp.int32(0)] * count
    seen = jnp.int32(0)
    for j in range(names_ref.shape[1]):
        slot = table_ref[names_ref[0, j]]
        hit = lax.div(slot, jnp.int32(holder_slots)) == holder
        for k in range(count):
            chosen = hit & (seen == k)
            blocks[k] = jnp.where(chosen, jnp.int32(j), blocks[k])
            slots[k] = jnp.where(chosen, lax.rem(slot, jnp.int32(holder_slots)), slots[k])
        seen = seen + hit.astype(jnp.int32)
    return blocks, slots


def panel_copies(k, slot, down_ref, up_ref, out_ref, sems):
    depth = down_ref.shape[2]
    width = up_ref.shape[2]
    return [
        pltpu.make_async_copy(down_ref.at[slot], out_ref.at[k, :, pl.ds(0, depth)], sems.at[k, 0]),
        pltpu.make_async_copy(up_ref.at[slot], out_ref.at[k, :, pl.ds(depth, width)], sems.at[k, 1]),
    ]


def write_plan(capacity, scalars, down_ref, up_ref, near_ref, plan_ref, sems):
    holder_slots = down_ref.shape[0]
    names_ref, first_ref, second_ref, third_ref, table_ref, live_ref = scalars
    here = lax.axis_index("pool")
    find = functools.partial(
        pick, table_ref=table_ref, holder_slots=holder_slots, count=capacity
    )
    near_slots = find(first_ref, holder=here)[1]
    copies = []
    for k, slot in enumerate(near_slots):
        copies += run_copies(panel_copies(k, slot, down_ref, up_ref, near_ref, sems))
    inner = (here == 1) | (here == 2)
    own = find(names_ref, holder=here)
    near = find(names_ref, holder=here ^ 1)
    across = find(names_ref, holder=here ^ 3)
    late = find(names_ref, holder=here ^ 2)
    rows = [
        own[0],
        near[0],
        across[0],
        late[0],
        own[1],
        across[1],
        find(second_ref, holder=here)[1],
        find(third_ref, holder=here)[1],
        find(first_ref, holder=here ^ 3)[1],
        [inner.astype(jnp.int32)] * capacity,
        *[[live_ref[0, block] for block in phase[0]] for phase in (own, near, across, late)],
    ]
    for number, row in enumerate(rows):
        for k in range(capacity):
            plan_ref[number * capacity + k] = row[k]
    return copies


OWN, ACROSS, TO_INNER, TO_OUTER, FORWARD, INNER, LIVE, PLAN_ROWS = 4, 5, 6, 7, 8, 9, 10, 14


def pack_kernel(starts, choose, capacity, inputs, plan_ref, *refs):
    out_ref, sems = refs[inputs], refs[-1]

    def run(start, down_ref, up_ref):
        copies = []
        for k in range(capacity):
            slot = plan_ref[start + k]
            copies += run_copies(panel_copies(k, slot, down_ref, up_ref, out_ref, sems))
        for copy in copies:
            copy.wait()

    if len(starts) == 1:
        run(starts[0], *refs[:2])
    else:
        first = plan_ref[choose] != 0
        pl.when(first)(functools.partial(run, starts[0], *refs[:2]))
        pl.when(jnp.logical_not(first))(functools.partial(run, starts[1], *refs[2:4]))


def pack_panels(plan, choices, choose, capacity, after=(), cost=None, carried=None):
    sources = [a for _, *pair in choices for a in pair]
    rank, depth = sources[0].shape[1:]
    width = sources[1].shape[2]
    operands = [plan, *sources, *after]
    out = jax.ShapeDtypeStruct((capacity, rank, depth + width), sources[0].dtype)
    outs, aliases = [out], {}
    if carried is not None:
        aliases = {len(operands): 1}
        operands.append(carried)
        outs.append(jax.ShapeDtypeStruct(carried.shape, carried.dtype))
    results = pl.pallas_call(
        functools.partial(pack_kernel, [start for start, *_ in choices], choose, capacity, len(operands) - 1),
        in_specs=[SMEM] + [ANY] * (len(operands) - 1),
        out_specs=[ANY] * len(outs),
        out_shape=outs,
        input_output_aliases=aliases,
        scratch_shapes=[pltpu.SemaphoreType.DMA((capacity, 2))],
        compiler_params=PARAMS,
        cost_estimate=cost or NO_COST,
    )(*operands)
    return results[0] if carried is None else results


def each_block(phases, choose, plan_ref, refs, act):
    number = 0
    for row, count, rows in phases:
        mine, refs = refs[: len(rows)], refs[len(rows) :]

        def run(ref, row_of, number=number, row=row, count=count):
            for k in range(count):
                panel = ref.at[k if row_of is None else plan_ref[row_of + k]]
                act(number + k, plan_ref[row + k], panel)

        if len(rows) == 1:
            run(mine[0], rows[0])
        else:
            first = plan_ref[choose] != 0
            pl.when(first)(functools.partial(run, mine[0], rows[0]))
            pl.when(jnp.logical_not(first))(functools.partial(run, mine[1], rows[1]))
        number += count


def split_phases(phases):
    shapes = [(row, count, [source[1] for source in sources]) for row, count, sources in phases]
    return shapes, [source[0] for _, _, sources in phases for source in sources]


def shrink_kernel(phases, choose, plan_ref, token_ref, *refs):
    out_ref = refs[-1]
    depth = token_ref.shape[2]

    def act(number, block, panel_ref):
        out_ref[number] = lax.dot_general(
            panel_ref[:, :depth],
            token_ref[block],
            (((1,), (1,)), ((), ())),
            preferred_element_type=jnp.float32,
        ).astype(out_ref.dtype)

    each_block(phases, choose, plan_ref, refs, act)


def shrink(plan, row_blocks, phases, choose, after=(), kind=jnp.float32, cost=None):
    shapes, panels = split_phases(phases)
    total = sum(count for _, count, _ in phases)
    shape = (total, panels[0].shape[1], row_blocks.shape[1])
    return pl.pallas_call(
        functools.partial(shrink_kernel, shapes, choose),
        in_specs=[SMEM] + [VMEM] * (1 + len(panels)) + [ANY] * len(after),
        out_specs=VMEM,
        out_shape=jax.ShapeDtypeStruct(shape, kind),
        compiler_params=PARAMS,
        cost_estimate=cost or NO_COST,
    )(plan, row_blocks, *panels, *after)


def exchange(part):
    return [part] + [swap(part, "tensor", m) for m in range(1, lax.axis_size("tensor"))]


def combine_kernel(phases, choose, part_count, live_row, plan_ref, *refs):
    parts = refs[:part_count]
    mine_ref, far_ref = refs[part_count : part_count + 2]
    out_ref, held_ref, sems = refs[-3:]
    total, block_rows, width = held_ref.shape

    def copy_of(number, block):
        rows = pl.ds(pl.multiple_of(block * block_rows, block_rows), block_rows)
        return pltpu.make_async_copy(held_ref.at[number], out_ref.at[rows], sems.at[number])

    def act(number, block, panel_ref):
        shrunk = parts[0][number].astype(jnp.float32)
        for part in parts[1:]:
            shrunk = shrunk + part[number].astype(jnp.float32)
        start = panel_ref.shape[1] - width
        delta = lax.dot_general(
            shrunk.astype(jnp.bfloat16),
            panel_ref[:, start : start + width],
            (((0,), (0,)), ((), ())),
            preferred_element_type=jnp.float32,
        )
        rows = pl.ds(pl.multiple_of(block * block_rows, block_rows), block_rows)
        row = lax.broadcasted_iota(jnp.int32, delta.shape, 0)
        value = mine_ref[rows, :] + far_ref[rows, :].astype(jnp.float32) + ADAPTER_SCALE * delta
        value = jnp.where(row < plan_ref[live_row + number], value, 0.0)
        held_ref[number] = value.astype(held_ref.dtype)
        copy_of(number, block).start()

    each_block(phases, choose, plan_ref, refs[part_count + 2 :], act)
    number = 0
    for row, count, _ in phases:
        for k in range(count):
            copy_of(number, plan_ref[row + k]).wait()
            number += 1


def combine(plan, live_row, parts, base, phases, choose, out=None, cost=None):
    block_rows = parts[0].shape[2]
    rows, width = base[0].shape
    shapes, panels = split_phases(phases)
    total = sum(count for _, count, _ in phases)
    operands = [*parts, *base, *panels]
    specs = [VMEM] * len(operands)
    aliases = {}
    if out is not None:
        specs.append(ANY)
        operands.append(out)
        aliases = {len(operands): 0}
    return pl.pallas_call(
        functools.partial(combine_kernel, shapes, choose, len(parts), live_row),
        in_specs=[SMEM] + specs,
        out_specs=ANY,
        out_shape=pltpu.HBM((rows, width), jnp.bfloat16),
        input_output_aliases=aliases,
        scratch_shapes=[
            pltpu.VMEM((total, block_rows, width), jnp.bfloat16),
            pltpu.SemaphoreType.DMA((total,)),
        ],
        compiler_params=PARAMS,
        cost_estimate=cost or NO_COST,
    )(plan, *operands)


def on_line_of_four(tokens, weight, row_blocks, down, up, names, table, live, capacity):
    def across(value, pairs):
        return lax.ppermute(value, "pool", pairs)

    others = [swap(names, "pool", m) for m in range(1, 4)]
    inner_up = across(up, [(0, 0), (1, 2), (2, 1), (3, 3)])
    inner_down = across(down, [(0, 0), (1, 2), (2, 1), (3, 3)])
    choose = INNER * capacity
    held = in_hbm(down), in_hbm(up)
    planning = [in_hbm(names), *others, in_hbm(table), in_hbm(live), *held, capacity]
    *sent, kept, near_out, plan = base_parts(tokens, weight, up.shape[2], planning, [inner_up])

    def pack(choices, after, cost=None, carried=None):
        choices = [(row * capacity, *panels) for row, *panels in choices]
        return pack_panels(plan, choices, choose, capacity, after, cost, carried)

    outer_out, near_out = pack([(TO_OUTER, *held)], [], carried=near_out)
    near = across(near_out, [(0, 1), (1, 0), (2, 3), (3, 2)])
    to_outer = across(outer_out, [(0, 3), (1, 1), (2, 2), (3, 0)])
    base = base_sum(sent, kept)
    late_out = pack(
        [(FORWARD, inner_down, inner_up), (TO_INNER, *held)], [base[0], outer_out], LONG
    )
    late = across(late_out, [(0, 2), (1, 0), (2, 3), (3, 1)])

    first = [(0, capacity, [(down, OWN * capacity)]), (capacity, capacity, [(near, None)])]
    first_up = [(0, capacity, [(up, OWN * capacity)]), first[1]]
    middle = [(2 * capacity, capacity, [(inner_down, ACROSS * capacity), (to_outer, None)])]
    middle_up = [(2 * capacity, capacity, [(inner_up, ACROSS * capacity), (to_outer, None)])]
    last = [(3 * capacity, capacity, [(late, None)])]

    def write(number, parts, phases, out, cost=None):
        live_row = (LIVE + number) * capacity
        return combine(plan, live_row, parts, base, phases, choose, out, cost)

    first_parts = exchange(shrink(plan, row_blocks, first, choose, [late_out]))
    out = write(0, first_parts, first_up, None, MIDDLE)
    middle_part = shrink(plan, row_blocks, middle, choose, [in_hbm(out)])
    middle_parts = exchange(middle_part)
    last_parts = exchange(shrink(plan, row_blocks, last, choose, [middle_part], jnp.bfloat16))
    out = write(2, middle_parts, middle_up, out)
    return write(3, last_parts, last, out)


def on_any_pool(tokens, weight, row_blocks, down, up, names, table, live, capacity):
    pool_size = lax.axis_size("pool")
    here = lax.axis_index("pool")
    holder_slots = down.shape[0]
    asked = table[lax.all_gather(names[0], "pool")]
    count = jnp.arange(capacity, dtype=jnp.int32)
    arrived = []
    for distance in range(pool_size):
        slots = asked[lax.rem(here + distance, pool_size)]
        hit = slots // holder_slots == here
        chosen = hit[None, :] & (jnp.cumsum(hit.astype(jnp.int32))[None, :] == 1 + count[:, None])
        plan = jnp.sum(jnp.where(chosen, (slots % holder_slots)[None, :], 0), axis=1)
        panels = pack_panels(plan, [(0, down, up)], 0, capacity)
        pairs = [(i, (i + distance) % pool_size) for i in range(pool_size)]
        arrived.append(lax.ppermute(panels, "pool", pairs) if distance else panels)
    arrived = jnp.concatenate(arrived)
    owners = asked[here] // holder_slots
    blocks = jnp.arange(owners.shape[0], dtype=jnp.int32)
    earlier = (owners[:, None] == owners[None, :]) & (blocks[:, None] > blocks[None, :])
    ranks = jnp.sum(earlier.astype(jnp.int32), axis=1)
    places = lax.rem(here - owners + pool_size, pool_size) * capacity + ranks
    plan = jnp.concatenate([blocks, places, live[0]])
    *sent, kept = base_parts(tokens, weight, up.shape[2])
    base = base_sum(sent, kept)
    phases = [(0, blocks.shape[0], [(arrived, blocks.shape[0])])]
    parts = exchange(shrink(plan, row_blocks, phases, 0))
    live_row = 2 * blocks.shape[0]
    return combine(plan, live_row, parts, base, phases, 0)


def on_device(
    tokens,
    value_weight,
    adapter_down_weight,
    adapter_up_weight,
    adapter_of_block,
    adapter_pool_slot,
    live_block_tokens,
):
    pool_size = lax.axis_size("pool")
    blocks = adapter_of_block.shape[1]
    capacity = -(-blocks // pool_size)
    row_blocks = tokens.reshape(blocks, tokens.shape[0] // blocks, tokens.shape[1])
    line = pool_size == 4 and blocks == capacity * pool_size
    route = on_line_of_four if line else on_any_pool
    return route(
        tokens,
        value_weight,
        row_blocks,
        jnp.transpose(adapter_down_weight, (0, 2, 1)),
        adapter_up_weight,
        adapter_of_block,
        adapter_pool_slot,
        live_block_tokens,
        capacity,
    )


def solution(mesh):
    return jax.shard_map(
        on_device,
        mesh=mesh,
        in_specs=(
            P(("groups", "pool"), "tensor"),
            P("tensor", None),
            P(("groups", "pool"), "tensor", None),
            P(("groups", "pool"), None, "tensor"),
            P(("groups", "pool"), None),
            P("groups"),
            P(("groups", "pool"), None),
        ),
        out_specs=P(("groups", "pool"), "tensor"),
        check_vma=False,
    )
```

```python
import functools

import jax
import jax.numpy as jnp
from jax import lax
from jax.experimental import pallas as pl
from jax.experimental.pallas import tpu as pltpu
from jax.sharding import PartitionSpec as P

ADAPTER_SCALE = 0.5
ROW_TILE = 256
PARAMS = pltpu.CompilerParams(vmem_limit_bytes=20 * 1024 * 1024)
NO_COST = pl.CostEstimate(flops=0, bytes_accessed=0, transcendentals=0)
BASE = pl.CostEstimate(flops=4 * 10**9, bytes_accessed=0, transcendentals=0)
SHORT = pl.CostEstimate(flops=2 * 10**9, bytes_accessed=0, transcendentals=0)
MIDDLE = pl.CostEstimate(flops=0 * 10**9, bytes_accessed=0, transcendentals=0)
LONG = pl.CostEstimate(flops=6 * 10**9, bytes_accessed=0, transcendentals=0)
ANY = pl.BlockSpec(memory_space=pl.ANY)
SMEM = pl.BlockSpec(memory_space=pltpu.SMEM)
VMEM = pl.BlockSpec(memory_space=pltpu.VMEM)


def in_hbm(value):
    return pltpu.with_memory_space_constraint(value, pltpu.HBM)


def swap(value, axis, distance):
    pairs = [(i, i ^ distance) for i in range(lax.axis_size(axis))]
    return lax.ppermute(value, axis, pairs)


def run_copies(copies):
    for copy in copies:
        copy.start()
    return copies


def piece_rows(rows):
    large = rows * 3 // 8
    return [large, large, rows - 2 * large]


def base_kernel(order, capacity, tokens_ref, weight_ref, *refs):
    if capacity:
        *asked, down_ref, up_ref = refs[:6]
        *scalars, scalar_sems, panel_sems = refs[-6:]
        near_ref, plan_ref, *held = refs[-11:-6]
        refs = [*refs[-15:-11], *held]
        loads = [
            pltpu.make_async_copy(source, scalar, scalar_sems.at[i])
            for i, (source, scalar) in enumerate(zip(asked, scalars))
        ]
        run_copies(loads)
    *sent_refs, kept_ref, tokens, weight, sems = refs
    half, rows, width = kept_ref.shape
    parts = sems.shape[1]
    tile, slab = rows // parts, weight.shape[0] // parts
    place = lax.axis_index("tensor")

    def copy_of(number, source, held, size, i):
        span = pl.ds(i * size, size)
        return pltpu.make_async_copy(source.at[span], held.at[span], sems.at[number, i])

    token_copies = [copy_of(0, tokens_ref, tokens, tile, i) for i in range(parts)]
    weight_copies = [copy_of(1, weight_ref, weight, slab, i) for i in range(parts)]

    def add(first, low, high, fresh):
        for number, offset in enumerate(order):
            columns = pl.ds(pl.multiple_of((place ^ offset) * width, width), width)
            part = jnp.dot(
                tokens[first : first + tile, low:high],
                weight[low:high, columns],
                preferred_element_type=jnp.float32,
            )
            if number >= half:
                targets = [(kept_ref, number - half, first, 0, tile)]
            else:
                targets, start = [], 0
                for sent_ref in sent_refs:
                    stop = start + sent_ref.shape[1]
                    above, below = max(first, start), min(first + tile, stop)
                    if above < below:
                        targets.append(
                            (sent_ref, number, above - start, above - first, below - above)
                        )
                    start = stop
            for ref, index, at, source, size in targets:
                value = part[source : source + size]
                if not fresh:
                    value = value + ref[index, at : at + size, :]
                ref[index, at : at + size, :] = value

    run_copies([token_copies[0], *weight_copies])
    packing = []
    if capacity:
        for load in loads:
            load.wait()
        packing = write_plan(
            capacity, scalars, down_ref, up_ref, near_ref, plan_ref, panel_sems
        )
    token_copies[0].wait()
    for i, copy in enumerate(weight_copies):
        copy.wait()
        if i == 0:
            run_copies(token_copies[1:])
        add(0, i * slab, (i + 1) * slab, i == 0)
    for i in range(1, parts):
        token_copies[i].wait()
        add(i * tile, 0, weight.shape[0], True)
    for copy in packing:
        copy.wait()


def base_chunks(tokens, weight, order, width, planning=None, after=()):
    rows = tokens.shape[0]
    half = len(order) // 2
    sizes = [*piece_rows(rows), rows]
    specs = [VMEM] * len(sizes)
    shapes = [jax.ShapeDtypeStruct((half, size, width), jnp.float32) for size in sizes]
    scratch = [
        pltpu.VMEM(tokens.shape, tokens.dtype),
        pltpu.VMEM(weight.shape, weight.dtype),
        pltpu.SemaphoreType.DMA((2, 4)),
    ]
    operands, capacity = [], 0
    if planning is not None:
        *operands, capacity = planning
        down, up = operands[-2:]
        specs += [ANY, SMEM]
        shapes += [
            jax.ShapeDtypeStruct((capacity, down.shape[1], down.shape[2] + width), down.dtype),
            jax.ShapeDtypeStruct((PLAN_ROWS * capacity,), jnp.int32),
        ]
        scratch += [pltpu.SMEM(operand.shape, operand.dtype) for operand in operands[:4]]
        scratch += [pltpu.SemaphoreType.DMA((4,)), pltpu.SemaphoreType.DMA((capacity, 2))]
    return pl.pallas_call(
        functools.partial(base_kernel, order, capacity),
        in_specs=[ANY] * (2 + len(operands) + len(after)),
        out_specs=specs,
        out_shape=shapes,
        scratch_shapes=scratch,
        compiler_params=PARAMS,
        cost_estimate=BASE,
    )(in_hbm(tokens), in_hbm(weight), *operands, *after)


def add_kernel(kept_ref, *refs):
    *arrived_refs, out_ref, mine_ref = refs
    half = kept_ref.shape[0] // 2
    start = 0
    for arrived_ref in arrived_refs:
        rows = pl.ds(start, arrived_ref.shape[1])
        for i in range(half):
            mine_ref[i, rows, :] = kept_ref[i, rows, :] + arrived_ref[i]
            out = kept_ref[half + i, rows, :] + arrived_ref[half + i]
            out_ref[i, rows, :] = out.astype(out_ref.dtype)
        start += arrived_ref.shape[1]


def add_halves(kept, arrived, sent_type):
    count, rows, width = kept.shape
    shape = (count // 2, rows, width)
    return pl.pallas_call(
        add_kernel,
        in_specs=[VMEM] * (1 + len(arrived)),
        out_shape=[
            jax.ShapeDtypeStruct(shape, sent_type),
            jax.ShapeDtypeStruct(shape, jnp.float32),
        ],
        compiler_params=PARAMS,
        cost_estimate=NO_COST,
    )(kept, *arrived)


def base_parts(tokens, weight, width, planning=None, after=()):
    size = lax.axis_size("tensor")
    kept_order = [k for k in range(size) if not k & 1]
    kept_order.sort(key=lambda k: [k >> bit & 1 for bit in range(1, size.bit_length())])
    return base_chunks(tokens, weight, [k ^ 1 for k in kept_order] + kept_order, width, planning, after)


def base_sum(sent, kept):
    arrived = [swap(piece, "tensor", 1) for piece in sent]
    distance = 2
    size = lax.axis_size("tensor")
    while distance < size:
        sent_type = jnp.bfloat16 if 2 * distance == size else jnp.float32
        sent, kept = add_halves(kept, arrived, sent_type)
        arrived = [swap(sent, "tensor", distance)]
        distance *= 2
    return kept[0], arrived[0][0]


def pick(asked_ref, index, table_ref, holder, holder_slots, count):
    blocks = [jnp.int32(0)] * count
    slots = [jnp.int32(0)] * count
    seen = jnp.int32(0)
    for j in range(asked_ref.shape[1]):
        slot = table_ref[asked_ref[index, j]]
        hit = lax.div(slot, jnp.int32(holder_slots)) == holder
        for k in range(count):
            chosen = hit & (seen == k)
            blocks[k] = jnp.where(chosen, jnp.int32(j), blocks[k])
            slots[k] = jnp.where(chosen, lax.rem(slot, jnp.int32(holder_slots)), slots[k])
        seen = seen + hit.astype(jnp.int32)
    return blocks, slots


def panel_copies(k, slot, down_ref, up_ref, out_ref, sems):
    depth = down_ref.shape[2]
    width = up_ref.shape[2]
    return [
        pltpu.make_async_copy(down_ref.at[slot], out_ref.at[k, :, pl.ds(0, depth)], sems.at[k, 0]),
        pltpu.make_async_copy(up_ref.at[slot], out_ref.at[k, :, pl.ds(depth, width)], sems.at[k, 1]),
    ]


def join_kernel(*refs):
    *row_refs, out_ref = refs
    for i, row_ref in enumerate(row_refs):
        out_ref[i : i + 1, :] = row_ref[...]


def join(rows):
    return pl.pallas_call(
        join_kernel,
        in_specs=[VMEM] * len(rows),
        out_specs=VMEM,
        out_shape=jax.ShapeDtypeStruct((len(rows), rows[0].shape[1]), rows[0].dtype),
        cost_estimate=SHORT,
    )(*rows)


def write_plan(capacity, scalars, down_ref, up_ref, near_ref, plan_ref, sems):
    holder_slots = down_ref.shape[0]
    names_ref, asked_ref, table_ref, live_ref = scalars
    here = lax.axis_index("pool")
    find = functools.partial(
        pick, table_ref=table_ref, holder_slots=holder_slots, count=capacity
    )
    near_slots = find(asked_ref, 0, holder=here)[1]
    copies = []
    for k, slot in enumerate(near_slots):
        copies += run_copies(panel_copies(k, slot, down_ref, up_ref, near_ref, sems))
    inner = (here == 1) | (here == 2)
    own = find(names_ref, 0, holder=here)
    near = find(names_ref, 0, holder=here ^ 1)
    across = find(names_ref, 0, holder=here ^ 3)
    late = find(names_ref, 0, holder=here ^ 2)
    rows = [
        own[0],
        near[0],
        across[0],
        late[0],
        own[1],
        across[1],
        find(asked_ref, 1, holder=here)[1],
        find(asked_ref, 2, holder=here)[1],
        find(asked_ref, 0, holder=here ^ 3)[1],
        [inner.astype(jnp.int32)] * capacity,
        *[[live_ref[0, block] for block in phase[0]] for phase in (own, near, across, late)],
    ]
    for number, row in enumerate(rows):
        for k in range(capacity):
            plan_ref[number * capacity + k] = row[k]
    return copies


OWN, ACROSS, TO_INNER, TO_OUTER, FORWARD, INNER, LIVE, PLAN_ROWS = 4, 5, 6, 7, 8, 9, 10, 14


def pack_kernel(starts, choose, capacity, inputs, plan_ref, *refs):
    out_ref, sems = refs[inputs], refs[-1]

    def run(start, down_ref, up_ref):
        copies = []
        for k in range(capacity):
            slot = plan_ref[start + k]
            copies += run_copies(panel_copies(k, slot, down_ref, up_ref, out_ref, sems))
        for copy in copies:
            copy.wait()

    if len(starts) == 1:
        run(starts[0], *refs[:2])
    else:
        first = plan_ref[choose] != 0
        pl.when(first)(functools.partial(run, starts[0], *refs[:2]))
        pl.when(jnp.logical_not(first))(functools.partial(run, starts[1], *refs[2:4]))


def pack_panels(plan, choices, choose, capacity, after=(), cost=None, carried=None):
    sources = [a for _, *pair in choices for a in pair]
    rank, depth = sources[0].shape[1:]
    width = sources[1].shape[2]
    operands = [plan, *sources, *after]
    out = jax.ShapeDtypeStruct((capacity, rank, depth + width), sources[0].dtype)
    outs, aliases = [out], {}
    if carried is not None:
        aliases = {len(operands): 1}
        operands.append(carried)
        outs.append(jax.ShapeDtypeStruct(carried.shape, carried.dtype))
    results = pl.pallas_call(
        functools.partial(pack_kernel, [start for start, *_ in choices], choose, capacity, len(operands) - 1),
        in_specs=[SMEM] + [ANY] * (len(operands) - 1),
        out_specs=[ANY] * len(outs),
        out_shape=outs,
        input_output_aliases=aliases,
        scratch_shapes=[pltpu.SemaphoreType.DMA((capacity, 2))],
        compiler_params=PARAMS,
        cost_estimate=cost or NO_COST,
    )(*operands)
    return results[0] if carried is None else results


def each_block(phases, choose, plan_ref, refs, act):
    number = 0
    for row, count, rows in phases:
        mine, refs = refs[: len(rows)], refs[len(rows) :]

        def run(ref, row_of, number=number, row=row, count=count):
            for k in range(count):
                panel = ref.at[k if row_of is None else plan_ref[row_of + k]]
                act(number + k, plan_ref[row + k], panel)

        if len(rows) == 1:
            run(mine[0], rows[0])
        else:
            first = plan_ref[choose] != 0
            pl.when(first)(functools.partial(run, mine[0], rows[0]))
            pl.when(jnp.logical_not(first))(functools.partial(run, mine[1], rows[1]))
        number += count


def split_phases(phases):
    shapes = [(row, count, [source[1] for source in sources]) for row, count, sources in phases]
    return shapes, [source[0] for _, _, sources in phases for source in sources]


def shrink_kernel(phases, choose, plan_ref, token_ref, *refs):
    out_ref = refs[-1]
    depth = token_ref.shape[2]

    def act(number, block, panel_ref):
        out_ref[number] = lax.dot_general(
            panel_ref[:, :depth],
            token_ref[block],
            (((1,), (1,)), ((), ())),
            preferred_element_type=jnp.float32,
        ).astype(out_ref.dtype)

    each_block(phases, choose, plan_ref, refs, act)


def shrink(plan, row_blocks, phases, choose, after=(), kind=jnp.float32, cost=None):
    shapes, panels = split_phases(phases)
    total = sum(count for _, count, _ in phases)
    shape = (total, panels[0].shape[1], row_blocks.shape[1])
    return pl.pallas_call(
        functools.partial(shrink_kernel, shapes, choose),
        in_specs=[SMEM] + [VMEM] * (1 + len(panels)) + [ANY] * len(after),
        out_specs=VMEM,
        out_shape=jax.ShapeDtypeStruct(shape, kind),
        compiler_params=PARAMS,
        cost_estimate=cost or NO_COST,
    )(plan, row_blocks, *panels, *after)


def exchange(part):
    return [part] + [swap(part, "tensor", m) for m in range(1, lax.axis_size("tensor"))]


def combine_kernel(phases, choose, part_count, live_row, plan_ref, *refs):
    parts = refs[:part_count]
    mine_ref, far_ref = refs[part_count : part_count + 2]
    out_ref, held_ref, sems = refs[-3:]
    total, block_rows, width = held_ref.shape

    def copy_of(number, block):
        rows = pl.ds(pl.multiple_of(block * block_rows, block_rows), block_rows)
        return pltpu.make_async_copy(held_ref.at[number], out_ref.at[rows], sems.at[number])

    def act(number, block, panel_ref):
        shrunk = parts[0][number].astype(jnp.float32)
        for part in parts[1:]:
            shrunk = shrunk + part[number].astype(jnp.float32)
        start = panel_ref.shape[1] - width
        delta = lax.dot_general(
            shrunk.astype(jnp.bfloat16),
            panel_ref[:, start : start + width],
            (((0,), (0,)), ((), ())),
            preferred_element_type=jnp.float32,
        )
        rows = pl.ds(pl.multiple_of(block * block_rows, block_rows), block_rows)
        row = lax.broadcasted_iota(jnp.int32, delta.shape, 0)
        value = mine_ref[rows, :] + far_ref[rows, :].astype(jnp.float32) + ADAPTER_SCALE * delta
        value = jnp.where(row < plan_ref[live_row + number], value, 0.0)
        held_ref[number] = value.astype(held_ref.dtype)
        copy_of(number, block).start()

    each_block(phases, choose, plan_ref, refs[part_count + 2 :], act)
    number = 0
    for row, count, _ in phases:
        for k in range(count):
            copy_of(number, plan_ref[row + k]).wait()
            number += 1


def combine(plan, live_row, parts, base, phases, choose, out=None, cost=None):
    block_rows = parts[0].shape[2]
    rows, width = base[0].shape
    shapes, panels = split_phases(phases)
    total = sum(count for _, count, _ in phases)
    operands = [*parts, *base, *panels]
    specs = [VMEM] * len(operands)
    aliases = {}
    if out is not None:
        specs.append(ANY)
        operands.append(out)
        aliases = {len(operands): 0}
    return pl.pallas_call(
        functools.partial(combine_kernel, shapes, choose, len(parts), live_row),
        in_specs=[SMEM] + specs,
        out_specs=ANY,
        out_shape=pltpu.HBM((rows, width), jnp.bfloat16),
        input_output_aliases=aliases,
        scratch_shapes=[
            pltpu.VMEM((total, block_rows, width), jnp.bfloat16),
            pltpu.SemaphoreType.DMA((total,)),
        ],
        compiler_params=PARAMS,
        cost_estimate=cost or NO_COST,
    )(plan, *operands)


def on_line_of_four(tokens, weight, row_blocks, down, up, names, table, live, capacity):
    def across(value, pairs):
        return lax.ppermute(value, "pool", pairs)

    others = [swap(names, "pool", m) for m in range(1, 4)]
    inner_up = across(up, [(0, 0), (1, 2), (2, 1), (3, 3)])
    inner_down = across(down, [(0, 0), (1, 2), (2, 1), (3, 3)])
    choose = INNER * capacity
    held = in_hbm(down), in_hbm(up)
    planning = [in_hbm(names), join(others), in_hbm(table), in_hbm(live), *held, capacity]
    *sent, kept, near_out, plan = base_parts(tokens, weight, up.shape[2], planning, [inner_up])

    def pack(choices, after, cost=None, carried=None):
        choices = [(row * capacity, *panels) for row, *panels in choices]
        return pack_panels(plan, choices, choose, capacity, after, cost, carried)

    near = across(near_out, [(0, 1), (1, 0), (2, 3), (3, 2)])
    base = base_sum(sent, kept)
    outer_out = pack([(TO_OUTER, *held)], [base[0]])
    to_outer = across(outer_out, [(0, 3), (1, 1), (2, 2), (3, 0)])
    late_out = pack(
        [(FORWARD, inner_down, inner_up), (TO_INNER, *held)], [outer_out], LONG
    )
    late = across(late_out, [(0, 2), (1, 0), (2, 3), (3, 1)])

    first = [(0, capacity, [(down, OWN * capacity)]), (capacity, capacity, [(near, None)])]
    first_up = [(0, capacity, [(up, OWN * capacity)]), first[1]]
    middle = [(2 * capacity, capacity, [(inner_down, ACROSS * capacity), (to_outer, None)])]
    middle_up = [(2 * capacity, capacity, [(inner_up, ACROSS * capacity), (to_outer, None)])]
    last = [(3 * capacity, capacity, [(late, None)])]

    def write(number, parts, phases, out, cost=None):
        live_row = (LIVE + number) * capacity
        return combine(plan, live_row, parts, base, phases, choose, out, cost)

    first_parts = exchange(shrink(plan, row_blocks, first, choose, [late_out]))
    out = write(0, first_parts, first_up, None, MIDDLE)
    middle_part = shrink(plan, row_blocks, middle, choose, [in_hbm(out)])
    middle_parts = exchange(middle_part)
    last_parts = exchange(shrink(plan, row_blocks, last, choose, [middle_part], jnp.bfloat16))
    out = write(2, middle_parts, middle_up, out)
    return write(3, last_parts, last, out)


def on_any_pool(tokens, weight, row_blocks, down, up, names, table, live, capacity):
    pool_size = lax.axis_size("pool")
    here = lax.axis_index("pool")
    holder_slots = down.shape[0]
    asked = table[lax.all_gather(names[0], "pool")]
    count = jnp.arange(capacity, dtype=jnp.int32)
    arrived = []
    for distance in range(pool_size):
        slots = asked[lax.rem(here + distance, pool_size)]
        hit = slots // holder_slots == here
        chosen = hit[None, :] & (jnp.cumsum(hit.astype(jnp.int32))[None, :] == 1 + count[:, None])
        plan = jnp.sum(jnp.where(chosen, (slots % holder_slots)[None, :], 0), axis=1)
        panels = pack_panels(plan, [(0, down, up)], 0, capacity)
        pairs = [(i, (i + distance) % pool_size) for i in range(pool_size)]
        arrived.append(lax.ppermute(panels, "pool", pairs) if distance else panels)
    arrived = jnp.concatenate(arrived)
    owners = asked[here] // holder_slots
    blocks = jnp.arange(owners.shape[0], dtype=jnp.int32)
    earlier = (owners[:, None] == owners[None, :]) & (blocks[:, None] > blocks[None, :])
    ranks = jnp.sum(earlier.astype(jnp.int32), axis=1)
    places = lax.rem(here - owners + pool_size, pool_size) * capacity + ranks
    plan = jnp.concatenate([blocks, places, live[0]])
    *sent, kept = base_parts(tokens, weight, up.shape[2])
    base = base_sum(sent, kept)
    phases = [(0, blocks.shape[0], [(arrived, blocks.shape[0])])]
    parts = exchange(shrink(plan, row_blocks, phases, 0))
    live_row = 2 * blocks.shape[0]
    return combine(plan, live_row, parts, base, phases, 0)


def on_device(
    tokens,
    value_weight,
    adapter_down_weight,
    adapter_up_weight,
    adapter_of_block,
    adapter_pool_slot,
    live_block_tokens,
):
    pool_size = lax.axis_size("pool")
    blocks = adapter_of_block.shape[1]
    capacity = -(-blocks // pool_size)
    row_blocks = tokens.reshape(blocks, tokens.shape[0] // blocks, tokens.shape[1])
    line = pool_size == 4 and blocks == capacity * pool_size
    route = on_line_of_four if line else on_any_pool
    return route(
        tokens,
        value_weight,
        row_blocks,
        jnp.transpose(adapter_down_weight, (0, 2, 1)),
        adapter_up_weight,
        adapter_of_block,
        adapter_pool_slot,
        live_block_tokens,
        capacity,
    )


def solution(mesh):
    return jax.shard_map(
        on_device,
        mesh=mesh,
        in_specs=(
            P(("groups", "pool"), "tensor"),
            P("tensor", None),
            P(("groups", "pool"), "tensor", None),
            P(("groups", "pool"), None, "tensor"),
            P(("groups", "pool"), None),
            P("groups"),
            P(("groups", "pool"), None),
        ),
        out_specs=P(("groups", "pool"), "tensor"),
        check_vma=False,
    )
```

```python
import functools

import jax
import jax.numpy as jnp
from jax import lax
from jax.experimental import pallas as pl
from jax.experimental.pallas import tpu as pltpu
from jax.sharding import PartitionSpec as P

ADAPTER_SCALE = 0.5
ROW_TILE = 256
PARAMS = pltpu.CompilerParams(vmem_limit_bytes=20 * 1024 * 1024)
NO_COST = pl.CostEstimate(flops=0, bytes_accessed=0, transcendentals=0)
BASE = pl.CostEstimate(flops=4 * 10**9, bytes_accessed=0, transcendentals=0)
SHORT = pl.CostEstimate(flops=2 * 10**9, bytes_accessed=0, transcendentals=0)
MIDDLE = pl.CostEstimate(flops=0 * 10**9, bytes_accessed=0, transcendentals=0)
LONG = pl.CostEstimate(flops=6 * 10**9, bytes_accessed=0, transcendentals=0)
ANY = pl.BlockSpec(memory_space=pl.ANY)
SMEM = pl.BlockSpec(memory_space=pltpu.SMEM)
VMEM = pl.BlockSpec(memory_space=pltpu.VMEM)


def in_hbm(value):
    return pltpu.with_memory_space_constraint(value, pltpu.HBM)


def swap(value, axis, distance):
    pairs = [(i, i ^ distance) for i in range(lax.axis_size(axis))]
    return lax.ppermute(value, axis, pairs)


def run_copies(copies):
    for copy in copies:
        copy.start()
    return copies


def piece_rows(rows):
    large = rows * 3 // 8
    return [large, large, rows - 2 * large]


def base_kernel(order, capacity, tokens_ref, weight_ref, *refs):
    if capacity:
        *asked, down_ref, up_ref = refs[:4]
        *scalars, scalar_sems, panel_sems = refs[-4:]
        near_ref, plan_ref, *held = refs[-9:-4]
        refs = [*refs[-13:-9], *held]
        loads = [
            pltpu.make_async_copy(source, scalar, scalar_sems.at[i])
            for i, (source, scalar) in enumerate(zip(asked, scalars))
        ]
        run_copies(loads)
    *sent_refs, kept_ref, tokens, weight, sems = refs
    half, rows, width = kept_ref.shape
    parts = sems.shape[1]
    tile, slab = rows // parts, weight.shape[0] // parts
    place = lax.axis_index("tensor")

    def copy_of(number, source, held, size, i):
        span = pl.ds(i * size, size)
        return pltpu.make_async_copy(source.at[span], held.at[span], sems.at[number, i])

    token_copies = [copy_of(0, tokens_ref, tokens, tile, i) for i in range(parts)]
    weight_copies = [copy_of(1, weight_ref, weight, slab, i) for i in range(parts)]

    def add(first, low, high, fresh):
        for number, offset in enumerate(order):
            columns = pl.ds(pl.multiple_of((place ^ offset) * width, width), width)
            part = jnp.dot(
                tokens[first : first + tile, low:high],
                weight[low:high, columns],
                preferred_element_type=jnp.float32,
            )
            if number >= half:
                targets = [(kept_ref, number - half, first, 0, tile)]
            else:
                targets, start = [], 0
                for sent_ref in sent_refs:
                    stop = start + sent_ref.shape[1]
                    above, below = max(first, start), min(first + tile, stop)
                    if above < below:
                        targets.append(
                            (sent_ref, number, above - start, above - first, below - above)
                        )
                    start = stop
            for ref, index, at, source, size in targets:
                value = part[source : source + size]
                if not fresh:
                    value = value + ref[index, at : at + size, :]
                ref[index, at : at + size, :] = value

    run_copies([token_copies[0], *weight_copies])
    packing = []
    if capacity:
        for load in loads:
            load.wait()
        packing = write_plan(
            capacity, scalars, down_ref, up_ref, near_ref, plan_ref, panel_sems
        )
    token_copies[0].wait()
    for i, copy in enumerate(weight_copies):
        copy.wait()
        if i == 0:
            run_copies(token_copies[1:])
        add(0, i * slab, (i + 1) * slab, i == 0)
    for i in range(1, parts):
        token_copies[i].wait()
        add(i * tile, 0, weight.shape[0], True)
    for copy in packing:
        copy.wait()


def base_chunks(tokens, weight, order, width, planning=None, after=()):
    rows = tokens.shape[0]
    half = len(order) // 2
    sizes = [*piece_rows(rows), rows]
    specs = [VMEM] * len(sizes)
    shapes = [jax.ShapeDtypeStruct((half, size, width), jnp.float32) for size in sizes]
    scratch = [
        pltpu.VMEM(tokens.shape, tokens.dtype),
        pltpu.VMEM(weight.shape, weight.dtype),
        pltpu.SemaphoreType.DMA((2, 4)),
    ]
    operands, capacity = [], 0
    if planning is not None:
        *operands, capacity = planning
        down, up = operands[-2:]
        specs += [ANY, SMEM]
        shapes += [
            jax.ShapeDtypeStruct((capacity, down.shape[1], down.shape[2] + width), down.dtype),
            jax.ShapeDtypeStruct((PLAN_ROWS * capacity,), jnp.int32),
        ]
        scratch += [pltpu.SMEM(operand.shape, operand.dtype) for operand in operands[:2]]
        scratch += [pltpu.SemaphoreType.DMA((2,)), pltpu.SemaphoreType.DMA((capacity, 2))]
    return pl.pallas_call(
        functools.partial(base_kernel, order, capacity),
        in_specs=[ANY] * (2 + len(operands) + len(after)),
        out_specs=specs,
        out_shape=shapes,
        scratch_shapes=scratch,
        compiler_params=PARAMS,
        cost_estimate=BASE,
    )(in_hbm(tokens), in_hbm(weight), *operands, *after)


def add_kernel(kept_ref, *refs):
    *arrived_refs, out_ref, mine_ref = refs
    half = kept_ref.shape[0] // 2
    start = 0
    for arrived_ref in arrived_refs:
        rows = pl.ds(start, arrived_ref.shape[1])
        for i in range(half):
            mine_ref[i, rows, :] = kept_ref[i, rows, :] + arrived_ref[i]
            out = kept_ref[half + i, rows, :] + arrived_ref[half + i]
            out_ref[i, rows, :] = out.astype(out_ref.dtype)
        start += arrived_ref.shape[1]


def add_halves(kept, arrived, sent_type):
    count, rows, width = kept.shape
    shape = (count // 2, rows, width)
    return pl.pallas_call(
        add_kernel,
        in_specs=[VMEM] * (1 + len(arrived)),
        out_shape=[
            jax.ShapeDtypeStruct(shape, sent_type),
            jax.ShapeDtypeStruct(shape, jnp.float32),
        ],
        compiler_params=PARAMS,
        cost_estimate=NO_COST,
    )(kept, *arrived)


def base_parts(tokens, weight, width, planning=None, after=()):
    size = lax.axis_size("tensor")
    kept_order = [k for k in range(size) if not k & 1]
    kept_order.sort(key=lambda k: [k >> bit & 1 for bit in range(1, size.bit_length())])
    return base_chunks(tokens, weight, [k ^ 1 for k in kept_order] + kept_order, width, planning, after)


def base_sum(sent, kept):
    arrived = [swap(piece, "tensor", 1) for piece in sent]
    distance = 2
    size = lax.axis_size("tensor")
    while distance < size:
        sent_type = jnp.bfloat16 if 2 * distance == size else jnp.float32
        sent, kept = add_halves(kept, arrived, sent_type)
        arrived = [swap(sent, "tensor", distance)]
        distance *= 2
    return kept[0], arrived[0][0]


def pick(asked_ref, index, holder, holder_slots, count):
    blocks = [jnp.int32(0)] * count
    slots = [jnp.int32(0)] * count
    seen = jnp.int32(0)
    for j in range(asked_ref.shape[1]):
        slot = asked_ref[index, j]
        hit = lax.div(slot, jnp.int32(holder_slots)) == holder
        for k in range(count):
            chosen = hit & (seen == k)
            blocks[k] = jnp.where(chosen, jnp.int32(j), blocks[k])
            slots[k] = jnp.where(chosen, lax.rem(slot, jnp.int32(holder_slots)), slots[k])
        seen = seen + hit.astype(jnp.int32)
    return blocks, slots


def panel_copies(k, slot, down_ref, up_ref, out_ref, sems):
    depth = down_ref.shape[2]
    width = up_ref.shape[2]
    return [
        pltpu.make_async_copy(down_ref.at[slot], out_ref.at[k, :, pl.ds(0, depth)], sems.at[k, 0]),
        pltpu.make_async_copy(up_ref.at[slot], out_ref.at[k, :, pl.ds(depth, width)], sems.at[k, 1]),
    ]


def write_plan(capacity, scalars, down_ref, up_ref, near_ref, plan_ref, sems):
    holder_slots = down_ref.shape[0]
    asked_ref, live_ref = scalars
    here = lax.axis_index("pool")
    find = functools.partial(
        pick, holder_slots=holder_slots, count=capacity
    )
    near_slots = find(asked_ref, 1, holder=here)[1]
    copies = []
    for k, slot in enumerate(near_slots):
        copies += run_copies(panel_copies(k, slot, down_ref, up_ref, near_ref, sems))
    inner = (here == 1) | (here == 2)
    own = find(asked_ref, 0, holder=here)
    near = find(asked_ref, 0, holder=here ^ 1)
    across = find(asked_ref, 0, holder=here ^ 3)
    late = find(asked_ref, 0, holder=here ^ 2)
    rows = [
        own[0],
        near[0],
        across[0],
        late[0],
        own[1],
        across[1],
        find(asked_ref, 2, holder=here)[1],
        find(asked_ref, 3, holder=here)[1],
        find(asked_ref, 1, holder=here ^ 3)[1],
        [inner.astype(jnp.int32)] * capacity,
        *[[live_ref[0, block] for block in phase[0]] for phase in (own, near, across, late)],
    ]
    for number, row in enumerate(rows):
        for k in range(capacity):
            plan_ref[number * capacity + k] = row[k]
    return copies


OWN, ACROSS, TO_INNER, TO_OUTER, FORWARD, INNER, LIVE, PLAN_ROWS = 4, 5, 6, 7, 8, 9, 10, 14


def pack_kernel(starts, choose, capacity, inputs, plan_ref, *refs):
    out_ref, sems = refs[inputs], refs[-1]

    def run(start, down_ref, up_ref):
        copies = []
        for k in range(capacity):
            slot = plan_ref[start + k]
            copies += run_copies(panel_copies(k, slot, down_ref, up_ref, out_ref, sems))
        for copy in copies:
            copy.wait()

    if len(starts) == 1:
        run(starts[0], *refs[:2])
    else:
        first = plan_ref[choose] != 0
        pl.when(first)(functools.partial(run, starts[0], *refs[:2]))
        pl.when(jnp.logical_not(first))(functools.partial(run, starts[1], *refs[2:4]))


def pack_panels(plan, choices, choose, capacity, after=(), cost=None, carried=None):
    sources = [a for _, *pair in choices for a in pair]
    rank, depth = sources[0].shape[1:]
    width = sources[1].shape[2]
    operands = [plan, *sources, *after]
    out = jax.ShapeDtypeStruct((capacity, rank, depth + width), sources[0].dtype)
    outs, aliases = [out], {}
    if carried is not None:
        aliases = {len(operands): 1}
        operands.append(carried)
        outs.append(jax.ShapeDtypeStruct(carried.shape, carried.dtype))
    results = pl.pallas_call(
        functools.partial(pack_kernel, [start for start, *_ in choices], choose, capacity, len(operands) - 1),
        in_specs=[SMEM] + [ANY] * (len(operands) - 1),
        out_specs=[ANY] * len(outs),
        out_shape=outs,
        input_output_aliases=aliases,
        scratch_shapes=[pltpu.SemaphoreType.DMA((capacity, 2))],
        compiler_params=PARAMS,
        cost_estimate=cost or NO_COST,
    )(*operands)
    return results[0] if carried is None else results


def each_block(phases, choose, plan_ref, refs, act):
    number = 0
    for row, count, rows in phases:
        mine, refs = refs[: len(rows)], refs[len(rows) :]

        def run(ref, row_of, number=number, row=row, count=count):
            for k in range(count):
                panel = ref.at[k if row_of is None else plan_ref[row_of + k]]
                act(number + k, plan_ref[row + k], panel)

        if len(rows) == 1:
            run(mine[0], rows[0])
        else:
            first = plan_ref[choose] != 0
            pl.when(first)(functools.partial(run, mine[0], rows[0]))
            pl.when(jnp.logical_not(first))(functools.partial(run, mine[1], rows[1]))
        number += count


def split_phases(phases):
    shapes = [(row, count, [source[1] for source in sources]) for row, count, sources in phases]
    return shapes, [source[0] for _, _, sources in phases for source in sources]


def shrink_kernel(phases, choose, plan_ref, token_ref, *refs):
    out_ref = refs[-1]
    depth = token_ref.shape[2]

    def act(number, block, panel_ref):
        out_ref[number] = lax.dot_general(
            panel_ref[:, :depth],
            token_ref[block],
            (((1,), (1,)), ((), ())),
            preferred_element_type=jnp.float32,
        ).astype(out_ref.dtype)

    each_block(phases, choose, plan_ref, refs, act)


def shrink(plan, row_blocks, phases, choose, after=(), kind=jnp.float32, cost=None):
    shapes, panels = split_phases(phases)
    total = sum(count for _, count, _ in phases)
    shape = (total, panels[0].shape[1], row_blocks.shape[1])
    return pl.pallas_call(
        functools.partial(shrink_kernel, shapes, choose),
        in_specs=[SMEM] + [VMEM] * (1 + len(panels)) + [ANY] * len(after),
        out_specs=VMEM,
        out_shape=jax.ShapeDtypeStruct(shape, kind),
        compiler_params=PARAMS,
        cost_estimate=cost or NO_COST,
    )(plan, row_blocks, *panels, *after)


def exchange(part):
    return [part] + [swap(part, "tensor", m) for m in range(1, lax.axis_size("tensor"))]


def combine_kernel(phases, choose, part_count, live_row, plan_ref, *refs):
    parts = refs[:part_count]
    mine_ref, far_ref = refs[part_count : part_count + 2]
    out_ref, held_ref, sems = refs[-3:]
    total, block_rows, width = held_ref.shape

    def copy_of(number, block):
        rows = pl.ds(pl.multiple_of(block * block_rows, block_rows), block_rows)
        return pltpu.make_async_copy(held_ref.at[number], out_ref.at[rows], sems.at[number])

    def act(number, block, panel_ref):
        shrunk = parts[0][number].astype(jnp.float32)
        for part in parts[1:]:
            shrunk = shrunk + part[number].astype(jnp.float32)
        start = panel_ref.shape[1] - width
        delta = lax.dot_general(
            shrunk.astype(jnp.bfloat16),
            panel_ref[:, start : start + width],
            (((0,), (0,)), ((), ())),
            preferred_element_type=jnp.float32,
        )
        rows = pl.ds(pl.multiple_of(block * block_rows, block_rows), block_rows)
        row = lax.broadcasted_iota(jnp.int32, delta.shape, 0)
        value = mine_ref[rows, :] + far_ref[rows, :].astype(jnp.float32) + ADAPTER_SCALE * delta
        value = jnp.where(row < plan_ref[live_row + number], value, 0.0)
        held_ref[number] = value.astype(held_ref.dtype)
        copy_of(number, block).start()

    each_block(phases, choose, plan_ref, refs[part_count + 2 :], act)
    number = 0
    for row, count, _ in phases:
        for k in range(count):
            copy_of(number, plan_ref[row + k]).wait()
            number += 1


def combine(plan, live_row, parts, base, phases, choose, out=None, cost=None):
    block_rows = parts[0].shape[2]
    rows, width = base[0].shape
    shapes, panels = split_phases(phases)
    total = sum(count for _, count, _ in phases)
    operands = [*parts, *base, *panels]
    specs = [VMEM] * len(operands)
    aliases = {}
    if out is not None:
        specs.append(ANY)
        operands.append(out)
        aliases = {len(operands): 0}
    return pl.pallas_call(
        functools.partial(combine_kernel, shapes, choose, len(parts), live_row),
        in_specs=[SMEM] + specs,
        out_specs=ANY,
        out_shape=pltpu.HBM((rows, width), jnp.bfloat16),
        input_output_aliases=aliases,
        scratch_shapes=[
            pltpu.VMEM((total, block_rows, width), jnp.bfloat16),
            pltpu.SemaphoreType.DMA((total,)),
        ],
        compiler_params=PARAMS,
        cost_estimate=cost or NO_COST,
    )(plan, *operands)


def on_line_of_four(tokens, weight, row_blocks, down, up, names, table, live, capacity):
    def across(value, pairs):
        return lax.ppermute(value, "pool", pairs)

    others = [swap(names, "pool", m) for m in range(1, 4)]
    inner_up = across(up, [(0, 0), (1, 2), (2, 1), (3, 3)])
    inner_down = across(down, [(0, 0), (1, 2), (2, 1), (3, 3)])
    choose = INNER * capacity
    held = in_hbm(down), in_hbm(up)
    asked = jnp.concatenate([names, *others])
    hits = asked[:, :, None] == jnp.arange(table.shape[0], dtype=jnp.int32)
    asked_slots = jnp.sum(jnp.where(hits, table, 0), axis=2)
    planning = [asked_slots, in_hbm(live), *held, capacity]
    *sent, kept, near_out, plan = base_parts(tokens, weight, up.shape[2], planning, [inner_up])

    def pack(choices, after, cost=None, carried=None):
        choices = [(row * capacity, *panels) for row, *panels in choices]
        return pack_panels(plan, choices, choose, capacity, after, cost, carried)

    near = across(near_out, [(0, 1), (1, 0), (2, 3), (3, 2)])
    base = base_sum(sent, kept)
    outer_out = pack([(TO_OUTER, *held)], [base[0]])
    to_outer = across(outer_out, [(0, 3), (1, 1), (2, 2), (3, 0)])
    late_out = pack(
        [(FORWARD, inner_down, inner_up), (TO_INNER, *held)], [outer_out], LONG
    )
    late = across(late_out, [(0, 2), (1, 0), (2, 3), (3, 1)])

    first = [(0, capacity, [(down, OWN * capacity)]), (capacity, capacity, [(near, None)])]
    first_up = [(0, capacity, [(up, OWN * capacity)]), first[1]]
    middle = [(2 * capacity, capacity, [(inner_down, ACROSS * capacity), (to_outer, None)])]
    middle_up = [(2 * capacity, capacity, [(inner_up, ACROSS * capacity), (to_outer, None)])]
    last = [(3 * capacity, capacity, [(late, None)])]

    def write(number, parts, phases, out, cost=None):
        live_row = (LIVE + number) * capacity
        return combine(plan, live_row, parts, base, phases, choose, out, cost)

    first_parts = exchange(shrink(plan, row_blocks, first, choose, [late_out]))
    out = write(0, first_parts, first_up, None, MIDDLE)
    middle_part = shrink(plan, row_blocks, middle, choose, [in_hbm(out)])
    middle_parts = exchange(middle_part)
    last_parts = exchange(shrink(plan, row_blocks, last, choose, [middle_part], jnp.bfloat16))
    out = write(2, middle_parts, middle_up, out)
    return write(3, last_parts, last, out)


def on_any_pool(tokens, weight, row_blocks, down, up, names, table, live, capacity):
    pool_size = lax.axis_size("pool")
    here = lax.axis_index("pool")
    holder_slots = down.shape[0]
    asked = table[lax.all_gather(names[0], "pool")]
    count = jnp.arange(capacity, dtype=jnp.int32)
    arrived = []
    for distance in range(pool_size):
        slots = asked[lax.rem(here + distance, pool_size)]
        hit = slots // holder_slots == here
        chosen = hit[None, :] & (jnp.cumsum(hit.astype(jnp.int32))[None, :] == 1 + count[:, None])
        plan = jnp.sum(jnp.where(chosen, (slots % holder_slots)[None, :], 0), axis=1)
        panels = pack_panels(plan, [(0, down, up)], 0, capacity)
        pairs = [(i, (i + distance) % pool_size) for i in range(pool_size)]
        arrived.append(lax.ppermute(panels, "pool", pairs) if distance else panels)
    arrived = jnp.concatenate(arrived)
    owners = asked[here] // holder_slots
    blocks = jnp.arange(owners.shape[0], dtype=jnp.int32)
    earlier = (owners[:, None] == owners[None, :]) & (blocks[:, None] > blocks[None, :])
    ranks = jnp.sum(earlier.astype(jnp.int32), axis=1)
    places = lax.rem(here - owners + pool_size, pool_size) * capacity + ranks
    plan = jnp.concatenate([blocks, places, live[0]])
    *sent, kept = base_parts(tokens, weight, up.shape[2])
    base = base_sum(sent, kept)
    phases = [(0, blocks.shape[0], [(arrived, blocks.shape[0])])]
    parts = exchange(shrink(plan, row_blocks, phases, 0))
    live_row = 2 * blocks.shape[0]
    return combine(plan, live_row, parts, base, phases, 0)


def on_device(
    tokens,
    value_weight,
    adapter_down_weight,
    adapter_up_weight,
    adapter_of_block,
    adapter_pool_slot,
    live_block_tokens,
):
    pool_size = lax.axis_size("pool")
    blocks = adapter_of_block.shape[1]
    capacity = -(-blocks // pool_size)
    row_blocks = tokens.reshape(blocks, tokens.shape[0] // blocks, tokens.shape[1])
    line = pool_size == 4 and blocks == capacity * pool_size
    route = on_line_of_four if line else on_any_pool
    return route(
        tokens,
        value_weight,
        row_blocks,
        jnp.transpose(adapter_down_weight, (0, 2, 1)),
        adapter_up_weight,
        adapter_of_block,
        adapter_pool_slot,
        live_block_tokens,
        capacity,
    )


def solution(mesh):
    return jax.shard_map(
        on_device,
        mesh=mesh,
        in_specs=(
            P(("groups", "pool"), "tensor"),
            P("tensor", None),
            P(("groups", "pool"), "tensor", None),
            P(("groups", "pool"), None, "tensor"),
            P(("groups", "pool"), None),
            P("groups"),
            P(("groups", "pool"), None),
        ),
        out_specs=P(("groups", "pool"), "tensor"),
        check_vma=False,
    )
```

```python
import functools

import jax
import jax.numpy as jnp
from jax import lax
from jax.experimental import pallas as pl
from jax.experimental.pallas import tpu as pltpu
from jax.sharding import PartitionSpec as P

ADAPTER_SCALE = 0.5
ROW_TILE = 256
PARAMS = pltpu.CompilerParams(vmem_limit_bytes=20 * 1024 * 1024)
NO_COST = pl.CostEstimate(flops=0, bytes_accessed=0, transcendentals=0)
BASE = pl.CostEstimate(flops=4 * 10**9, bytes_accessed=0, transcendentals=0)
SHORT = pl.CostEstimate(flops=10 * 10**9, bytes_accessed=0, transcendentals=0)
MIDDLE = pl.CostEstimate(flops=0 * 10**9, bytes_accessed=0, transcendentals=0)
LONG = pl.CostEstimate(flops=6 * 10**9, bytes_accessed=0, transcendentals=0)
ANY = pl.BlockSpec(memory_space=pl.ANY)
SMEM = pl.BlockSpec(memory_space=pltpu.SMEM)
VMEM = pl.BlockSpec(memory_space=pltpu.VMEM)


def in_hbm(value):
    return pltpu.with_memory_space_constraint(value, pltpu.HBM)


def swap(value, axis, distance):
    pairs = [(i, i ^ distance) for i in range(lax.axis_size(axis))]
    return lax.ppermute(value, axis, pairs)


def run_copies(copies):
    for copy in copies:
        copy.start()
    return copies


def piece_rows(rows):
    large = rows * 3 // 8
    return [large, large, rows - 2 * large]


def base_kernel(order, tokens_ref, weight_ref, *refs):
    *sent_refs, kept_ref, tokens, weight, sems = refs
    half, rows, width = kept_ref.shape
    parts = sems.shape[1]
    tile, slab = rows // parts, weight.shape[0] // parts
    place = lax.axis_index("tensor")

    def copy_of(number, source, held, size, i):
        span = pl.ds(i * size, size)
        return pltpu.make_async_copy(source.at[span], held.at[span], sems.at[number, i])

    token_copies = [copy_of(0, tokens_ref, tokens, tile, i) for i in range(parts)]
    weight_copies = [copy_of(1, weight_ref, weight, slab, i) for i in range(parts)]

    def add(first, low, high, fresh):
        for number, offset in enumerate(order):
            columns = pl.ds(pl.multiple_of((place ^ offset) * width, width), width)
            part = jnp.dot(
                tokens[first : first + tile, low:high],
                weight[low:high, columns],
                preferred_element_type=jnp.float32,
            )
            if number >= half:
                targets = [(kept_ref, number - half, first, 0, tile)]
            else:
                targets, start = [], 0
                for sent_ref in sent_refs:
                    stop = start + sent_ref.shape[1]
                    above, below = max(first, start), min(first + tile, stop)
                    if above < below:
                        targets.append(
                            (sent_ref, number, above - start, above - first, below - above)
                        )
                    start = stop
            for ref, index, at, source, size in targets:
                value = part[source : source + size]
                if not fresh:
                    value = value + ref[index, at : at + size, :]
                ref[index, at : at + size, :] = value

    run_copies([token_copies[0], *weight_copies])
    token_copies[0].wait()
    for i, copy in enumerate(weight_copies):
        copy.wait()
        if i == 0:
            run_copies(token_copies[1:])
        add(0, i * slab, (i + 1) * slab, i == 0)
    for copy in token_copies[1:]:
        copy.wait()
    for number, offset in enumerate(order):
        columns = pl.ds(pl.multiple_of((place ^ offset) * width, width), width)
        targets = [(kept_ref, number - half, 0)] if number >= half else []
        start = 0
        for sent_ref in sent_refs if number < half else []:
            targets.append((sent_ref, number, start))
            start += sent_ref.shape[1]
        for ref, index, start in targets:
            low, high = max(tile, start), start + ref.shape[1]
            ref[index, low - start :, :] = jnp.dot(
                tokens[low:high, :], weight[:, columns], preferred_element_type=jnp.float32
            )


def base_chunks(tokens, weight, order, width):
    rows = tokens.shape[0]
    half = len(order) // 2
    sizes = [*piece_rows(rows), rows]
    *sent, kept = pl.pallas_call(
        functools.partial(base_kernel, order),
        in_specs=[ANY] * 2,
        out_specs=[VMEM] * len(sizes),
        out_shape=[jax.ShapeDtypeStruct((half, size, width), jnp.float32) for size in sizes],
        scratch_shapes=[
            pltpu.VMEM(tokens.shape, tokens.dtype),
            pltpu.VMEM(weight.shape, weight.dtype),
            pltpu.SemaphoreType.DMA((2, 4)),
        ],
        compiler_params=PARAMS,
        cost_estimate=BASE,
    )(in_hbm(tokens), in_hbm(weight))
    return sent, kept


def add_kernel(kept_ref, *refs):
    *arrived_refs, out_ref, mine_ref = refs
    half = kept_ref.shape[0] // 2
    start = 0
    for arrived_ref in arrived_refs:
        rows = pl.ds(start, arrived_ref.shape[1])
        for i in range(half):
            mine_ref[i, rows, :] = kept_ref[i, rows, :] + arrived_ref[i]
            out = kept_ref[half + i, rows, :] + arrived_ref[half + i]
            out_ref[i, rows, :] = out.astype(out_ref.dtype)
        start += arrived_ref.shape[1]


def add_halves(kept, arrived, sent_type):
    count, rows, width = kept.shape
    shape = (count // 2, rows, width)
    return pl.pallas_call(
        add_kernel,
        in_specs=[VMEM] * (1 + len(arrived)),
        out_shape=[
            jax.ShapeDtypeStruct(shape, sent_type),
            jax.ShapeDtypeStruct(shape, jnp.float32),
        ],
        compiler_params=PARAMS,
        cost_estimate=NO_COST,
    )(kept, *arrived)


def base_parts(tokens, weight, width):
    size = lax.axis_size("tensor")
    kept_order = [k for k in range(size) if not k & 1]
    kept_order.sort(key=lambda k: [k >> bit & 1 for bit in range(1, size.bit_length())])
    return base_chunks(tokens, weight, [k ^ 1 for k in kept_order] + kept_order, width)


def base_sum(sent, kept):
    arrived = [swap(piece, "tensor", 1) for piece in sent]
    distance = 2
    size = lax.axis_size("tensor")
    while distance < size:
        sent_type = jnp.bfloat16 if 2 * distance == size else jnp.float32
        sent, kept = add_halves(kept, arrived, sent_type)
        arrived = [swap(sent, "tensor", distance)]
        distance *= 2
    return kept[0], arrived[0][0]


def pick(names_ref, table_ref, holder, holder_slots, count):
    blocks = [jnp.int32(0)] * count
    slots = [jnp.int32(0)] * count
    seen = jnp.int32(0)
    for j in range(names_ref.shape[1]):
        slot = table_ref[names_ref[0, j]]
        hit = lax.div(slot, jnp.int32(holder_slots)) == holder
        for k in range(count):
            chosen = hit & (seen == k)
            blocks[k] = jnp.where(chosen, jnp.int32(j), blocks[k])
            slots[k] = jnp.where(chosen, lax.rem(slot, jnp.int32(holder_slots)), slots[k])
        seen = seen + hit.astype(jnp.int32)
    return blocks, slots


def panel_copies(k, slot, down_ref, up_ref, out_ref, sems):
    depth = down_ref.shape[2]
    width = up_ref.shape[2]
    return [
        pltpu.make_async_copy(down_ref.at[slot], out_ref.at[k, :, pl.ds(0, depth)], sems.at[k, 0]),
        pltpu.make_async_copy(up_ref.at[slot], out_ref.at[k, :, pl.ds(depth, width)], sems.at[k, 1]),
    ]


def plan_kernel(capacity, *refs):
    sources, down_ref, up_ref = refs[:6], *refs[6:8]
    near_ref, plan_ref, *scalars, scalar_sems, sems = refs[-10:]
    holder_slots = down_ref.shape[0]
    loads = [
        pltpu.make_async_copy(source, scalar, scalar_sems.at[i])
        for i, (source, scalar) in enumerate(zip(sources, scalars))
    ]
    for load in run_copies(loads):
        load.wait()
    names_ref, first_ref, second_ref, third_ref, table_ref, live_ref = scalars
    here = lax.axis_index("pool")
    find = functools.partial(
        pick, table_ref=table_ref, holder_slots=holder_slots, count=capacity
    )
    near_slots = find(first_ref, holder=here)[1]
    copies = []
    for k, slot in enumerate(near_slots):
        copies += run_copies(panel_copies(k, slot, down_ref, up_ref, near_ref, sems))
    inner = (here == 1) | (here == 2)
    own = find(names_ref, holder=here)
    near = find(names_ref, holder=here ^ 1)
    across = find(names_ref, holder=here ^ 3)
    late = find(names_ref, holder=here ^ 2)
    rows = [
        own[0],
        near[0],
        across[0],
        late[0],
        own[1],
        across[1],
        find(second_ref, holder=here)[1],
        find(third_ref, holder=here)[1],
        find(first_ref, holder=here ^ 3)[1],
        [inner.astype(jnp.int32)] * capacity,
        *[[live_ref[0, block] for block in phase[0]] for phase in (own, near, across, late)],
    ]
    for number, row in enumerate(rows):
        for k in range(capacity):
            plan_ref[number * capacity + k] = row[k]
    for copy in copies:
        copy.wait()


OWN, ACROSS, TO_INNER, TO_OUTER, FORWARD, INNER, LIVE, PLAN_ROWS = 4, 5, 6, 7, 8, 9, 10, 14


def make_plan(names, others, table, live, down, up, capacity, after):
    rank, depth = down.shape[1:]
    return pl.pallas_call(
        functools.partial(plan_kernel, capacity),
        in_specs=[ANY] * (8 + len(after)),
        out_specs=[ANY, SMEM],
        out_shape=[
            jax.ShapeDtypeStruct((capacity, rank, depth + up.shape[2]), down.dtype),
            jax.ShapeDtypeStruct((PLAN_ROWS * capacity,), jnp.int32),
        ],
        scratch_shapes=[pltpu.SMEM(names.shape, jnp.int32)] * 4
        + [pltpu.SMEM(table.shape, jnp.int32), pltpu.SMEM(live.shape, jnp.int32)]
        + [pltpu.SemaphoreType.DMA((6,)), pltpu.SemaphoreType.DMA((capacity, 2))],
        compiler_params=PARAMS,
        cost_estimate=SHORT,
    )(in_hbm(names), *others, in_hbm(table), in_hbm(live), down, up, *after)


def pack_kernel(starts, choose, capacity, plan_ref, *refs):
    out_ref, sems = refs[-2:]

    def run(start, down_ref, up_ref):
        copies = []
        for k in range(capacity):
            slot = plan_ref[start + k]
            copies += run_copies(panel_copies(k, slot, down_ref, up_ref, out_ref, sems))
        for copy in copies:
            copy.wait()

    if len(starts) == 1:
        run(starts[0], *refs[:2])
    else:
        first = plan_ref[choose] != 0
        pl.when(first)(functools.partial(run, starts[0], *refs[:2]))
        pl.when(jnp.logical_not(first))(functools.partial(run, starts[1], *refs[2:4]))


def pack_panels(plan, choices, choose, capacity, after=(), cost=None):
    sources = [a for _, *pair in choices for a in pair]
    rank, depth = sources[0].shape[1:]
    width = sources[1].shape[2]
    return pl.pallas_call(
        functools.partial(pack_kernel, [start for start, *_ in choices], choose, capacity),
        in_specs=[SMEM] + [ANY] * (len(sources) + len(after)),
        out_specs=ANY,
        out_shape=jax.ShapeDtypeStruct((capacity, rank, depth + width), sources[0].dtype),
        scratch_shapes=[pltpu.SemaphoreType.DMA((capacity, 2))],
        compiler_params=PARAMS,
        cost_estimate=cost or NO_COST,
    )(plan, *sources, *after)


def each_block(phases, choose, plan_ref, refs, act):
    number = 0
    for row, count, rows in phases:
        mine, refs = refs[: len(rows)], refs[len(rows) :]

        def run(ref, row_of, number=number, row=row, count=count):
            for k in range(count):
                panel = ref.at[k if row_of is None else plan_ref[row_of + k]]
                act(number + k, plan_ref[row + k], panel)

        if len(rows) == 1:
            run(mine[0], rows[0])
        else:
            first = plan_ref[choose] != 0
            pl.when(first)(functools.partial(run, mine[0], rows[0]))
            pl.when(jnp.logical_not(first))(functools.partial(run, mine[1], rows[1]))
        number += count


def split_phases(phases):
    shapes = [(row, count, [source[1] for source in sources]) for row, count, sources in phases]
    return shapes, [source[0] for _, _, sources in phases for source in sources]


def shrink_kernel(phases, choose, plan_ref, token_ref, *refs):
    out_ref = refs[-1]
    depth = token_ref.shape[2]

    def act(number, block, panel_ref):
        out_ref[number] = lax.dot_general(
            panel_ref[:, :depth],
            token_ref[block],
            (((1,), (1,)), ((), ())),
            preferred_element_type=jnp.float32,
        ).astype(out_ref.dtype)

    each_block(phases, choose, plan_ref, refs, act)


def shrink(plan, row_blocks, phases, choose, after=(), kind=jnp.float32, cost=None):
    shapes, panels = split_phases(phases)
    total = sum(count for _, count, _ in phases)
    shape = (total, panels[0].shape[1], row_blocks.shape[1])
    return pl.pallas_call(
        functools.partial(shrink_kernel, shapes, choose),
        in_specs=[SMEM] + [VMEM] * (1 + len(panels)) + [ANY] * len(after),
        out_specs=VMEM,
        out_shape=jax.ShapeDtypeStruct(shape, kind),
        compiler_params=PARAMS,
        cost_estimate=cost or NO_COST,
    )(plan, row_blocks, *panels, *after)


def exchange(part):
    return [part] + [swap(part, "tensor", m) for m in range(1, lax.axis_size("tensor"))]


def combine_kernel(phases, choose, part_count, live_row, plan_ref, *refs):
    parts = refs[:part_count]
    mine_ref, far_ref = refs[part_count : part_count + 2]
    out_ref, held_ref, sems = refs[-3:]
    total, block_rows, width = held_ref.shape

    def copy_of(number, block):
        rows = pl.ds(pl.multiple_of(block * block_rows, block_rows), block_rows)
        return pltpu.make_async_copy(held_ref.at[number], out_ref.at[rows], sems.at[number])

    def act(number, block, panel_ref):
        shrunk = parts[0][number].astype(jnp.float32)
        for part in parts[1:]:
            shrunk = shrunk + part[number].astype(jnp.float32)
        start = panel_ref.shape[1] - width
        delta = lax.dot_general(
            shrunk.astype(jnp.bfloat16),
            panel_ref[:, start : start + width],
            (((0,), (0,)), ((), ())),
            preferred_element_type=jnp.float32,
        )
        rows = pl.ds(pl.multiple_of(block * block_rows, block_rows), block_rows)
        row = lax.broadcasted_iota(jnp.int32, delta.shape, 0)
        value = mine_ref[rows, :] + far_ref[rows, :].astype(jnp.float32) + ADAPTER_SCALE * delta
        value = jnp.where(row < plan_ref[live_row + number], value, 0.0)
        held_ref[number] = value.astype(held_ref.dtype)
        copy_of(number, block).start()

    each_block(phases, choose, plan_ref, refs[part_count + 2 :], act)
    number = 0
    for row, count, _ in phases:
        for k in range(count):
            copy_of(number, plan_ref[row + k]).wait()
            number += 1


def combine(plan, live_row, parts, base, phases, choose, out=None, cost=None):
    block_rows = parts[0].shape[2]
    rows, width = base[0].shape
    shapes, panels = split_phases(phases)
    total = sum(count for _, count, _ in phases)
    operands = [*parts, *base, *panels]
    specs = [VMEM] * len(operands)
    aliases = {}
    if out is not None:
        specs.append(ANY)
        operands.append(out)
        aliases = {len(operands): 0}
    return pl.pallas_call(
        functools.partial(combine_kernel, shapes, choose, len(parts), live_row),
        in_specs=[SMEM] + specs,
        out_specs=ANY,
        out_shape=pltpu.HBM((rows, width), jnp.bfloat16),
        input_output_aliases=aliases,
        scratch_shapes=[
            pltpu.VMEM((total, block_rows, width), jnp.bfloat16),
            pltpu.SemaphoreType.DMA((total,)),
        ],
        compiler_params=PARAMS,
        cost_estimate=cost or NO_COST,
    )(plan, *operands)


def on_line_of_four(tokens, weight, row_blocks, down, up, names, table, live, capacity):
    def across(value, pairs):
        return lax.ppermute(value, "pool", pairs)

    others = [swap(names, "pool", m) for m in range(1, 4)]
    inner_up = across(up, [(0, 0), (1, 2), (2, 1), (3, 3)])
    inner_down = across(down, [(0, 0), (1, 2), (2, 1), (3, 3)])
    sent, kept = base_parts(tokens, weight, up.shape[2])
    choose = INNER * capacity
    held = in_hbm(down), in_hbm(up)
    near_out, plan = make_plan(
        names, others, table, live, *held, capacity, [inner_up, sent[-1]]
    )

    def pack(choices, after, cost=None):
        choices = [(row * capacity, *panels) for row, *panels in choices]
        return pack_panels(plan, choices, choose, capacity, after, cost)

    near = across(near_out, [(0, 1), (1, 0), (2, 3), (3, 2)])
    base = base_sum(sent, kept)
    outer_out = pack([(TO_OUTER, *held)], [base[0]])
    to_outer = across(outer_out, [(0, 3), (1, 1), (2, 2), (3, 0)])
    late_out = pack(
        [(FORWARD, inner_down, inner_up), (TO_INNER, *held)], [outer_out], LONG
    )
    late = across(late_out, [(0, 2), (1, 0), (2, 3), (3, 1)])

    first = [(0, capacity, [(down, OWN * capacity)]), (capacity, capacity, [(near, None)])]
    first_up = [(0, capacity, [(up, OWN * capacity)]), first[1]]
    middle = [(2 * capacity, capacity, [(inner_down, ACROSS * capacity), (to_outer, None)])]
    middle_up = [(2 * capacity, capacity, [(inner_up, ACROSS * capacity), (to_outer, None)])]
    last = [(3 * capacity, capacity, [(late, None)])]

    def write(number, parts, phases, out, cost=None):
        live_row = (LIVE + number) * capacity
        return combine(plan, live_row, parts, base, phases, choose, out, cost)

    first_parts = exchange(shrink(plan, row_blocks, first, choose, [late_out]))
    out = write(0, first_parts, first_up, None, MIDDLE)
    middle_part = shrink(plan, row_blocks, middle, choose, [in_hbm(out)])
    middle_parts = exchange(middle_part)
    last_parts = exchange(shrink(plan, row_blocks, last, choose, [middle_part], jnp.bfloat16))
    out = write(2, middle_parts, middle_up, out)
    return write(3, last_parts, last, out)


def on_any_pool(tokens, weight, row_blocks, down, up, names, table, live, capacity):
    pool_size = lax.axis_size("pool")
    here = lax.axis_index("pool")
    holder_slots = down.shape[0]
    asked = table[lax.all_gather(names[0], "pool")]
    count = jnp.arange(capacity, dtype=jnp.int32)
    arrived = []
    for distance in range(pool_size):
        slots = asked[lax.rem(here + distance, pool_size)]
        hit = slots // holder_slots == here
        chosen = hit[None, :] & (jnp.cumsum(hit.astype(jnp.int32))[None, :] == 1 + count[:, None])
        plan = jnp.sum(jnp.where(chosen, (slots % holder_slots)[None, :], 0), axis=1)
        panels = pack_panels(plan, [(0, down, up)], 0, capacity)
        pairs = [(i, (i + distance) % pool_size) for i in range(pool_size)]
        arrived.append(lax.ppermute(panels, "pool", pairs) if distance else panels)
    arrived = jnp.concatenate(arrived)
    owners = asked[here] // holder_slots
    blocks = jnp.arange(owners.shape[0], dtype=jnp.int32)
    earlier = (owners[:, None] == owners[None, :]) & (blocks[:, None] > blocks[None, :])
    ranks = jnp.sum(earlier.astype(jnp.int32), axis=1)
    places = lax.rem(here - owners + pool_size, pool_size) * capacity + ranks
    plan = jnp.concatenate([blocks, places, live[0]])
    base = base_sum(*base_parts(tokens, weight, up.shape[2]))
    phases = [(0, blocks.shape[0], [(arrived, blocks.shape[0])])]
    parts = exchange(shrink(plan, row_blocks, phases, 0))
    live_row = 2 * blocks.shape[0]
    return combine(plan, live_row, parts, base, phases, 0)


def on_device(
    tokens,
    value_weight,
    adapter_down_weight,
    adapter_up_weight,
    adapter_of_block,
    adapter_pool_slot,
    live_block_tokens,
):
    pool_size = lax.axis_size("pool")
    blocks = adapter_of_block.shape[1]
    capacity = -(-blocks // pool_size)
    row_blocks = tokens.reshape(blocks, tokens.shape[0] // blocks, tokens.shape[1])
    line = pool_size == 4 and blocks == capacity * pool_size
    route = on_line_of_four if line else on_any_pool
    return route(
        tokens,
        value_weight,
        row_blocks,
        jnp.transpose(adapter_down_weight, (0, 2, 1)),
        adapter_up_weight,
        adapter_of_block,
        adapter_pool_slot,
        live_block_tokens,
        capacity,
    )


def solution(mesh):
    return jax.shard_map(
        on_device,
        mesh=mesh,
        in_specs=(
            P(("groups", "pool"), "tensor"),
            P("tensor", None),
            P(("groups", "pool"), "tensor", None),
            P(("groups", "pool"), None, "tensor"),
            P(("groups", "pool"), None),
            P("groups"),
            P(("groups", "pool"), None),
        ),
        out_specs=P(("groups", "pool"), "tensor"),
        check_vma=False,
    )
```

```python
import functools

import jax
import jax.numpy as jnp
from jax import lax
from jax.experimental import pallas as pl
from jax.experimental.pallas import tpu as pltpu
from jax.sharding import PartitionSpec as P

ADAPTER_SCALE = 0.5
ROW_TILE = 256
PANEL_PIECES = 4
PARAMS = pltpu.CompilerParams(vmem_limit_bytes=20 * 1024 * 1024)
NO_COST = pl.CostEstimate(flops=0, bytes_accessed=0, transcendentals=0)
BASE = pl.CostEstimate(flops=4 * 10**9, bytes_accessed=0, transcendentals=0)
SHORT = pl.CostEstimate(flops=10 * 10**9, bytes_accessed=0, transcendentals=0)
MIDDLE = pl.CostEstimate(flops=0 * 10**9, bytes_accessed=0, transcendentals=0)
LONG = pl.CostEstimate(flops=6 * 10**9, bytes_accessed=0, transcendentals=0)
ANY = pl.BlockSpec(memory_space=pl.ANY)
SMEM = pl.BlockSpec(memory_space=pltpu.SMEM)
VMEM = pl.BlockSpec(memory_space=pltpu.VMEM)


def in_hbm(value):
    return pltpu.with_memory_space_constraint(value, pltpu.HBM)


def swap(value, axis, distance):
    pairs = [(i, i ^ distance) for i in range(lax.axis_size(axis))]
    return lax.ppermute(value, axis, pairs)


def run_copies(copies):
    for copy in copies:
        copy.start()
    return copies


def piece_rows(rows):
    large = rows * 3 // 8
    return [large, large, rows - 2 * large]


def base_kernel(order, tokens_ref, weight_ref, *refs):
    *sent_refs, kept_ref, tokens, weight, sems = refs
    half, rows, width = kept_ref.shape
    parts = sems.shape[1]
    tile, slab = rows // parts, weight.shape[0] // parts
    place = lax.axis_index("tensor")

    def copy_of(number, source, held, size, i):
        span = pl.ds(i * size, size)
        return pltpu.make_async_copy(source.at[span], held.at[span], sems.at[number, i])

    token_copies = [copy_of(0, tokens_ref, tokens, tile, i) for i in range(parts)]
    weight_copies = [copy_of(1, weight_ref, weight, slab, i) for i in range(parts)]

    def add(first, low, high, fresh):
        for number, offset in enumerate(order):
            columns = pl.ds(pl.multiple_of((place ^ offset) * width, width), width)
            part = jnp.dot(
                tokens[first : first + tile, low:high],
                weight[low:high, columns],
                preferred_element_type=jnp.float32,
            )
            if number >= half:
                targets = [(kept_ref, number - half, first, 0, tile)]
            else:
                targets, start = [], 0
                for sent_ref in sent_refs:
                    stop = start + sent_ref.shape[1]
                    above, below = max(first, start), min(first + tile, stop)
                    if above < below:
                        targets.append(
                            (sent_ref, number, above - start, above - first, below - above)
                        )
                    start = stop
            for ref, index, at, source, size in targets:
                value = part[source : source + size]
                if not fresh:
                    value = value + ref[index, at : at + size, :]
                ref[index, at : at + size, :] = value

    run_copies([token_copies[0], *weight_copies])
    token_copies[0].wait()
    for i, copy in enumerate(weight_copies):
        copy.wait()
        if i == 0:
            run_copies(token_copies[1:])
        add(0, i * slab, (i + 1) * slab, i == 0)
    for i in range(1, parts):
        token_copies[i].wait()
        add(i * tile, 0, weight.shape[0], True)


def base_chunks(tokens, weight, order, width):
    rows = tokens.shape[0]
    half = len(order) // 2
    sizes = [*piece_rows(rows), rows]
    *sent, kept = pl.pallas_call(
        functools.partial(base_kernel, order),
        in_specs=[ANY] * 2,
        out_specs=[VMEM] * len(sizes),
        out_shape=[jax.ShapeDtypeStruct((half, size, width), jnp.float32) for size in sizes],
        scratch_shapes=[
            pltpu.VMEM(tokens.shape, tokens.dtype),
            pltpu.VMEM(weight.shape, weight.dtype),
            pltpu.SemaphoreType.DMA((2, 4)),
        ],
        compiler_params=PARAMS,
        cost_estimate=BASE,
    )(in_hbm(tokens), in_hbm(weight))
    return sent, kept


def add_kernel(kept_ref, *refs):
    *arrived_refs, out_ref, mine_ref = refs
    half = kept_ref.shape[0] // 2
    start = 0
    for arrived_ref in arrived_refs:
        rows = pl.ds(start, arrived_ref.shape[1])
        for i in range(half):
            mine_ref[i, rows, :] = kept_ref[i, rows, :] + arrived_ref[i]
            out = kept_ref[half + i, rows, :] + arrived_ref[half + i]
            out_ref[i, rows, :] = out.astype(out_ref.dtype)
        start += arrived_ref.shape[1]


def add_halves(kept, arrived, sent_type):
    count, rows, width = kept.shape
    shape = (count // 2, rows, width)
    return pl.pallas_call(
        add_kernel,
        in_specs=[VMEM] * (1 + len(arrived)),
        out_shape=[
            jax.ShapeDtypeStruct(shape, sent_type),
            jax.ShapeDtypeStruct(shape, jnp.float32),
        ],
        compiler_params=PARAMS,
        cost_estimate=NO_COST,
    )(kept, *arrived)


def base_parts(tokens, weight, width):
    size = lax.axis_size("tensor")
    kept_order = [k for k in range(size) if not k & 1]
    kept_order.sort(key=lambda k: [k >> bit & 1 for bit in range(1, size.bit_length())])
    return base_chunks(tokens, weight, [k ^ 1 for k in kept_order] + kept_order, width)


def base_sum(sent, kept):
    arrived = [swap(piece, "tensor", 1) for piece in sent]
    distance = 2
    size = lax.axis_size("tensor")
    while distance < size:
        sent_type = jnp.bfloat16 if 2 * distance == size else jnp.float32
        sent, kept = add_halves(kept, arrived, sent_type)
        arrived = [swap(sent, "tensor", distance)]
        distance *= 2
    return kept[0], arrived[0][0]


def pick(names_ref, table_ref, holder, holder_slots, count):
    blocks = [jnp.int32(0)] * count
    slots = [jnp.int32(0)] * count
    seen = jnp.int32(0)
    for j in range(names_ref.shape[1]):
        slot = table_ref[names_ref[0, j]]
        hit = lax.div(slot, jnp.int32(holder_slots)) == holder
        for k in range(count):
            chosen = hit & (seen == k)
            blocks[k] = jnp.where(chosen, jnp.int32(j), blocks[k])
            slots[k] = jnp.where(chosen, lax.rem(slot, jnp.int32(holder_slots)), slots[k])
        seen = seen + hit.astype(jnp.int32)
    return blocks, slots


def panel_copies(k, slot, down_ref, up_ref, out_ref, sems):
    depth = down_ref.shape[2]
    width = up_ref.shape[2]
    rows = down_ref.shape[1] // PANEL_PIECES
    copies = []
    for i in range(PANEL_PIECES):
        part = pl.ds(i * rows, rows)
        copies.append(
            pltpu.make_async_copy(
                down_ref.at[slot, part], out_ref.at[k, part, pl.ds(0, depth)], sems.at[k, i]
            )
        )
    copies.append(
        pltpu.make_async_copy(
            up_ref.at[slot], out_ref.at[k, :, pl.ds(depth, width)], sems.at[k, PANEL_PIECES]
        )
    )
    return copies


def plan_kernel(capacity, *refs):
    sources, down_ref, up_ref = refs[:6], *refs[6:8]
    near_ref, plan_ref, *scalars, scalar_sems, sems = refs[-10:]
    holder_slots = down_ref.shape[0]
    loads = [
        pltpu.make_async_copy(source, scalar, scalar_sems.at[i])
        for i, (source, scalar) in enumerate(zip(sources, scalars))
    ]
    for load in run_copies(loads):
        load.wait()
    names_ref, first_ref, second_ref, third_ref, table_ref, live_ref = scalars
    here = lax.axis_index("pool")
    find = functools.partial(
        pick, table_ref=table_ref, holder_slots=holder_slots, count=capacity
    )
    near_slots = find(first_ref, holder=here)[1]
    copies = []
    for k, slot in enumerate(near_slots):
        copies += run_copies(panel_copies(k, slot, down_ref, up_ref, near_ref, sems))
    inner = (here == 1) | (here == 2)
    own = find(names_ref, holder=here)
    near = find(names_ref, holder=here ^ 1)
    across = find(names_ref, holder=here ^ 3)
    late = find(names_ref, holder=here ^ 2)
    rows = [
        own[0],
        near[0],
        across[0],
        late[0],
        own[1],
        across[1],
        find(second_ref, holder=here)[1],
        find(third_ref, holder=here)[1],
        find(first_ref, holder=here ^ 3)[1],
        [inner.astype(jnp.int32)] * capacity,
        *[[live_ref[0, block] for block in phase[0]] for phase in (own, near, across, late)],
    ]
    for number, row in enumerate(rows):
        for k in range(capacity):
            plan_ref[number * capacity + k] = row[k]
    for copy in copies:
        copy.wait()


OWN, ACROSS, TO_INNER, TO_OUTER, FORWARD, INNER, LIVE, PLAN_ROWS = 4, 5, 6, 7, 8, 9, 10, 14


def make_plan(names, others, table, live, down, up, capacity, after):
    rank, depth = down.shape[1:]
    return pl.pallas_call(
        functools.partial(plan_kernel, capacity),
        in_specs=[ANY] * (8 + len(after)),
        out_specs=[ANY, SMEM],
        out_shape=[
            jax.ShapeDtypeStruct((capacity, rank, depth + up.shape[2]), down.dtype),
            jax.ShapeDtypeStruct((PLAN_ROWS * capacity,), jnp.int32),
        ],
        scratch_shapes=[pltpu.SMEM(names.shape, jnp.int32)] * 4
        + [pltpu.SMEM(table.shape, jnp.int32), pltpu.SMEM(live.shape, jnp.int32)]
        + [pltpu.SemaphoreType.DMA((6,)), pltpu.SemaphoreType.DMA((capacity, PANEL_PIECES + 1))],
        compiler_params=PARAMS,
        cost_estimate=SHORT,
    )(in_hbm(names), *others, in_hbm(table), in_hbm(live), down, up, *after)


def pack_kernel(starts, choose, capacity, plan_ref, *refs):
    out_ref, sems = refs[-2:]

    def run(start, down_ref, up_ref):
        copies = []
        for k in range(capacity):
            slot = plan_ref[start + k]
            copies += run_copies(panel_copies(k, slot, down_ref, up_ref, out_ref, sems))
        for copy in copies:
            copy.wait()

    if len(starts) == 1:
        run(starts[0], *refs[:2])
    else:
        first = plan_ref[choose] != 0
        pl.when(first)(functools.partial(run, starts[0], *refs[:2]))
        pl.when(jnp.logical_not(first))(functools.partial(run, starts[1], *refs[2:4]))


def pack_panels(plan, choices, choose, capacity, after=(), cost=None):
    sources = [a for _, *pair in choices for a in pair]
    rank, depth = sources[0].shape[1:]
    width = sources[1].shape[2]
    return pl.pallas_call(
        functools.partial(pack_kernel, [start for start, *_ in choices], choose, capacity),
        in_specs=[SMEM] + [ANY] * (len(sources) + len(after)),
        out_specs=ANY,
        out_shape=jax.ShapeDtypeStruct((capacity, rank, depth + width), sources[0].dtype),
        scratch_shapes=[pltpu.SemaphoreType.DMA((capacity, PANEL_PIECES + 1))],
        compiler_params=PARAMS,
        cost_estimate=cost or NO_COST,
    )(plan, *sources, *after)


def each_block(phases, choose, plan_ref, refs, act):
    number = 0
    for row, count, rows in phases:
        mine, refs = refs[: len(rows)], refs[len(rows) :]

        def run(ref, row_of, number=number, row=row, count=count):
            for k in range(count):
                panel = ref.at[k if row_of is None else plan_ref[row_of + k]]
                act(number + k, plan_ref[row + k], panel)

        if len(rows) == 1:
            run(mine[0], rows[0])
        else:
            first = plan_ref[choose] != 0
            pl.when(first)(functools.partial(run, mine[0], rows[0]))
            pl.when(jnp.logical_not(first))(functools.partial(run, mine[1], rows[1]))
        number += count


def split_phases(phases):
    shapes = [(row, count, [source[1] for source in sources]) for row, count, sources in phases]
    return shapes, [source[0] for _, _, sources in phases for source in sources]


def shrink_kernel(phases, choose, plan_ref, token_ref, *refs):
    out_ref = refs[-1]
    depth = token_ref.shape[2]

    def act(number, block, panel_ref):
        out_ref[number] = lax.dot_general(
            panel_ref[:, :depth],
            token_ref[block],
            (((1,), (1,)), ((), ())),
            preferred_element_type=jnp.float32,
        ).astype(out_ref.dtype)

    each_block(phases, choose, plan_ref, refs, act)


def shrink(plan, row_blocks, phases, choose, after=(), kind=jnp.float32, cost=None):
    shapes, panels = split_phases(phases)
    total = sum(count for _, count, _ in phases)
    shape = (total, panels[0].shape[1], row_blocks.shape[1])
    return pl.pallas_call(
        functools.partial(shrink_kernel, shapes, choose),
        in_specs=[SMEM] + [VMEM] * (1 + len(panels)) + [ANY] * len(after),
        out_specs=VMEM,
        out_shape=jax.ShapeDtypeStruct(shape, kind),
        compiler_params=PARAMS,
        cost_estimate=cost or NO_COST,
    )(plan, row_blocks, *panels, *after)


def exchange(part):
    return [part] + [swap(part, "tensor", m) for m in range(1, lax.axis_size("tensor"))]


def combine_kernel(phases, choose, part_count, live_row, plan_ref, *refs):
    parts = refs[:part_count]
    mine_ref, far_ref = refs[part_count : part_count + 2]
    out_ref, held_ref, sems = refs[-3:]
    total, block_rows, width = held_ref.shape

    def copy_of(number, block):
        rows = pl.ds(pl.multiple_of(block * block_rows, block_rows), block_rows)
        return pltpu.make_async_copy(held_ref.at[number], out_ref.at[rows], sems.at[number])

    def act(number, block, panel_ref):
        shrunk = parts[0][number].astype(jnp.float32)
        for part in parts[1:]:
            shrunk = shrunk + part[number].astype(jnp.float32)
        start = panel_ref.shape[1] - width
        delta = lax.dot_general(
            shrunk.astype(jnp.bfloat16),
            panel_ref[:, start : start + width],
            (((0,), (0,)), ((), ())),
            preferred_element_type=jnp.float32,
        )
        rows = pl.ds(pl.multiple_of(block * block_rows, block_rows), block_rows)
        row = lax.broadcasted_iota(jnp.int32, delta.shape, 0)
        value = mine_ref[rows, :] + far_ref[rows, :].astype(jnp.float32) + ADAPTER_SCALE * delta
        value = jnp.where(row < plan_ref[live_row + number], value, 0.0)
        held_ref[number] = value.astype(held_ref.dtype)
        copy_of(number, block).start()

    each_block(phases, choose, plan_ref, refs[part_count + 2 :], act)
    number = 0
    for row, count, _ in phases:
        for k in range(count):
            copy_of(number, plan_ref[row + k]).wait()
            number += 1


def combine(plan, live_row, parts, base, phases, choose, out=None, cost=None):
    block_rows = parts[0].shape[2]
    rows, width = base[0].shape
    shapes, panels = split_phases(phases)
    total = sum(count for _, count, _ in phases)
    operands = [*parts, *base, *panels]
    specs = [VMEM] * len(operands)
    aliases = {}
    if out is not None:
        specs.append(ANY)
        operands.append(out)
        aliases = {len(operands): 0}
    return pl.pallas_call(
        functools.partial(combine_kernel, shapes, choose, len(parts), live_row),
        in_specs=[SMEM] + specs,
        out_specs=ANY,
        out_shape=pltpu.HBM((rows, width), jnp.bfloat16),
        input_output_aliases=aliases,
        scratch_shapes=[
            pltpu.VMEM((total, block_rows, width), jnp.bfloat16),
            pltpu.SemaphoreType.DMA((total,)),
        ],
        compiler_params=PARAMS,
        cost_estimate=cost or NO_COST,
    )(plan, *operands)


def on_line_of_four(tokens, weight, row_blocks, down, up, names, table, live, capacity):
    def across(value, pairs):
        return lax.ppermute(value, "pool", pairs)

    others = [swap(names, "pool", m) for m in range(1, 4)]
    inner_up = across(up, [(0, 0), (1, 2), (2, 1), (3, 3)])
    inner_down = across(down, [(0, 0), (1, 2), (2, 1), (3, 3)])
    sent, kept = base_parts(tokens, weight, up.shape[2])
    choose = INNER * capacity
    held = in_hbm(down), in_hbm(up)
    near_out, plan = make_plan(
        names, others, table, live, *held, capacity, [inner_up, sent[-1]]
    )

    def pack(choices, after, cost=None):
        choices = [(row * capacity, *panels) for row, *panels in choices]
        return pack_panels(plan, choices, choose, capacity, after, cost)

    near = across(near_out, [(0, 1), (1, 0), (2, 3), (3, 2)])
    base = base_sum(sent, kept)
    outer_out = pack([(TO_OUTER, *held)], [base[0]])
    to_outer = across(outer_out, [(0, 3), (1, 1), (2, 2), (3, 0)])
    late_out = pack(
        [(FORWARD, inner_down, inner_up), (TO_INNER, *held)], [outer_out], LONG
    )
    late = across(late_out, [(0, 2), (1, 0), (2, 3), (3, 1)])

    first = [(0, capacity, [(down, OWN * capacity)]), (capacity, capacity, [(near, None)])]
    first_up = [(0, capacity, [(up, OWN * capacity)]), first[1]]
    middle = [(2 * capacity, capacity, [(inner_down, ACROSS * capacity), (to_outer, None)])]
    middle_up = [(2 * capacity, capacity, [(inner_up, ACROSS * capacity), (to_outer, None)])]
    last = [(3 * capacity, capacity, [(late, None)])]

    def write(number, parts, phases, out, cost=None):
        live_row = (LIVE + number) * capacity
        return combine(plan, live_row, parts, base, phases, choose, out, cost)

    first_parts = exchange(shrink(plan, row_blocks, first, choose, [late_out]))
    out = write(0, first_parts, first_up, None, MIDDLE)
    middle_part = shrink(plan, row_blocks, middle, choose, [in_hbm(out)])
    middle_parts = exchange(middle_part)
    last_parts = exchange(shrink(plan, row_blocks, last, choose, [middle_part], jnp.bfloat16))
    out = write(2, middle_parts, middle_up, out)
    return write(3, last_parts, last, out)


def on_any_pool(tokens, weight, row_blocks, down, up, names, table, live, capacity):
    pool_size = lax.axis_size("pool")
    here = lax.axis_index("pool")
    holder_slots = down.shape[0]
    asked = table[lax.all_gather(names[0], "pool")]
    count = jnp.arange(capacity, dtype=jnp.int32)
    arrived = []
    for distance in range(pool_size):
        slots = asked[lax.rem(here + distance, pool_size)]
        hit = slots // holder_slots == here
        chosen = hit[None, :] & (jnp.cumsum(hit.astype(jnp.int32))[None, :] == 1 + count[:, None])
        plan = jnp.sum(jnp.where(chosen, (slots % holder_slots)[None, :], 0), axis=1)
        panels = pack_panels(plan, [(0, down, up)], 0, capacity)
        pairs = [(i, (i + distance) % pool_size) for i in range(pool_size)]
        arrived.append(lax.ppermute(panels, "pool", pairs) if distance else panels)
    arrived = jnp.concatenate(arrived)
    owners = asked[here] // holder_slots
    blocks = jnp.arange(owners.shape[0], dtype=jnp.int32)
    earlier = (owners[:, None] == owners[None, :]) & (blocks[:, None] > blocks[None, :])
    ranks = jnp.sum(earlier.astype(jnp.int32), axis=1)
    places = lax.rem(here - owners + pool_size, pool_size) * capacity + ranks
    plan = jnp.concatenate([blocks, places, live[0]])
    base = base_sum(*base_parts(tokens, weight, up.shape[2]))
    phases = [(0, blocks.shape[0], [(arrived, blocks.shape[0])])]
    parts = exchange(shrink(plan, row_blocks, phases, 0))
    live_row = 2 * blocks.shape[0]
    return combine(plan, live_row, parts, base, phases, 0)


def on_device(
    tokens,
    value_weight,
    adapter_down_weight,
    adapter_up_weight,
    adapter_of_block,
    adapter_pool_slot,
    live_block_tokens,
):
    pool_size = lax.axis_size("pool")
    blocks = adapter_of_block.shape[1]
    capacity = -(-blocks // pool_size)
    row_blocks = tokens.reshape(blocks, tokens.shape[0] // blocks, tokens.shape[1])
    line = pool_size == 4 and blocks == capacity * pool_size
    route = on_line_of_four if line else on_any_pool
    return route(
        tokens,
        value_weight,
        row_blocks,
        jnp.transpose(adapter_down_weight, (0, 2, 1)),
        adapter_up_weight,
        adapter_of_block,
        adapter_pool_slot,
        live_block_tokens,
        capacity,
    )


def solution(mesh):
    return jax.shard_map(
        on_device,
        mesh=mesh,
        in_specs=(
            P(("groups", "pool"), "tensor"),
            P("tensor", None),
            P(("groups", "pool"), "tensor", None),
            P(("groups", "pool"), None, "tensor"),
            P(("groups", "pool"), None),
            P("groups"),
            P(("groups", "pool"), None),
        ),
        out_specs=P(("groups", "pool"), "tensor"),
        check_vma=False,
    )
```

```python
import functools

import jax
import jax.numpy as jnp
from jax import lax
from jax.experimental import pallas as pl
from jax.experimental.pallas import tpu as pltpu
from jax.sharding import PartitionSpec as P

ADAPTER_SCALE = 0.5
ROW_TILE = 256
PARAMS = pltpu.CompilerParams(vmem_limit_bytes=20 * 1024 * 1024)
NO_COST = pl.CostEstimate(flops=0, bytes_accessed=0, transcendentals=0)
BASE = pl.CostEstimate(flops=4 * 10**9, bytes_accessed=0, transcendentals=0)
SHORT = pl.CostEstimate(flops=10 * 10**9, bytes_accessed=0, transcendentals=0)
MIDDLE = pl.CostEstimate(flops=0 * 10**9, bytes_accessed=0, transcendentals=0)
LONG = pl.CostEstimate(flops=6 * 10**9, bytes_accessed=0, transcendentals=0)
ANY = pl.BlockSpec(memory_space=pl.ANY)
SMEM = pl.BlockSpec(memory_space=pltpu.SMEM)
VMEM = pl.BlockSpec(memory_space=pltpu.VMEM)


def in_hbm(value):
    return pltpu.with_memory_space_constraint(value, pltpu.HBM)


def swap(value, axis, distance):
    pairs = [(i, i ^ distance) for i in range(lax.axis_size(axis))]
    return lax.ppermute(value, axis, pairs)


def run_copies(copies):
    for copy in copies:
        copy.start()
    return copies


def piece_rows(rows):
    large = rows * 3 // 8
    return [large, large, rows - 2 * large]


def base_kernel(order, tokens_ref, weight_ref, *refs):
    *sent_refs, kept_ref, tokens, weight, sems = refs
    half, rows, width = kept_ref.shape
    parts = sems.shape[1]
    tile, slab = rows // parts, weight.shape[0] // parts
    place = lax.axis_index("tensor")

    def copy_of(number, source, held, size, i):
        span = pl.ds(i * size, size)
        return pltpu.make_async_copy(source.at[span], held.at[span], sems.at[number, i])

    token_copies = [copy_of(0, tokens_ref, tokens, tile, i) for i in range(parts)]
    weight_copies = [copy_of(1, weight_ref, weight, slab, i) for i in range(parts)]

    def add(first, low, high, fresh):
        for number, offset in enumerate(order):
            columns = pl.ds(pl.multiple_of((place ^ offset) * width, width), width)
            part = jnp.dot(
                tokens[first : first + tile, low:high],
                weight[low:high, columns],
                preferred_element_type=jnp.float32,
            )
            if number >= half:
                targets = [(kept_ref, number - half, first, 0, tile)]
            else:
                targets, start = [], 0
                for sent_ref in sent_refs:
                    stop = start + sent_ref.shape[1]
                    above, below = max(first, start), min(first + tile, stop)
                    if above < below:
                        targets.append(
                            (sent_ref, number, above - start, above - first, below - above)
                        )
                    start = stop
            for ref, index, at, source, size in targets:
                value = part[source : source + size]
                if not fresh:
                    value = value + ref[index, at : at + size, :]
                ref[index, at : at + size, :] = value

    run_copies([token_copies[0], *weight_copies])
    token_copies[0].wait()
    for i, copy in enumerate(weight_copies):
        copy.wait()
        if i == 0:
            run_copies(token_copies[1:])
        add(0, i * slab, (i + 1) * slab, i == 0)
    for i in range(1, parts):
        token_copies[i].wait()
        add(i * tile, 0, weight.shape[0], True)


def base_chunks(tokens, weight, order, width):
    rows = tokens.shape[0]
    half = len(order) // 2
    sizes = [*piece_rows(rows), rows]
    *sent, kept = pl.pallas_call(
        functools.partial(base_kernel, order),
        in_specs=[ANY] * 2,
        out_specs=[VMEM] * len(sizes),
        out_shape=[jax.ShapeDtypeStruct((half, size, width), jnp.float32) for size in sizes],
        scratch_shapes=[
            pltpu.VMEM(tokens.shape, tokens.dtype),
            pltpu.VMEM(weight.shape, weight.dtype),
            pltpu.SemaphoreType.DMA((2, 4)),
        ],
        compiler_params=PARAMS,
        cost_estimate=BASE,
    )(in_hbm(tokens), in_hbm(weight))
    return sent, kept


def add_kernel(kept_ref, *refs):
    *arrived_refs, out_ref, mine_ref = refs
    half = kept_ref.shape[0] // 2
    start = 0
    for arrived_ref in arrived_refs:
        rows = pl.ds(start, arrived_ref.shape[1])
        for i in range(half):
            mine_ref[i, rows, :] = kept_ref[i, rows, :] + arrived_ref[i]
            out = kept_ref[half + i, rows, :] + arrived_ref[half + i]
            out_ref[i, rows, :] = out.astype(out_ref.dtype)
        start += arrived_ref.shape[1]


def add_halves(kept, arrived, sent_type):
    count, rows, width = kept.shape
    shape = (count // 2, rows, width)
    return pl.pallas_call(
        add_kernel,
        in_specs=[VMEM] * (1 + len(arrived)),
        out_shape=[
            jax.ShapeDtypeStruct(shape, sent_type),
            jax.ShapeDtypeStruct(shape, jnp.float32),
        ],
        compiler_params=PARAMS,
        cost_estimate=NO_COST,
    )(kept, *arrived)


def base_parts(tokens, weight, width):
    size = lax.axis_size("tensor")
    kept_order = [k for k in range(size) if not k & 1]
    kept_order.sort(key=lambda k: [k >> bit & 1 for bit in range(1, size.bit_length())])
    return base_chunks(tokens, weight, [k ^ 1 for k in kept_order] + kept_order, width)


def base_sum(sent, kept):
    arrived = [swap(piece, "tensor", 1) for piece in sent]
    distance = 2
    size = lax.axis_size("tensor")
    while distance < size:
        sent_type = jnp.bfloat16 if 2 * distance == size else jnp.float32
        sent, kept = add_halves(kept, arrived, sent_type)
        arrived = [swap(sent, "tensor", distance)]
        distance *= 2
    return kept[0], arrived[0][0]


def pick(names_ref, table_ref, holder, holder_slots, count):
    blocks = [jnp.int32(0)] * count
    slots = [jnp.int32(0)] * count
    seen = jnp.int32(0)
    for j in range(names_ref.shape[1]):
        slot = table_ref[names_ref[0, j]]
        hit = lax.div(slot, jnp.int32(holder_slots)) == holder
        for k in range(count):
            chosen = hit & (seen == k)
            blocks[k] = jnp.where(chosen, jnp.int32(j), blocks[k])
            slots[k] = jnp.where(chosen, lax.rem(slot, jnp.int32(holder_slots)), slots[k])
        seen = seen + hit.astype(jnp.int32)
    return blocks, slots


def panel_copies(k, slot, down_ref, up_ref, out_ref, sems):
    depth = down_ref.shape[2]
    width = up_ref.shape[2]
    return [
        pltpu.make_async_copy(down_ref.at[slot], out_ref.at[k, :, pl.ds(0, depth)], sems.at[k, 0]),
        pltpu.make_async_copy(up_ref.at[slot], out_ref.at[k, :, pl.ds(depth, width)], sems.at[k, 1]),
    ]


def plan_kernel(capacity, *refs):
    sources, down_ref, up_ref = refs[:6], *refs[6:8]
    near_ref, plan_ref, *scalars, scalar_sems, sems = refs[-10:]
    holder_slots = down_ref.shape[0]
    loads = [
        pltpu.make_async_copy(source, scalar, scalar_sems.at[i])
        for i, (source, scalar) in enumerate(zip(sources, scalars))
    ]
    for load in run_copies(loads):
        load.wait()
    names_ref, first_ref, second_ref, third_ref, table_ref, live_ref = scalars
    here = lax.axis_index("pool")
    find = functools.partial(
        pick, table_ref=table_ref, holder_slots=holder_slots, count=capacity
    )
    near_slots = find(first_ref, holder=here)[1]
    copies = []
    for k, slot in enumerate(near_slots):
        copies += run_copies(panel_copies(k, slot, down_ref, up_ref, near_ref, sems))
    inner = (here == 1) | (here == 2)
    own = find(names_ref, holder=here)
    near = find(names_ref, holder=here ^ 1)
    across = find(names_ref, holder=here ^ 3)
    late = find(names_ref, holder=here ^ 2)
    rows = [
        own[0],
        near[0],
        across[0],
        late[0],
        own[1],
        across[1],
        find(second_ref, holder=here)[1],
        find(third_ref, holder=here)[1],
        find(first_ref, holder=here ^ 3)[1],
        [inner.astype(jnp.int32)] * capacity,
        *[[live_ref[0, block] for block in phase[0]] for phase in (own, near, across, late)],
    ]
    for number, row in enumerate(rows):
        for k in range(capacity):
            plan_ref[number * capacity + k] = row[k]
    for copy in copies:
        copy.wait()


OWN, ACROSS, TO_INNER, TO_OUTER, FORWARD, INNER, LIVE, PLAN_ROWS = 4, 5, 6, 7, 8, 9, 10, 14


def make_plan(names, others, table, live, down, up, capacity, after):
    rank, depth = down.shape[1:]
    return pl.pallas_call(
        functools.partial(plan_kernel, capacity),
        in_specs=[ANY] * (8 + len(after)),
        out_specs=[ANY, SMEM],
        out_shape=[
            jax.ShapeDtypeStruct((capacity, rank, depth + up.shape[2]), down.dtype),
            jax.ShapeDtypeStruct((PLAN_ROWS * capacity,), jnp.int32),
        ],
        scratch_shapes=[pltpu.SMEM(names.shape, jnp.int32)] * 4
        + [pltpu.SMEM(table.shape, jnp.int32), pltpu.SMEM(live.shape, jnp.int32)]
        + [pltpu.SemaphoreType.DMA((6,)), pltpu.SemaphoreType.DMA((capacity, 2))],
        compiler_params=PARAMS,
        cost_estimate=SHORT,
    )(in_hbm(names), *others, in_hbm(table), in_hbm(live), down, up, *after)


def pack_kernel(starts, choose, capacity, plan_ref, *refs):
    out_ref, sems = refs[-2:]

    def run(start, down_ref, up_ref):
        copies = []
        for k in range(capacity):
            slot = plan_ref[start + k]
            copies += run_copies(panel_copies(k, slot, down_ref, up_ref, out_ref, sems))
        for copy in copies:
            copy.wait()

    if len(starts) == 1:
        run(starts[0], *refs[:2])
    else:
        first = plan_ref[choose] != 0
        pl.when(first)(functools.partial(run, starts[0], *refs[:2]))
        pl.when(jnp.logical_not(first))(functools.partial(run, starts[1], *refs[2:4]))


def pack_panels(plan, choices, choose, capacity, after=(), cost=None):
    sources = [a for _, *pair in choices for a in pair]
    rank, depth = sources[0].shape[1:]
    width = sources[1].shape[2]
    return pl.pallas_call(
        functools.partial(pack_kernel, [start for start, *_ in choices], choose, capacity),
        in_specs=[SMEM] + [ANY] * (len(sources) + len(after)),
        out_specs=ANY,
        out_shape=jax.ShapeDtypeStruct((capacity, rank, depth + width), sources[0].dtype),
        scratch_shapes=[pltpu.SemaphoreType.DMA((capacity, 2))],
        compiler_params=PARAMS,
        cost_estimate=cost or NO_COST,
    )(plan, *sources, *after)


def each_block(phases, choose, plan_ref, refs, act):
    number = 0
    for row, count, rows in phases:
        mine, refs = refs[: len(rows)], refs[len(rows) :]

        def run(ref, row_of, number=number, row=row, count=count):
            for k in range(count):
                panel = ref.at[k if row_of is None else plan_ref[row_of + k]]
                act(number + k, plan_ref[row + k], panel)

        if len(rows) == 1:
            run(mine[0], rows[0])
        else:
            first = plan_ref[choose] != 0
            pl.when(first)(functools.partial(run, mine[0], rows[0]))
            pl.when(jnp.logical_not(first))(functools.partial(run, mine[1], rows[1]))
        number += count


def split_phases(phases):
    shapes = [(row, count, [source[1] for source in sources]) for row, count, sources in phases]
    return shapes, [source[0] for _, _, sources in phases for source in sources]


def shrink_kernel(phases, choose, plan_ref, token_ref, *refs):
    out_ref = refs[-1]
    depth = token_ref.shape[2]

    def act(number, block, panel_ref):
        out_ref[number] = lax.dot_general(
            panel_ref[:, :depth],
            token_ref[block],
            (((1,), (1,)), ((), ())),
            preferred_element_type=jnp.float32,
        ).astype(out_ref.dtype)

    each_block(phases, choose, plan_ref, refs, act)


def shrink(plan, row_blocks, phases, choose, after=(), kind=jnp.float32, cost=None):
    shapes, panels = split_phases(phases)
    total = sum(count for _, count, _ in phases)
    shape = (total, panels[0].shape[1], row_blocks.shape[1])
    return pl.pallas_call(
        functools.partial(shrink_kernel, shapes, choose),
        in_specs=[SMEM] + [VMEM] * (1 + len(panels)) + [ANY] * len(after),
        out_specs=VMEM,
        out_shape=jax.ShapeDtypeStruct(shape, kind),
        compiler_params=PARAMS,
        cost_estimate=cost or NO_COST,
    )(plan, row_blocks, *panels, *after)


def exchange(part):
    return [part] + [swap(part, "tensor", m) for m in range(1, lax.axis_size("tensor"))]


def combine_kernel(phases, choose, part_count, live_row, plan_ref, *refs):
    parts = refs[:part_count]
    mine_ref, far_ref = refs[part_count : part_count + 2]
    out_ref, held_ref, sems = refs[-3:]
    total, block_rows, width = held_ref.shape

    def copy_of(number, block):
        rows = pl.ds(pl.multiple_of(block * block_rows, block_rows), block_rows)
        return pltpu.make_async_copy(held_ref.at[number], out_ref.at[rows], sems.at[number])

    def act(number, block, panel_ref):
        shrunk = parts[0][number].astype(jnp.float32)
        for part in parts[1:]:
            shrunk = shrunk + part[number].astype(jnp.float32)
        start = panel_ref.shape[1] - width
        delta = lax.dot_general(
            shrunk.astype(jnp.bfloat16),
            panel_ref[:, start : start + width],
            (((0,), (0,)), ((), ())),
            preferred_element_type=jnp.float32,
        )
        rows = pl.ds(pl.multiple_of(block * block_rows, block_rows), block_rows)
        row = lax.broadcasted_iota(jnp.int32, delta.shape, 0)
        value = mine_ref[rows, :] + far_ref[rows, :].astype(jnp.float32) + ADAPTER_SCALE * delta
        value = jnp.where(row < plan_ref[live_row + number], value, 0.0)
        held_ref[number] = value.astype(held_ref.dtype)
        copy_of(number, block).start()

    each_block(phases, choose, plan_ref, refs[part_count + 2 :], act)
    number = 0
    for row, count, _ in phases:
        for k in range(count):
            copy_of(number, plan_ref[row + k]).wait()
            number += 1


def combine(plan, live_row, parts, base, phases, choose, out=None, cost=None):
    block_rows = parts[0].shape[2]
    rows, width = base[0].shape
    shapes, panels = split_phases(phases)
    total = sum(count for _, count, _ in phases)
    operands = [*parts, *base, *panels]
    specs = [VMEM] * len(operands)
    aliases = {}
    if out is not None:
        specs.append(ANY)
        operands.append(out)
        aliases = {len(operands): 0}
    return pl.pallas_call(
        functools.partial(combine_kernel, shapes, choose, len(parts), live_row),
        in_specs=[SMEM] + specs,
        out_specs=ANY,
        out_shape=pltpu.HBM((rows, width), jnp.bfloat16),
        input_output_aliases=aliases,
        scratch_shapes=[
            pltpu.VMEM((total, block_rows, width), jnp.bfloat16),
            pltpu.SemaphoreType.DMA((total,)),
        ],
        compiler_params=PARAMS,
        cost_estimate=cost or NO_COST,
    )(plan, *operands)


def on_line_of_four(tokens, weight, row_blocks, down, up, names, table, live, capacity):
    def across(value, pairs):
        return lax.ppermute(value, "pool", pairs)

    others = [swap(names, "pool", m) for m in range(1, 4)]
    inner_up = across(up, [(0, 0), (1, 2), (2, 1), (3, 3)])
    inner_down = across(down, [(0, 0), (1, 2), (2, 1), (3, 3)])
    sent, kept = base_parts(tokens, weight, up.shape[2])
    choose = INNER * capacity
    held = down, up
    near_out, plan = make_plan(
        names, others, table, live, *held, capacity, [inner_up, sent[-1]]
    )

    def pack(choices, after, cost=None):
        choices = [(row * capacity, *panels) for row, *panels in choices]
        return pack_panels(plan, choices, choose, capacity, after, cost)

    near = across(near_out, [(0, 1), (1, 0), (2, 3), (3, 2)])
    base = base_sum(sent, kept)
    outer_out = pack([(TO_OUTER, *held)], [base[0]])
    to_outer = across(outer_out, [(0, 3), (1, 1), (2, 2), (3, 0)])
    late_out = pack(
        [(FORWARD, inner_down, inner_up), (TO_INNER, *held)], [outer_out], LONG
    )
    late = across(late_out, [(0, 2), (1, 0), (2, 3), (3, 1)])

    first = [(0, capacity, [(down, OWN * capacity)]), (capacity, capacity, [(near, None)])]
    first_up = [(0, capacity, [(up, OWN * capacity)]), first[1]]
    middle = [(2 * capacity, capacity, [(inner_down, ACROSS * capacity), (to_outer, None)])]
    middle_up = [(2 * capacity, capacity, [(inner_up, ACROSS * capacity), (to_outer, None)])]
    last = [(3 * capacity, capacity, [(late, None)])]

    def write(number, parts, phases, out, cost=None):
        live_row = (LIVE + number) * capacity
        return combine(plan, live_row, parts, base, phases, choose, out, cost)

    first_parts = exchange(shrink(plan, row_blocks, first, choose, [late_out]))
    out = write(0, first_parts, first_up, None, MIDDLE)
    middle_part = shrink(plan, row_blocks, middle, choose, [in_hbm(out)])
    middle_parts = exchange(middle_part)
    last_parts = exchange(shrink(plan, row_blocks, last, choose, [middle_part], jnp.bfloat16))
    out = write(2, middle_parts, middle_up, out)
    return write(3, last_parts, last, out)


def on_any_pool(tokens, weight, row_blocks, down, up, names, table, live, capacity):
    pool_size = lax.axis_size("pool")
    here = lax.axis_index("pool")
    holder_slots = down.shape[0]
    asked = table[lax.all_gather(names[0], "pool")]
    count = jnp.arange(capacity, dtype=jnp.int32)
    arrived = []
    for distance in range(pool_size):
        slots = asked[lax.rem(here + distance, pool_size)]
        hit = slots // holder_slots == here
        chosen = hit[None, :] & (jnp.cumsum(hit.astype(jnp.int32))[None, :] == 1 + count[:, None])
        plan = jnp.sum(jnp.where(chosen, (slots % holder_slots)[None, :], 0), axis=1)
        panels = pack_panels(plan, [(0, down, up)], 0, capacity)
        pairs = [(i, (i + distance) % pool_size) for i in range(pool_size)]
        arrived.append(lax.ppermute(panels, "pool", pairs) if distance else panels)
    arrived = jnp.concatenate(arrived)
    owners = asked[here] // holder_slots
    blocks = jnp.arange(owners.shape[0], dtype=jnp.int32)
    earlier = (owners[:, None] == owners[None, :]) & (blocks[:, None] > blocks[None, :])
    ranks = jnp.sum(earlier.astype(jnp.int32), axis=1)
    places = lax.rem(here - owners + pool_size, pool_size) * capacity + ranks
    plan = jnp.concatenate([blocks, places, live[0]])
    base = base_sum(*base_parts(tokens, weight, up.shape[2]))
    phases = [(0, blocks.shape[0], [(arrived, blocks.shape[0])])]
    parts = exchange(shrink(plan, row_blocks, phases, 0))
    live_row = 2 * blocks.shape[0]
    return combine(plan, live_row, parts, base, phases, 0)


def on_device(
    tokens,
    value_weight,
    adapter_down_weight,
    adapter_up_weight,
    adapter_of_block,
    adapter_pool_slot,
    live_block_tokens,
):
    pool_size = lax.axis_size("pool")
    blocks = adapter_of_block.shape[1]
    capacity = -(-blocks // pool_size)
    row_blocks = tokens.reshape(blocks, tokens.shape[0] // blocks, tokens.shape[1])
    line = pool_size == 4 and blocks == capacity * pool_size
    route = on_line_of_four if line else on_any_pool
    return route(
        tokens,
        value_weight,
        row_blocks,
        jnp.transpose(adapter_down_weight, (0, 2, 1)),
        adapter_up_weight,
        adapter_of_block,
        adapter_pool_slot,
        live_block_tokens,
        capacity,
    )


def solution(mesh):
    return jax.shard_map(
        on_device,
        mesh=mesh,
        in_specs=(
            P(("groups", "pool"), "tensor"),
            P("tensor", None),
            P(("groups", "pool"), "tensor", None),
            P(("groups", "pool"), None, "tensor"),
            P(("groups", "pool"), None),
            P("groups"),
            P(("groups", "pool"), None),
        ),
        out_specs=P(("groups", "pool"), "tensor"),
        check_vma=False,
    )
```
